128 devices in a mesh: grp: 8 (over x, core), exp: 16 (over z, y).
Axes of the slice: x: 4, y: 4, z: 4, core: 2. Of those that a mesh axis runs over, the one named last changes fastest.
Arguments:
- images: bfloat16 [128, 197, 768], P(('grp', 'exp')), may hold values from -6 to 6
- cotangent: bfloat16 [128, 197, 768], P(('grp', 'exp')), may hold values from -6 to 6
- expert_ids: int32 [128, 197, 2], P(('grp', 'exp')), may hold values from 0 to 15, all different within a row; in each aligned block of 197 rows (0 to 196, 197 to 393, ..., all dimensions but the last counted through in order) at most 33 rows name the same one
- kept_routes: int32 [128, 197, 2], P(('grp', 'exp')), may hold values 0 or 1
- qkv_master: float32 [768, 2304], P('grp'), may hold values from -0.21875 to 0.21875
- qkv_first: float32 [768, 2304], P('grp'), may hold values from -64 to 64
- qkv_second: float32 [768, 2304], P('grp'), may hold values from 12.608 to 50.432
- proj_master: float32 [768, 768], P('grp'), may hold values from -1.25 to 1.25
- proj_first: float32 [768, 768], P('grp'), may hold values from -14 to 14
- proj_second: float32 [768, 768], P('grp'), may hold values from 0.50432 to 2.26944
- router_master: float32 [768, 16], P('grp'), may hold values from -0.15625 to 0.15625
- router_first: float32 [768, 16], P('grp'), may hold values from -768 to 768
- router_second: float32 [768, 16], P('grp'), may hold values from 1765.12 to 7060.48
- norm_master: float32 [768, 4], P('grp'), may hold values from -0.3 to 1.5, as said below
- norm_first: float32 [768, 4], P('grp'), may hold values from -96 to 96
- norm_second: float32 [768, 4], P('grp'), may hold values from 25.216 to 100.864
- inner_master: float32 [16, 768, 3072], P('exp', None, 'grp'), may hold values from -0.21875 to 0.21875
- inner_first: float32 [16, 768, 3072], P('exp', None, 'grp'), may hold values from -10 to 10
- inner_second: float32 [16, 768, 3072], P('exp', None, 'grp'), may hold values from 0.28368 to 1.13472
- outer_master: float32 [16, 3072, 768], P('exp', 'grp'), may hold values from -1.75 to 1.75
- outer_first: float32 [16, 3072, 768], P('exp', 'grp'), may hold values from -1.25 to 1.25
- outer_second: float32 [16, 3072, 768], P('exp', 'grp'), may hold values from 0.0044325 to 0.017853126
Outputs:
- result: bfloat16 [128, 197, 768], P(('grp', 'exp'))
- image_grad: float32 [128, 197, 768], P(('grp', 'exp'))
- qkv_moment: float32 [768, 2304], P('grp')
- qkv_square: float32 [768, 2304], P('grp')
- qkv_weight: float32 [768, 2304], P('grp')
- proj_moment: float32 [768, 768], P('grp')
- proj_square: float32 [768, 768], P('grp')
- proj_weight: float32 [768, 768], P('grp')
- router_moment: float32 [768, 16], P('grp')
- router_square: float32 [768, 16], P('grp')
- router_weight: float32 [768, 16], P('grp')
- norm_moment: float32 [768, 4], P('grp')
- norm_square: float32 [768, 4], P('grp')
- norm_weight: float32 [768, 4], P('grp')
- inner_moment: float32 [16, 768, 3072], P('exp', None, 'grp')
- inner_square: float32 [16, 768, 3072], P('exp', None, 'grp')
- inner_weight: float32 [16, 768, 3072], P('exp', None, 'grp')
- outer_moment: float32 [16, 3072, 768], P('exp', 'grp')
- outer_square: float32 [16, 3072, 768], P('exp', 'grp')
- outer_weight: float32 [16, 3072, 768], P('exp', 'grp')
The draws below stay inside these ranges and needn't reach their ends.
Inputs may be any that keep to these rules, and one draw needn't show every extreme that they name: `expert_ids`: each token names two different experts. Among the tokens of one device no expert is named by more than 33 routes, a bound that some block reaches. `norm_master`: columns 0 and 2 are gains, columns 1 and 3 biases.
All inputs are finite; a program needn't handle non-finite values. No bound on the sum of `kept_routes` on one device may be relied on, other than what follows from the above.
Results may differ from the reference program's by a relative error of at most 0.015.
Values may be sent and summed in bfloat16 or wider, within the bound.
No kernel may reach another device: no remote copies, remote signals or barrier semaphores. Data moves between devices by JAX's collectives and lax.ppermute only.
A program may use at most 192 MiB of HBM per device.

```python
import math
import jax
import jax.numpy as jnp
import numpy as np
from jax import lax

D = 768
HEADS = 12
HEAD_DIM = 64
FF = 3072
IMAGE = 197
IMG_DEV = 1
STEP = 10
EXPERTS = 16
CAP = 33
IMAGES = 128
TOKENS = 25216
N_GRP = 8
N_EXP = 16


def draw_norm_master(key, part):
    key = jax.random.fold_in(key, 5)
    gains = jax.random.uniform(jax.random.fold_in(key, 1), (D, 2), jnp.float32, 0.5, 1.5)
    shifts = jax.random.uniform(jax.random.fold_in(key, 2), (D, 2), jnp.float32, -0.3, 0.3)
    return jnp.stack([gains[:, 0], shifts[:, 0], gains[:, 1], shifts[:, 1]], axis=1)


def touch_ends(values, key, low, largest):
    dims = values.shape
    spot = [jax.random.randint(jax.random.fold_in(key, axis), (), 0, dims[axis]) for axis in range(len(dims))]
    values = values.at[tuple(spot)].set(low)
    longest = dims.index(max(dims))
    spot[longest] = (spot[longest] + 1) % dims[longest]
    return values.at[tuple(spot)].set(largest)


def levels(key, extent, pieces, least, largest):
    level, own = 1.0, jax.random.fold_in(key, 6)
    for axis_at, shards_of in pieces:
        steps = jnp.exp(jax.random.uniform(jax.random.fold_in(own, axis_at), (shards_of,), jnp.float32, least / len(pieces), largest / len(pieces)))
        level = level * jnp.repeat(steps, extent[axis_at] // shards_of).reshape([-1 if axis == axis_at else 1 for axis in range(len(extent))])
    return level


def shared_out(stream_key, own, number, rows, count, top, most, slope):
    sequence = jax.random.permutation(stream_key, count)
    heavy_load, common = portions_of(count, rows * top, most, slope, True), portions_of(count, rows * top, most, slope, False)
    places = jnp.arange(count)

    def named(tallies, turn):
        used = int((tallies > 0).sum())
        fixed = max(1, used // 4)
        passed = fixed + (places - fixed + turn * (used - fixed)) % max(1, count - fixed)
        return jnp.zeros((count,), jnp.int32).at[sequence[jnp.where(places < fixed, places, passed)]].set(jnp.asarray(tallies, jnp.int32))

    tallies = jnp.where(number % 4 == 0, named(heavy_load, number // 4), named(common, number - number // 4 - 1))
    mixed = jax.random.permutation(jax.random.fold_in(own, 3), count)
    giver, sink = mixed[0:count // 2 * 2:2], mixed[1:count // 2 * 2:2]
    slack = jnp.minimum(tallies[giver] - 1, most - tallies[sink]) // 2
    slack = jnp.where((giver == sequence[0]) | (sink == sequence[0]) | (tallies[sink] == 0), 0, jnp.maximum(slack, 0))
    passed = jax.random.randint(jax.random.fold_in(own, 4), (count // 2,), 0, 1 << 20) % (slack + 1)
    tallies = tallies.at[giver].add(-passed).at[sink].add(passed)
    labels = jnp.searchsorted(jnp.cumsum(tallies), jnp.arange(rows * top), side="right").astype(jnp.int32)
    listing = labels.reshape(top, rows).T
    listing = listing[jax.random.permutation(jax.random.fold_in(own, 1), rows)]
    turn = jax.random.randint(jax.random.fold_in(own, 2), (rows, 1), 0, top)
    return jnp.take_along_axis(listing, (jnp.arange(top)[None, :] + turn) % top, axis=1)


def portions_of(count, total, limit, slope, full):
    loads = [(1 << 20) // math.isqrt(grade ** slope) + 1 for grade in range(1, count + 1)]
    largest = limit if full else min(limit, max(-(-total // count), total * loads[0] // sum(loads)))
    least = 1 if total - largest >= count - 1 else 0
    holding, surplus = [largest] + [least] * (count - 1), total - largest - least * (count - 1)
    while surplus > 0:
        candidates = [i for i in range(1, count) if holding[i] < largest] or [i for i in range(1, count) if holding[i] < limit]
        whole, remaining = sum([loads[i] for i in candidates]), surplus
        for i in candidates:
            more = min(limit - holding[i], max(1, remaining * loads[i] // whole), surplus)
            holding[i] = holding[i] + more
            surplus = surplus - more
    return np.array(holding)


def noise(stream_key, extent, spread, most, shards=(), kind=jnp.bfloat16):
    values = spread * jax.random.normal(stream_key, extent, jnp.float32)
    if shards:
        values = values * levels(stream_key, extent, shards, -0.22, 0.18)
    return jnp.clip(values, -most, most).astype(kind)


def setup_inputs(seed: int = 0) -> dict:
    seeds = jax.random.split(jax.random.key(seed), 23)
    images = noise(seeds[0], (IMAGES, IMAGE, D), 1.0, 6.0, ((0, 128),))
    cotangent = noise(seeds[1], (IMAGES, IMAGE, D), 1.0, 6.0, ((0, 128),))
    expert_ids_keys = jax.random.split(jax.random.fold_in(seeds[2], 1), IMAGES * IMAGE // (IMG_DEV * IMAGE))
    expert_ids_turns = jax.random.permutation(jax.random.fold_in(seeds[2], 3), IMAGES * IMAGE // (IMG_DEV * IMAGE))
    expert_ids = jax.vmap(lambda own, number: shared_out(jax.random.fold_in(seeds[2], 2), own, number, IMG_DEV * IMAGE, EXPERTS, 2, CAP, 1))(expert_ids_keys, expert_ids_turns).reshape((IMAGES, IMAGE, 2))
    kept_routes = touch_ends((jax.random.randint(seeds[3], (IMAGES, IMAGE, 2), 0, 8) < 7).astype(jnp.int32), jax.random.fold_in(seeds[3], 1), 0, 1)
    qkv_master = noise(seeds[4], (D, 3 * D), D ** -0.5, 0.21875, ((0, 8),), jnp.float32)
    qkv_first = noise(seeds[5], (D, 3 * D), (0.07 * TOKENS ** 0.5), 64.0, ((0, 8),), jnp.float32)
    qkv_second = jnp.clip(jnp.exp(math.log(50.432) - 1.3862944 * jax.random.uniform(seeds[6], (D, 3 * D), jnp.float32) ** levels(seeds[6], (D, 3 * D), ((0, 8),), -0.2, 0.2)), 12.608, 50.432)
    proj_master = noise(seeds[7], (D, D), (D // 32) ** -0.5, 1.25, ((0, 8),), jnp.float32)
    proj_first = noise(seeds[8], (D, D), (0.015 * TOKENS ** 0.5), 14.0, ((0, 8),), jnp.float32)
    proj_second = jnp.clip(jnp.exp(math.log(2.26944) - 1.5040773 * jax.random.uniform(seeds[9], (D, D), jnp.float32) ** levels(seeds[9], (D, D), ((0, 8),), -0.2, 0.2)), 0.50432, 2.26944)
    router_master = noise(seeds[10], (D, EXPERTS), (2 * D) ** -0.5, 0.15625, ((0, 8),), jnp.float32)
    router_first = noise(seeds[11], (D, EXPERTS), (0.8 * TOKENS ** 0.5), 768.0, ((0, 8),), jnp.float32)
    router_second = jnp.clip(jnp.exp(math.log(7060.48) - 1.3862944 * jax.random.uniform(seeds[12], (D, EXPERTS), jnp.float32) ** levels(seeds[12], (D, EXPERTS), ((0, 8),), -0.2, 0.2)), 1765.12, 7060.48)
    norm_master = draw_norm_master(jax.random.fold_in(seeds[22], 71), 0)
    norm_first = noise(seeds[14], (D, 4), (0.1 * TOKENS ** 0.5), 96.0, ((0, 8),), jnp.float32)
    norm_second = jnp.clip(jnp.exp(math.log(100.864) - 1.3862944 * jax.random.uniform(seeds[15], (D, 4), jnp.float32) ** levels(seeds[15], (D, 4), ((0, 8),), -0.2, 0.2)), 25.216, 100.864)
    inner_master = noise(seeds[16], (EXPERTS, D, FF), D ** -0.5, 0.21875, ((0, 16), (2, 8)), jnp.float32)
    inner_first = noise(seeds[17], (EXPERTS, D, FF), (0.042 * (TOKENS * EXPERTS ** -1) ** 0.5), 10.0, ((0, 16), (2, 8)), jnp.float32)
    inner_second = jnp.clip(jnp.exp(math.log(1.13472) - 1.3862944 * jax.random.uniform(seeds[18], (EXPERTS, D, FF), jnp.float32) ** levels(seeds[18], (EXPERTS, D, FF), ((0, 16), (2, 8)), -0.2, 0.2)), 0.28368, 1.13472)
    outer_master = noise(seeds[19], (EXPERTS, FF, D), (max(FF // (EXPERTS * EXPERTS), 1)) ** -0.5, 1.75, ((0, 16), (1, 8)), jnp.float32)
    outer_first = noise(seeds[20], (EXPERTS, FF, D), (0.085 * (TOKENS * EXPERTS ** -3) ** 0.5), 1.25, ((0, 16), (1, 8)), jnp.float32)
    outer_second = jnp.clip(jnp.exp(math.log(0.017853126) - 1.393215 * jax.random.uniform(seeds[21], (EXPERTS, FF, D), jnp.float32) ** levels(seeds[21], (EXPERTS, FF, D), ((0, 16), (1, 8)), -0.2, 0.2)), 0.0044325, 0.017853126)
    return dict(images=images, cotangent=cotangent, expert_ids=expert_ids, kept_routes=kept_routes, qkv_master=qkv_master, qkv_first=qkv_first, qkv_second=qkv_second, proj_master=proj_master, proj_first=proj_first, proj_second=proj_second, router_master=router_master, router_first=router_first, router_second=router_second, norm_master=norm_master, norm_first=norm_first, norm_second=norm_second, inner_master=inner_master, inner_first=inner_first, inner_second=inner_second, outer_master=outer_master, outer_first=outer_first, outer_second=outer_second)


@jax.custom_vjp
def low(v):
    return lax.optimization_barrier(v.astype(jnp.bfloat16)).astype(jnp.float32)

@jax.custom_vjp
def low_back(v):
    return v

def low_keep(v):
    return (low(v), None)

def low_pass(kept, grad):
    return (grad,)

def back_keep(v):
    return (v, None)

def back_low(kept, grad):
    return (low(grad),)
low.defvjp(low_keep, low_pass)
low_back.defvjp(back_keep, back_low)
norm_epsilon = 1e-06
beta_first = 0.9
beta_second = 0.999
adam_epsilon = 1e-08
weight_decay = 0.1
highest = lax.Precision.HIGHEST

def layer_norm(values, gain, shift):
    centered = values - lax.optimization_barrier(jnp.mean(values, axis=-1, keepdims=True))
    variance = lax.optimization_barrier(jnp.mean(centered * centered, axis=-1, keepdims=True))
    return centered * lax.rsqrt(variance + norm_epsilon) * gain + shift

def adamw(master, first, second, gradient, rate):
    first = beta_first * first + (1.0 - beta_first) * gradient
    second = beta_second * second + (1.0 - beta_second) * gradient * gradient
    corrected = first / (1.0 - beta_first ** STEP)
    scaled = jnp.sqrt(second / (1.0 - beta_second ** STEP)) + adam_epsilon
    return (first, second, master - rate * (corrected / scaled + weight_decay * master))

def route_places(expert_ids):
    sources = N_GRP * N_EXP
    flat_ids = expert_ids.reshape(sources, IMG_DEV * IMAGE * 2)
    marks = (flat_ids[:, :, None] == jnp.arange(EXPERTS, dtype=jnp.int32)[None, None, :]).astype(jnp.int32)
    earlier = jnp.cumsum(marks, axis=1) - marks
    slots = lax.optimization_barrier(jnp.sum(earlier * marks, axis=2))
    anchor = jnp.arange(sources, dtype=jnp.int32)[:, None] * CAP
    return (flat_ids * (sources * CAP) + anchor + slots).reshape(-1)

def reference(images, cotangent, expert_ids, kept_routes, qkv_master, qkv_first, qkv_second, proj_master, proj_first, proj_second, router_master, router_first, router_second, norm_master, norm_first, norm_second, inner_master, inner_first, inner_second, outer_master, outer_first, outer_second):
    sources = N_GRP * N_EXP
    places = route_places(expert_ids)
    id_rows = expert_ids.reshape(TOKENS, 2)
    keep = kept_routes.reshape(TOKENS, 2).astype(jnp.float32)
    chosen = (id_rows[:, :, None] == jnp.arange(EXPERTS, dtype=jnp.int32)[None, None, :]).astype(jnp.float32)
    score_scale = HEAD_DIM ** (-0.5)

    def forward(source, qkv_w, proj_w, router_w, norm_w, inner_w, outer_w):
        qkv_w = low(qkv_w)
        proj_w = low(proj_w)
        router_w = low(router_w)
        norm_w = low(norm_w)
        inner_w = low(inner_w)
        outer_w = low(outer_w)
        normed = low(layer_norm(source, norm_w[:, 0], norm_w[:, 1]))
        triple = low_back(low(jnp.dot(normed, qkv_w, precision=highest)))
        triple = triple.reshape(IMAGES, IMAGE, 3, HEADS, HEAD_DIM)

        def attend(image_part):
            scores = low_back(jnp.einsum('qhd,khd->hqk', image_part[:, 0], image_part[:, 1], precision=highest) * score_scale)
            weights = low(jax.nn.softmax(scores, axis=-1))
            mixed = jnp.einsum('hqk,khd->qhd', weights, image_part[:, 2], precision=highest)
            return low_back(low(mixed))
        attended = lax.map(jax.checkpoint(attend), triple).reshape(TOKENS, D)
        middle = source + low_back(jnp.dot(attended, proj_w, precision=highest))
        second = low(layer_norm(middle, norm_w[:, 2], norm_w[:, 3]))
        logits = low_back(jnp.dot(second, router_w, precision=highest))
        router_probs = jax.nn.softmax(logits, axis=-1)
        gates = lax.optimization_barrier(jnp.sum(router_probs[:, None, :] * chosen, axis=-1)) * keep
        copies = low_back(second[:, None, :] * keep[:, :, None]).reshape(TOKENS * 2, D)
        buffer = jnp.zeros((EXPERTS * sources * CAP, D), jnp.float32).at[places].add(copies)
        buffer = buffer.reshape(EXPERTS, sources * CAP, D)

        def expert(operands):
            inputs, first_w, last_w = operands
            hidden = low_back(jnp.dot(inputs, first_w, precision=highest))
            active = low(jax.nn.gelu(hidden))
            return low_back(low(jnp.dot(active, last_w, precision=highest)))
        outputs = lax.map(jax.checkpoint(expert), (buffer, inner_w, outer_w)).reshape(EXPERTS * sources * CAP, D)
        returned = outputs[places].reshape(TOKENS, 2, D)
        return middle + lax.optimization_barrier(jnp.sum(gates[:, :, None] * returned, axis=1))
    source = images.reshape(TOKENS, D).astype(jnp.float32)
    output, pullback = jax.vjp(forward, source, qkv_master, proj_master, router_master, norm_master, inner_master, outer_master)
    grads = pullback(cotangent.reshape(TOKENS, D).astype(jnp.float32))
    result = output.astype(jnp.bfloat16).reshape(IMAGES, IMAGE, D)
    image_grad = grads[0].reshape(IMAGES, IMAGE, D)
    qkv_moment, qkv_square, qkv_weight = adamw(qkv_master, qkv_first, qkv_second, grads[1], 0.04)
    proj_moment, proj_square, proj_weight = adamw(proj_master, proj_first, proj_second, grads[2], 0.2)
    router_moment, router_square, router_weight = adamw(router_master, router_first, router_second, grads[3], 0.03)
    norm_moment, norm_square, norm_weight = adamw(norm_master, norm_first, norm_second, grads[4], 0.3)
    inner_moment, inner_square, inner_weight = adamw(inner_master, inner_first, inner_second, grads[5], 0.04)
    outer_moment, outer_square, outer_weight = adamw(outer_master, outer_first, outer_second, grads[6], 0.15)
    return (result, image_grad, qkv_moment, qkv_square, qkv_weight, proj_moment, proj_square, proj_weight, router_moment, router_square, router_weight, norm_moment, norm_square, norm_weight, inner_moment, inner_square, inner_weight, outer_moment, outer_square, outer_weight)
```

```python
import jax
import jax.numpy as jnp
from jax import lax
from jax.experimental import pallas as pl
from jax.experimental.pallas import tpu as pltpu
from jax.sharding import PartitionSpec as P

HEADS = 12
HEAD_DIM = 64
STEP = 10
D = 768
TOK = 197
ROWS = 208
EXPERTS = 16
CAP = 40
SLOTS = EXPERTS * CAP
DENSE = 3200
GRP = 8
OWN = D // GRP
PIECE = 48
WIDE = 384
HID = 384

norm_epsilon = 1e-06
beta_first = 0.9
beta_second = 0.999
adam_epsilon = 1e-08
weight_decay = 0.1
score_scale = HEAD_DIM ** (-0.5)
low = jnp.bfloat16
full = jnp.float32


def dot(a, b, dims=((1,), (0,))):
    return lax.dot_general(a, b, (dims, ((), ())), preferred_element_type=jnp.float32)


NT = ((1,), (1,))
TN = ((0,), (0,))


def unit_rows(values):
    centered = values - jnp.mean(values, axis=-1, keepdims=True)
    variance = jnp.mean(centered * centered, axis=-1, keepdims=True)
    scale = lax.rsqrt(variance + norm_epsilon)
    return centered * scale, scale


def norm_rows(w_ref):
    return w_ref[:, 3072:3200].astype(full).T[16:24]


def lanes(shape):
    return lax.broadcasted_iota(jnp.int32, shape, 1)


def half_masks():
    lane = lanes((1, 128))
    first = (lane < HEAD_DIM).astype(full)
    return first.astype(low), (1.0 - first).astype(low)


def forward_kernel(
    x_ref, g_ref, w_ref, ids_ref, keep_ref, trow_ref,
    send_ref, m_ref, a_ref, qkv_ref, p_ref, o_ref, c_ref, r_ref,
    x_pad, g_pad,
):
    x_pad[192:ROWS, :] = jnp.zeros((ROWS - 192, D), full)
    x_pad[0:TOK, :] = x_ref[0].astype(full)
    g_pad[192:ROWS, :] = jnp.zeros((ROWS - 192, D), full)
    g_pad[0:TOK, :] = g_ref[0].astype(full)
    norms = norm_rows(w_ref)
    x = x_pad[...]
    a = (unit_rows(x)[0] * norms[0:1] + norms[1:2]).astype(low)
    a_ref[...] = a
    for part in range(3):
        cols = slice(part * D, part * D + D)
        qkv_ref[:, cols] = dot(a, w_ref[:, cols]).astype(low)
    first, second = half_masks()
    seen = lanes((ROWS, ROWS)) < TOK
    low_half = lanes((ROWS, 128)) < HEAD_DIM
    for pair in range(HEADS // 2):
        at = pair * 128
        q = qkv_ref[:, at : at + 128]
        k = qkv_ref[:, D + at : D + at + 128]
        v = qkv_ref[:, 2 * D + at : 2 * D + at + 128]
        mixed = []
        for side, mask in enumerate((first, second)):
            s = dot(q * mask, k, NT) * score_scale
            s = jnp.where(seen, s, -1e30)
            e = jnp.exp(s - jnp.max(s, axis=1, keepdims=True))
            p = (e / jnp.sum(e, axis=1, keepdims=True)).astype(low)
            p_ref[2 * pair + side] = p
            mixed.append(dot(p, v))
        o_ref[:, at : at + 128] = jnp.where(low_half, mixed[0], mixed[1]).astype(low)
    m = x + dot(o_ref[...], w_ref[:, 2304:3072])
    m_ref[...] = m
    c = (unit_rows(m)[0] * norms[2:3] + norms[3:4]).astype(low)
    c_ref[...] = c
    lane = lanes((ROWS, 128))
    logits = jnp.where(lane < EXPERTS, dot(c, w_ref[:, 3072:3200]), -1e30)
    e = jnp.exp(logits - jnp.max(logits, axis=1, keepdims=True))
    r = e / jnp.sum(e, axis=1, keepdims=True)
    r_ref[...] = r
    slot = lax.broadcasted_iota(jnp.int32, (SLOTS, ROWS), 0)
    g = g_pad[...]
    picks, grads = [], []
    for j in range(2):
        chosen = lane == ids_ref[:, j : j + 1]
        gate = jnp.sum(jnp.where(chosen, r, 0.0), axis=1, keepdims=True) * keep_ref[:, j : j + 1]
        picks.append((slot == trow_ref[j : j + 1, :]).astype(full).astype(low))
        grads.append((gate * g).astype(low))
    send_ref[:, 0:D] = dot(picks[0] + picks[1], c).astype(low)
    send_ref[:, D:] = (dot(picks[0], grads[0]) + dot(picks[1], grads[1])).astype(low)


def expert_kernel(got_ref, w_ref, back_ref, grad_ref, z_sum, dx_sum, xt, dzt):
    step = pl.program_id(0)

    @pl.when(step == 0)
    def _():
        xt[...] = got_ref[:, 0:D].T
        dzt[...] = got_ref[:, D:].T
        z_sum[...] = jnp.zeros_like(z_sum)
        dx_sum[...] = jnp.zeros_like(dx_sum)

    wi = jnp.concatenate([w_ref[0:D, 0:HID], w_ref[D:, 0:HID]], axis=1)
    wot = jnp.concatenate([w_ref[0:D, HID:], w_ref[D:, HID:]], axis=1)
    u = dot(got_ref[:, 0:D], wi)
    dh = dot(got_ref[:, D:], wot)
    square = u * u
    inner = u * (0.7978845608028654 + (0.7978845608028654 * 0.044715) * square)
    t = jnp.tanh(inner)
    half = 0.5 * t + 0.5
    h = (u * half).astype(low)
    slope = (0.5 * u) * (1.0 - t * t)
    slope = slope * (0.7978845608028654 + (3 * 0.7978845608028654 * 0.044715) * square) + half
    du = (slope * dh).astype(low)
    z_sum[...] += dot(h, wot, NT)
    dx_sum[...] += dot(du, wi, NT)
    gi = dot(xt[...], du).astype(low)
    got_grad = dot(dzt[...], h).astype(low)
    grad_ref[0:D, 0:HID] = gi[:, 0:HID]
    grad_ref[D:, 0:HID] = gi[:, HID:]
    grad_ref[0:D, HID:] = got_grad[:, 0:HID]
    grad_ref[D:, HID:] = got_grad[:, HID:]

    @pl.when(step == pl.num_programs(0) - 1)
    def _():
        back_ref[:, 0:D] = z_sum[...].astype(low)
        back_ref[:, D:] = dx_sum[...].astype(low)


def spread(grad, first_group, out_ref):
    for g in range(GRP):
        for r in range(2):
            rows = slice(g * OWN + r * PIECE, g * OWN + (r + 1) * PIECE)
            for k in range(grad.shape[1] // WIDE):
                at = ((g * 2 + r) * 8 + first_group + k) * PIECE
                out_ref[at : at + PIECE, :] = grad[rows, k * WIDE : (k + 1) * WIDE]


def backward_kernel(
    back_ref, x_ref, g_ref, w_ref, ids_ref, tcol_ref,
    m_ref, a_ref, qkv_ref, p_ref, o_ref, c_ref, r_ref, keep_ref,
    result_ref, image_ref, grads_ref, extra_ref,
    x_pad, g_pad, dqkv,
):
    x_pad[192:ROWS, :] = jnp.zeros((ROWS - 192, D), full)
    x_pad[0:TOK, :] = x_ref[0].astype(full)
    g_pad[192:ROWS, :] = jnp.zeros((ROWS - 192, D), full)
    g_pad[0:TOK, :] = g_ref[0].astype(full)
    norms = norm_rows(w_ref)
    g = g_pad[...]
    m = m_ref[...]
    r = r_ref[...]
    lane = lanes((ROWS, 128))
    slot = lanes((ROWS, SLOTS))
    z = back_ref[:, 0:D]
    total = m
    dr = jnp.zeros((ROWS, 128), full)
    picks = []
    for j in range(2):
        pick = (slot == tcol_ref[:, j : j + 1]).astype(full).astype(low)
        picks.append(pick)
        keep = keep_ref[:, j : j + 1]
        chosen = lane == ids_ref[:, j : j + 1]
        gate = jnp.sum(jnp.where(chosen, r, 0.0), axis=1, keepdims=True) * keep
        zj = dot(pick, z)
        total = total + gate * zj
        dgate = jnp.sum(g * zj, axis=1, keepdims=True) * keep
        dr = dr + jnp.where(chosen, dgate, 0.0)
    result_ref[0] = total[0:TOK].astype(low)
    dl = (r * (dr - jnp.sum(dr * r, axis=1, keepdims=True))).astype(low)
    c = c_ref[...]
    extra_ref[0:16, :] = dot(dl, c, TN)[0:16]
    dc = dot(dl, w_ref[:, 3072:3200], NT) + dot(picks[0] + picks[1], back_ref[:, D:])
    xh, scale = unit_rows(m)
    dn2 = jnp.sum(dc * xh, axis=0, keepdims=True)
    dn3 = jnp.sum(dc, axis=0, keepdims=True)
    dxh = dc * norms[2:3]
    dm = g + scale * (
        dxh
        - jnp.mean(dxh, axis=1, keepdims=True)
        - xh * jnp.mean(dxh * xh, axis=1, keepdims=True)
    )
    dmb = dm.astype(low)
    spread(dot(o_ref[...].T, dmb).astype(low), 6, grads_ref)
    do = dot(dmb, w_ref[:, 2304:3072], NT).astype(low)
    first, second = half_masks()
    low_half = lane < HEAD_DIM
    for pair in range(HEADS // 2):
        at = pair * 128
        q = qkv_ref[:, at : at + 128]
        k = qkv_ref[:, D + at : D + at + 128]
        v = qkv_ref[:, 2 * D + at : 2 * D + at + 128]
        dop = do[:, at : at + 128]
        parts = []
        for side, mask in enumerate((first, second)):
            p_low = p_ref[2 * pair + side]
            p = p_low.astype(full)
            dp = dot(dop * mask, v, NT)
            ds = (p * (dp - jnp.sum(dp * p, axis=1, keepdims=True))).astype(low)
            parts.append((dot(ds, k), dot(ds, q, TN), dot(p_low, dop, TN)))
        for which, factor in enumerate((score_scale, score_scale, 1.0)):
            both = jnp.where(low_half, parts[0][which], parts[1][which]) * factor
            dqkv[:, which * D + at : which * D + at + 128] = both.astype(low)
    at_rows = a_ref[...].T
    da = jnp.zeros((ROWS, D), full)
    for part in range(3):
        cols = slice(part * D, part * D + D)
        spread(dot(at_rows, dqkv[:, cols]).astype(low), 2 * part, grads_ref)
        da = da + dot(dqkv[:, cols], w_ref[:, cols], NT)
    xh, scale = unit_rows(x_pad[...])
    extra_ref[16:24, :] = jnp.concatenate(
        [
            jnp.sum(da * xh, axis=0, keepdims=True),
            jnp.sum(da, axis=0, keepdims=True),
            dn2,
            dn3,
            jnp.zeros((4, D), full),
        ],
        axis=0,
    )
    dxh = da * norms[0:1]
    dx = dm + scale * (
        dxh
        - jnp.mean(dxh, axis=1, keepdims=True)
        - xh * jnp.mean(dxh * xh, axis=1, keepdims=True)
    )
    image_ref[0] = dx[0:TOK]


def adamw(master, first, second, gradient, rate):
    first = beta_first * first + (1.0 - beta_first) * gradient
    second = beta_second * second + (1.0 - beta_second) * gradient * gradient
    corrected = first / (1.0 - beta_first**STEP)
    scaled = jnp.sqrt(second / (1.0 - beta_second**STEP)) + adam_epsilon
    return (first, second, master - rate * (corrected / scaled + weight_decay * master))


def owner_kernel(*refs):
    pieces, inputs, outputs = refs[0], refs[1:7], refs[7:13]
    for r in range(2):
        rows = slice(r * PIECE, (r + 1) * PIECE)
        for k in range(8):
            piece = pieces[(r * 8 + k) * PIECE : (r * 8 + k + 1) * PIECE, :].astype(full)
            side, group, rate = (0, k, 0.04) if k < 6 else (3, k - 6, 0.2)
            cols = slice(group * WIDE, (group + 1) * WIDE)
            new = adamw(*[inputs[side + i][rows, cols] for i in range(3)], piece, rate)
            for i in range(3):
                outputs[side + i][rows, cols] = new[i]


def shape(*dims, dtype=jnp.float32):
    return jax.ShapeDtypeStruct(dims, dtype)


def in_vmem(count):
    return [pl.BlockSpec(memory_space=pltpu.VMEM)] * count


def params(mib):
    return pltpu.CompilerParams(vmem_limit_bytes=mib * 2**20)


def token_forward(*args):
    return pl.pallas_call(
        forward_kernel,
        out_shape=(
            shape(SLOTS, 2 * D, dtype=low),
            shape(ROWS, D),
            shape(ROWS, D, dtype=low),
            shape(ROWS, 3 * D, dtype=low),
            shape(HEADS, ROWS, ROWS, dtype=low),
            shape(ROWS, D, dtype=low),
            shape(ROWS, D, dtype=low),
            shape(ROWS, 128),
        ),
        in_specs=in_vmem(6),
        out_specs=tuple(in_vmem(8)),
        scratch_shapes=[pltpu.VMEM((ROWS, D), full)] * 2,
        compiler_params=params(40),
        cost_estimate=pl.CostEstimate(
            flops=4 * 10**9, bytes_accessed=12 * 10**6, transcendentals=10**6
        ),
        name="token_forward",
    )(*args)


def experts_both_ways(got, weights):
    return pl.pallas_call(
        expert_kernel,
        grid=(GRP // 2,),
        out_shape=(shape(SLOTS, 2 * D, dtype=low), shape(GRP * D, D, dtype=low)),
        in_specs=[
            pl.BlockSpec((SLOTS, 2 * D), lambda i: (0, 0)),
            pl.BlockSpec((2 * D, D), lambda i: (i, 0)),
        ],
        out_specs=(
            pl.BlockSpec((SLOTS, 2 * D), lambda i: (0, 0)),
            pl.BlockSpec((2 * D, D), lambda i: (i, 0)),
        ),
        scratch_shapes=[
            pltpu.VMEM((SLOTS, D), full),
            pltpu.VMEM((SLOTS, D), full),
            pltpu.VMEM((D, SLOTS), low),
            pltpu.VMEM((D, SLOTS), low),
        ],
        compiler_params=params(52),
        cost_estimate=pl.CostEstimate(
            flops=18 * 10**9, bytes_accessed=23 * 10**6, transcendentals=2 * 10**6
        ),
        name="experts",
    )(got, weights)


def token_backward(*args):
    return pl.pallas_call(
        backward_kernel,
        out_shape=(
            shape(1, TOK, D, dtype=low),
            shape(1, TOK, D),
            shape(GRP * 16 * PIECE, WIDE, dtype=low),
            shape(24, D),
        ),
        in_specs=in_vmem(14),
        out_specs=tuple(in_vmem(4)),
        scratch_shapes=[
            pltpu.VMEM((ROWS, D), full),
            pltpu.VMEM((ROWS, D), full),
            pltpu.VMEM((ROWS, 3 * D), low),
        ],
        compiler_params=params(48),
        cost_estimate=pl.CostEstimate(
            flops=7 * 10**9, bytes_accessed=18 * 10**6, transcendentals=10**4
        ),
        name="token_backward",
    )(*args)


def owner_step(pieces, arrays):
    return pl.pallas_call(
        owner_kernel,
        out_shape=tuple(shape(*a.shape) for a in arrays),
        in_specs=in_vmem(7),
        out_specs=tuple(in_vmem(6)),
        compiler_params=params(24),
        cost_estimate=pl.CostEstimate(
            flops=10**7, bytes_accessed=8 * 10**6, transcendentals=10**6
        ),
        name="owner_step",
    )(pieces, *arrays)


def on_device(
    images,
    cotangent,
    expert_ids,
    kept_routes,
    qkv_master,
    qkv_first,
    qkv_second,
    proj_master,
    proj_first,
    proj_second,
    router_master,
    router_first,
    router_second,
    norm_master,
    norm_first,
    norm_second,
    inner_master,
    inner_first,
    inner_second,
    outer_master,
    outer_first,
    outer_second,
):
    dense = jnp.concatenate(
        [
            qkv_master.astype(low),
            proj_master.astype(low),
            router_master.astype(low),
            norm_master.astype(low),
            jnp.zeros((OWN, DENSE - 3092), low),
        ],
        axis=1,
    )
    dense = lax.all_gather(dense, "grp", axis=0, tiled=True)
    mine = jnp.concatenate([inner_master[0].astype(low), outer_master[0].astype(low).T], axis=1)
    weights = lax.all_gather(mine, "grp", axis=0, tiled=True)

    ids = expert_ids.reshape(TOK, 2)
    kept = kept_routes.reshape(TOK, 2)
    flat = ids.reshape(-1)
    marks = (flat[:, None] == jnp.arange(EXPERTS, dtype=jnp.int32)[None, :]).astype(jnp.int32)
    slots = jnp.sum((jnp.cumsum(marks, axis=0) - marks) * marks, axis=1).reshape(TOK, 2)
    target = jnp.where(kept > 0, ids * CAP + slots, -1)
    padding = ((0, ROWS - TOK), (0, 0))
    target = jnp.pad(target, padding, constant_values=-1)
    ids = jnp.pad(ids, padding, constant_values=-1)
    keep = jnp.pad(kept.astype(full), padding)

    send, m, a, qkv, p, o, c, r = token_forward(images, cotangent, dense, ids, keep, target.T)
    got = lax.all_to_all(
        send.reshape(EXPERTS, CAP, 2 * D), "exp", split_axis=0, concat_axis=0, tiled=True
    )
    back, expert_grads = experts_both_ways(got.reshape(SLOTS, 2 * D), weights)
    expert_grads = lax.psum_scatter(expert_grads, "grp", scatter_dimension=0, tiled=True)
    back = lax.all_to_all(
        back.reshape(EXPERTS, CAP, 2 * D), "exp", split_axis=0, concat_axis=0, tiled=True
    )
    result, image_grad, grads, extra = token_backward(
        back.reshape(SLOTS, 2 * D), images, cotangent, dense, ids, target,
        m, a, qkv, p, o, c, r, keep,
    )
    grads = lax.psum_scatter(grads, "grp", scatter_dimension=0, tiled=True)

    extra = jnp.moveaxis(extra.reshape(24, GRP, OWN), 1, 0)
    extra = lax.all_to_all(extra, "grp", split_axis=0, concat_axis=0, tiled=True)
    extra = jnp.broadcast_to(jnp.sum(extra, axis=0)[None], (EXPERTS, 24, OWN))
    extra = lax.all_to_all(extra, "exp", split_axis=0, concat_axis=0, tiled=True)
    extra = jnp.sum(extra, axis=0).T

    pieces = lax.all_to_all(
        grads.reshape(16, PIECE, WIDE), "exp", split_axis=0, concat_axis=0, tiled=True
    )
    piece = jnp.sum(pieces.astype(full), axis=0).astype(low)
    pieces = lax.all_to_all(
        jnp.broadcast_to(piece[None], (16, PIECE, WIDE)),
        "exp",
        split_axis=0,
        concat_axis=0,
        tiled=True,
    )
    qkv_moment, qkv_square, qkv_weight, proj_moment, proj_square, proj_weight = owner_step(
        pieces.reshape(16 * PIECE, WIDE),
        (qkv_master, qkv_first, qkv_second, proj_master, proj_first, proj_second),
    )
    router_moment, router_square, router_weight = adamw(
        router_master, router_first, router_second, extra[:, 0:16], 0.03
    )
    norm_moment, norm_square, norm_weight = adamw(
        norm_master, norm_first, norm_second, extra[:, 16:20], 0.3
    )
    inner_grad = expert_grads[:, 0:HID].astype(full)
    outer_grad = expert_grads[:, HID:].T.astype(full)
    inner_moment, inner_square, inner_weight = adamw(
        inner_master, inner_first, inner_second, inner_grad[None], 0.04
    )
    outer_moment, outer_square, outer_weight = adamw(
        outer_master, outer_first, outer_second, outer_grad[None], 0.15
    )
    return (
        result,
        image_grad,
        qkv_moment,
        qkv_square,
        qkv_weight,
        proj_moment,
        proj_square,
        proj_weight,
        router_moment,
        router_square,
        router_weight,
        norm_moment,
        norm_square,
        norm_weight,
        inner_moment,
        inner_square,
        inner_weight,
        outer_moment,
        outer_square,
        outer_weight,
    )


def solution(mesh):
    in_specs = (
        P(("grp", "exp"), None, None),
        P(("grp", "exp"), None, None),
        P(("grp", "exp"), None, None),
        P(("grp", "exp"), None, None),
        P("grp", None),
        P("grp", None),
        P("grp", None),
        P("grp", None),
        P("grp", None),
        P("grp", None),
        P("grp", None),
        P("grp", None),
        P("grp", None),
        P("grp", None),
        P("grp", None),
        P("grp", None),
        P("exp", None, "grp"),
        P("exp", None, "grp"),
        P("exp", None, "grp"),
        P("exp", "grp", None),
        P("exp", "grp", None),
        P("exp", "grp", None),
    )
    out_specs = (
        P(("grp", "exp"), None, None),
        P(("grp", "exp"), None, None),
        P("grp", None),
        P("grp", None),
        P("grp", None),
        P("grp", None),
        P("grp", None),
        P("grp", None),
        P("grp", None),
        P("grp", None),
        P("grp", None),
        P("grp", None),
        P("grp", None),
        P("grp", None),
        P("exp", None, "grp"),
        P("exp", None, "grp"),
        P("exp", None, "grp"),
        P("exp", "grp", None),
        P("exp", "grp", None),
        P("exp", "grp", None),
    )
    return jax.shard_map(
        on_device, mesh=mesh, in_specs=in_specs, out_specs=out_specs, check_vma=False
    )
```

```python
import jax
import jax.numpy as jnp
from jax import lax
from jax.experimental import pallas as pl
from jax.experimental.pallas import tpu as pltpu
from jax.sharding import PartitionSpec as P

HEADS = 12
HEAD_DIM = 64
STEP = 10
D = 768
TOK = 197
ROWS = 208
EXPERTS = 16
CAP = 33
SLOTS = EXPERTS * CAP
DENSE = 3200
GRP = 8
OWN = D // GRP
PIECE = 48
WIDE = 384
HID = 384
HALF = D // 2

norm_epsilon = 1e-06
beta_first = 0.9
beta_second = 0.999
adam_epsilon = 1e-08
weight_decay = 0.1
score_scale = HEAD_DIM ** (-0.5)
low = jnp.bfloat16
full = jnp.float32


def dot(a, b, dims=((1,), (0,))):
    return lax.dot_general(a, b, (dims, ((), ())), preferred_element_type=jnp.float32)


NT = ((1,), (1,))
TN = ((0,), (0,))


def unit_rows(values):
    centered = values - jnp.mean(values, axis=-1, keepdims=True)
    variance = jnp.mean(centered * centered, axis=-1, keepdims=True)
    scale = lax.rsqrt(variance + norm_epsilon)
    return centered * scale, scale


def norm_rows(w_ref):
    return w_ref[:, 3072:3200].astype(full).T[16:24]


def pack_kernel(qkv_ref, proj_ref, router_ref, norm_ref, *refs):
    first_out, second_out, qkv_in, proj_in, sem = refs
    loads = [
        pltpu.make_async_copy(source, target, sem.at[i])
        for i, (source, target) in enumerate(((qkv_ref, qkv_in), (proj_ref, proj_in)))
    ]
    for load in loads:
        load.start()
    rest = [router_ref[...], norm_ref[...], jnp.zeros((DENSE - 3092, OWN), full)]
    rest = jnp.concatenate(rest, axis=0).T.astype(low)
    for load in loads:
        load.wait()
    for i, out_ref in enumerate((first_out, second_out)):
        rows = slice(i * PIECE, (i + 1) * PIECE)
        out_ref[:, 0:2304] = qkv_in[rows, :].astype(low)
        out_ref[:, 2304:3072] = proj_in[rows, :].astype(low)
        out_ref[:, 3072:3200] = rest[rows, :]


def dense_pieces(first, second):
    def along(step, value):
        hops = [(2 * x + c, 2 * ((x + step) % 4) + c) for x in range(4) for c in range(2)]
        return lax.ppermute(value, "grp", hops)

    def across(value):
        return lax.ppermute(value, "grp", [(i, i ^ 1) for i in range(GRP)])

    up_first, down_second = along(1, first), along(3, second)
    up_second, down_first = along(1, second), along(3, first)
    far_first, far_second = along(1, up_first), along(3, down_second)
    here = [first, second, up_first, up_second, down_first, down_second, far_first, far_second]
    return here + [across(piece) for piece in here]


def piece_rows(place):
    x, c = place // 2, place % 2
    rows = []
    for core in (c, 1 - c):
        for step in (0, 3, 1, 2):
            near = OWN * (2 * ((x + step) % 4) + core)
            rows += [near, near + PIECE]
    return jnp.stack(rows).astype(jnp.int32)


def dense_copies(rows_ref, pieces, w_ref, sem):
    copies = []
    for i, piece in enumerate(pieces):
        at = pl.multiple_of(rows_ref[i], PIECE)
        copies.append(pltpu.make_async_copy(piece, w_ref.at[pl.ds(at, PIECE), :], sem.at[i]))
        copies[-1].start()
    return copies


class Moves:
    def __init__(self, sem):
        self.sem, self.open = sem, {}

    def start(self, name, source, target):
        self.open[name] = pltpu.make_async_copy(source, target, self.sem.at[len(self.open)])
        self.open[name].start()

    def wait(self, *names):
        for name in names:
            self.open[name].wait()


def padded(ref, pad_ref):
    pad_ref[192:ROWS, :] = jnp.zeros((ROWS - 192, D), full)
    pad_ref[0:TOK, :] = ref[0].astype(full)
    return pad_ref[...]


def lanes(shape):
    return lax.broadcasted_iota(jnp.int32, shape, 1)


def half_masks():
    lane = lanes((1, 128))
    first = (lane < HEAD_DIM).astype(full)
    return first.astype(low), (1.0 - first).astype(low)


def forward_kernel(rows_ref, ids_ref, keep_ref, trow_ref, x_hbm, g_hbm, *refs):
    pieces, refs = refs[:16], refs[16:]
    outs, refs = refs[:8], refs[8:]
    send_ref = outs[0]
    m_ref, a_ref, qkv_ref, p_ref, o_ref, c_ref, r_ref = refs[:7]
    x_ref, g_ref, x_pad, g_pad, w_ref, w_sem, sem, spare = refs[7:]
    moves = Moves(sem)
    moves.start("x", x_hbm, x_ref)
    copies = dense_copies(rows_ref, pieces, w_ref, w_sem)
    moves.start("g", g_hbm, g_ref)
    moves.wait("x")
    x = padded(x_ref, x_pad)
    unit = unit_rows(x)[0]
    moves.wait("g")
    g = padded(g_ref, g_pad)
    for copy in copies:
        copy.wait()
    norms = norm_rows(w_ref)
    a = (unit * norms[0:1] + norms[1:2]).astype(low)
    a_ref[...] = a
    moves.start("a", a_ref, outs[2])
    for part in range(3):
        cols = slice(part * D, part * D + D)
        qkv_ref[:, cols] = dot(a, w_ref[:, cols]).astype(low)
    moves.start("qkv", qkv_ref, outs[3])
    first, second = half_masks()
    seen = lanes((ROWS, ROWS)) < TOK
    low_half = lanes((ROWS, 128)) < HEAD_DIM
    for pair in range(HEADS // 2):
        at = pair * 128
        q = qkv_ref[:, at : at + 128]
        k = qkv_ref[:, D + at : D + at + 128]
        v = qkv_ref[:, 2 * D + at : 2 * D + at + 128]
        mixed = []
        for side, mask in enumerate((first, second)):
            s = dot(q * mask, k, NT) * score_scale
            s = jnp.where(seen, s, -1e30)
            e = jnp.exp(s - jnp.max(s, axis=1, keepdims=True))
            p = (e / jnp.sum(e, axis=1, keepdims=True)).astype(low)
            p_ref[2 * pair + side] = p
            mixed.append(dot(p, v))
        o_ref[:, at : at + 128] = jnp.where(low_half, mixed[0], mixed[1]).astype(low)
    moves.start("p", p_ref, outs[4])
    moves.start("o", o_ref, outs[5])
    m = x + dot(o_ref[...], w_ref[:, 2304:3072])
    m_ref[...] = m
    moves.start("m", m_ref, outs[1])
    c = (unit_rows(m)[0] * norms[2:3] + norms[3:4]).astype(low)
    c_ref[...] = c
    moves.start("c", c_ref, outs[6])
    lane = lanes((ROWS, 128))
    logits = jnp.where(lane < EXPERTS, dot(c, w_ref[:, 3072:3200]), -1e30)
    e = jnp.exp(logits - jnp.max(logits, axis=1, keepdims=True))
    r = e / jnp.sum(e, axis=1, keepdims=True)
    r_ref[...] = r
    moves.start("r", r_ref, outs[7])
    slot = lax.broadcasted_iota(jnp.int32, (SLOTS, ROWS), 0)
    picks, grads = [], []
    for j in range(2):
        chosen = lane == ids_ref[:, j : j + 1]
        gate = jnp.sum(jnp.where(chosen, r, 0.0), axis=1, keepdims=True) * keep_ref[:, j : j + 1]
        picks.append((slot == trow_ref[j : j + 1, :]).astype(full).astype(low))
        grads.append((gate * g).astype(low))
    for part, value in enumerate(
        (dot(picks[0] + picks[1], c), dot(picks[0], grads[0]) + dot(picks[1], grads[1]))
    ):
        spare[...] = value
        for e in range(EXPERTS):
            rows = slice(e * CAP, (e + 1) * CAP)
            send_ref[e, :, part * D : (part + 1) * D] = spare[rows, :].astype(low)
    moves.wait("a", "qkv", "p", "o", "m", "c", "r")


def expert_kernel(
    got_ref, w_ref, back_ref, h_ref, du_ref, xt_ref, dzt_ref, z_sum, dx_sum, xs, dzs
):
    step = pl.program_id(0)

    @pl.when(step == 0)
    def _():
        for e in range(EXPERTS):
            rows = slice(e * CAP, (e + 1) * CAP)
            z_sum[rows, :] = got_ref[e, :, 0:D].astype(full)
            dx_sum[rows, :] = got_ref[e, :, D:].astype(full)
        xs[...] = z_sum[...].astype(low)
        dzs[...] = dx_sum[...].astype(low)
        xt_ref[...] = xs[...].T
        dzt_ref[...] = dzs[...].T
        z_sum[...] = jnp.zeros_like(z_sum)
        dx_sum[...] = jnp.zeros_like(dx_sum)

    wi = jnp.concatenate([w_ref[0:D, 0:HID], w_ref[D:, 0:HID]], axis=1)
    wot = jnp.concatenate([w_ref[0:D, HID:], w_ref[D:, HID:]], axis=1)
    u = dot(xs[...], wi)
    dh = dot(dzs[...], wot)
    square = u * u
    inner = u * (0.7978845608028654 + (0.7978845608028654 * 0.044715) * square)
    t = jnp.tanh(inner)
    half = 0.5 * t + 0.5
    h = (u * half).astype(low)
    slope = (0.5 * u) * (1.0 - t * t)
    slope = slope * (0.7978845608028654 + (3 * 0.7978845608028654 * 0.044715) * square) + half
    du = (slope * dh).astype(low)
    h_ref[...] = h
    du_ref[...] = du
    z_sum[...] += dot(h, wot, NT)
    dx_sum[...] += dot(du, wi, NT)

    @pl.when(step == pl.num_programs(0) - 1)
    def _():
        for e in range(EXPERTS):
            rows = slice(e * CAP, (e + 1) * CAP)
            back_ref[e, :, 0:D] = z_sum[rows, :].astype(low)
            back_ref[e, :, D:] = dx_sum[rows, :].astype(low)


def expert_grad_kernel(xt_ref, dzt_ref, h_ref, du_ref, out_ref):
    gi = dot(xt_ref[...], du_ref[...]).astype(low)
    go = dot(dzt_ref[...], h_ref[...]).astype(low)
    for i in range(2):
        cols = slice(i * HID, (i + 1) * HID)
        out_ref[i * HALF : (i + 1) * HALF, 0:HID] = gi[:, cols]
        out_ref[i * HALF : (i + 1) * HALF, HID:] = go[:, cols]


def spread(grad, part, grads_ref):
    for g in range(GRP):
        for r in range(2):
            rows = slice(g * OWN + r * PIECE, g * OWN + (r + 1) * PIECE)
            for k in range(2):
                cols = slice(k * WIDE, (k + 1) * WIDE)
                grads_ref[g * 2 + r, part * 2 + k] = grad[rows, cols]


def backward_kernel(rows_ref, ids_ref, tcol_ref, keep_ref, back_ref, *refs):
    ins, pieces, refs = refs[:9], refs[9:25], refs[25:]
    outs, refs = refs[:4], refs[4:]
    m_ref, r_ref, g_ref, c_ref, o_ref, qkv_ref, p_ref, a_ref, x_ref = refs[:9]
    result_ref, image_ref, grads_ref, extra_ref = refs[9:13]
    x_pad, g_pad, spare, dqkv, w_ref, w_sem, sem = refs[13:]
    moves = Moves(sem)
    for name in range(1, 5):
        moves.start(name, ins[name - 1], refs[name - 1])
    copies = dense_copies(rows_ref, pieces, w_ref, w_sem)
    for name in range(5, 10):
        moves.start(name, ins[name - 1], refs[name - 1])

    def rows_of(part):
        for e in range(EXPERTS):
            rows = slice(e * CAP, (e + 1) * CAP)
            spare[rows, :] = back_ref[e, :, part * D : (part + 1) * D].astype(full)
        return spare[...].astype(low)

    moves.wait(1, 2, 3)
    g = padded(g_ref, g_pad)
    m = m_ref[...]
    r = r_ref[...]
    lane = lanes((ROWS, 128))
    slot = lanes((ROWS, SLOTS))
    z = rows_of(0)
    total = m
    dr = jnp.zeros((ROWS, 128), full)
    picks = []
    for j in range(2):
        pick = (slot == tcol_ref[:, j : j + 1]).astype(full).astype(low)
        picks.append(pick)
        keep = keep_ref[:, j : j + 1]
        chosen = lane == ids_ref[:, j : j + 1]
        gate = jnp.sum(jnp.where(chosen, r, 0.0), axis=1, keepdims=True) * keep
        zj = dot(pick, z)
        total = total + gate * zj
        dgate = jnp.sum(g * zj, axis=1, keepdims=True) * keep
        dr = dr + jnp.where(chosen, dgate, 0.0)
    result_ref[0] = total[0:TOK].astype(low)
    moves.start("result", result_ref, outs[0])
    for copy in copies:
        copy.wait()
    norms = norm_rows(w_ref)
    moves.wait(4)
    dl = (r * (dr - jnp.sum(dr * r, axis=1, keepdims=True))).astype(low)
    c = c_ref[...]
    extra_ref[0:16, :] = dot(dl, c, TN)[0:16]
    dc = dot(dl, w_ref[:, 3072:3200], NT) + dot(picks[0] + picks[1], rows_of(1))
    xh, scale = unit_rows(m)
    dn2 = jnp.sum(dc * xh, axis=0, keepdims=True)
    dn3 = jnp.sum(dc, axis=0, keepdims=True)
    dxh = dc * norms[2:3]
    dm = g + scale * (
        dxh
        - jnp.mean(dxh, axis=1, keepdims=True)
        - xh * jnp.mean(dxh * xh, axis=1, keepdims=True)
    )
    dmb = dm.astype(low)
    moves.wait(5)
    spread(dot(o_ref[...].T, dmb).astype(low), 3, grads_ref)
    moves.start("proj", grads_ref.at[:, 6:8], outs[2].at[:, 6:8])
    do = dot(dmb, w_ref[:, 2304:3072], NT).astype(low)
    first, second = half_masks()
    low_half = lane < HEAD_DIM
    moves.wait(6, 7)
    for pair in range(HEADS // 2):
        at = pair * 128
        q = qkv_ref[:, at : at + 128]
        k = qkv_ref[:, D + at : D + at + 128]
        v = qkv_ref[:, 2 * D + at : 2 * D + at + 128]
        dop = do[:, at : at + 128]
        parts = []
        for side, mask in enumerate((first, second)):
            p_low = p_ref[2 * pair + side]
            p = p_low.astype(full)
            dp = dot(dop * mask, v, NT)
            ds = (p * (dp - jnp.sum(dp * p, axis=1, keepdims=True))).astype(low)
            parts.append((dot(ds, k), dot(ds, q, TN), dot(p_low, dop, TN)))
        for which, factor in enumerate((score_scale, score_scale, 1.0)):
            both = jnp.where(low_half, parts[0][which], parts[1][which]) * factor
            dqkv[:, which * D + at : which * D + at + 128] = both.astype(low)
    moves.wait(8, 9)
    at_rows = a_ref[...].T
    da = jnp.zeros((ROWS, D), full)
    for part in range(3):
        cols = slice(part * D, part * D + D)
        spread(dot(at_rows, dqkv[:, cols]).astype(low), part, grads_ref)
        groups = slice(2 * part, 2 * part + 2)
        moves.start(("qkv", part), grads_ref.at[:, groups], outs[2].at[:, groups])
        da = da + dot(dqkv[:, cols], w_ref[:, cols], NT)
    xh, scale = unit_rows(padded(x_ref, x_pad))
    extra_ref[16:24, :] = jnp.concatenate(
        [
            jnp.sum(da * xh, axis=0, keepdims=True),
            jnp.sum(da, axis=0, keepdims=True),
            dn2,
            dn3,
            jnp.zeros((4, D), full),
        ],
        axis=0,
    )
    moves.start("extra", extra_ref, outs[3])
    dxh = da * norms[0:1]
    dx = dm + scale * (
        dxh
        - jnp.mean(dxh, axis=1, keepdims=True)
        - xh * jnp.mean(dxh * xh, axis=1, keepdims=True)
    )
    image_ref[0] = dx[0:TOK]
    moves.start("image", image_ref, outs[1])
    moves.wait("result", "proj", ("qkv", 0), ("qkv", 1), ("qkv", 2), "extra", "image")


def adamw(master, first, second, gradient, rate):
    first = beta_first * first + (1.0 - beta_first) * gradient
    second = beta_second * second + (1.0 - beta_second) * gradient * gradient
    corrected = first / (1.0 - beta_first**STEP)
    scaled = jnp.sqrt(second / (1.0 - beta_second**STEP)) + adam_epsilon
    return (first, second, master - rate * (corrected / scaled + weight_decay * master))


def owner_kernel(pieces_ref, *refs):
    inputs, outputs = refs[:6], refs[6:]

    def update(side, rate):
        for r in range(2):
            rows = slice(r * PIECE, (r + 1) * PIECE)
            for k in range(2):
                cols = slice(k * WIDE, (k + 1) * WIDE)
                grad = pieces_ref[r, k].astype(full)
                new = adamw(*[ref[rows, cols] for ref in inputs[side : side + 3]], grad, rate)
                for ref, value in zip(outputs[side : side + 3], new):
                    ref[rows, cols] = value

    last = pl.program_id(0) == 3
    pl.when(jnp.logical_not(last))(lambda: update(0, 0.04))
    pl.when(last)(lambda: update(3, 0.2))


def expert_step_kernel(inner_ref, outer_ref, *refs):
    inputs, outputs = refs[:6], refs[-6:]
    new = adamw(*[ref[0] for ref in inputs[:3]], inner_ref[...].astype(full), 0.04)
    new = new + adamw(*[ref[0] for ref in inputs[3:]], outer_ref[...].astype(full).T, 0.15)
    for ref, value in zip(outputs, new):
        ref[0] = value


def expert_step(half, grad, arrays, partial):
    inner = pl.BlockSpec((1, HALF, 128), lambda i: (0, half, i))
    outer = pl.BlockSpec((1, 128, HALF), lambda i: (0, i, half))
    return pl.pallas_call(
        expert_step_kernel,
        grid=(3,),
        out_shape=tuple(hbm(*a.shape) for a in arrays),
        in_specs=[
            pl.BlockSpec((HALF, 128), lambda i: (0, i)),
            pl.BlockSpec((HALF, 128), lambda i: (0, 3 + i)),
        ]
        + [inner] * 3
        + [outer] * 3
        + in_place(len(partial)),
        out_specs=(inner,) * 3 + (outer,) * 3,
        input_output_aliases={8 + i: i for i in range(len(partial))},
        compiler_params=params(16),
        cost_estimate=pl.CostEstimate(
            flops=10**7, bytes_accessed=8 * 10**6, transcendentals=10**6
        ),
        name="expert_step",
    )(*pinned([grad, grad, *arrays, *partial]))


def shape(*dims, dtype=jnp.float32):
    return jax.ShapeDtypeStruct(dims, dtype)


def in_vmem(count):
    return [pl.BlockSpec(memory_space=pltpu.VMEM)] * count


def pinned(values):
    return [pltpu.with_memory_space_constraint(v, pltpu.HBM) for v in values]


def hbm(*dims, dtype=jnp.float32):
    return pltpu.HBM(dims, dtype)


def in_smem():
    return pl.BlockSpec(memory_space=pltpu.SMEM)


def in_place(count):
    return [pl.BlockSpec(memory_space=pl.ANY)] * count


def params(mib):
    return pltpu.CompilerParams(vmem_limit_bytes=mib * 2**20)


def pack(qkv, proj, router, norm):
    return pl.pallas_call(
        pack_kernel,
        out_shape=(shape(PIECE, DENSE, dtype=low),) * 2,
        in_specs=in_place(2) + in_vmem(2),
        out_specs=tuple(in_vmem(2)),
        scratch_shapes=vmem_like((qkv, proj)) + [pltpu.SemaphoreType.DMA((2,))],
        compiler_params=params(16),
        cost_estimate=pl.CostEstimate(flops=10**5, bytes_accessed=2 * 10**6, transcendentals=0),
        name="pack",
    )(*pinned((qkv, proj)), router.T, norm.T)


def flat_type(value):
    return value.inner_aval if hasattr(value, "inner_aval") else value


def vmem_like(shapes):
    return [pltpu.VMEM(s.shape, s.dtype) for s in map(flat_type, shapes)]


def token_forward(*args):
    outs = (
        pltpu.VMEM((EXPERTS, CAP, 2 * D), low),
        hbm(ROWS, D),
        hbm(ROWS, D, dtype=low),
        hbm(ROWS, 3 * D, dtype=low),
        hbm(HEADS, ROWS, ROWS, dtype=low),
        hbm(ROWS, D, dtype=low),
        hbm(ROWS, D, dtype=low),
        hbm(ROWS, 128),
    )
    return pl.pallas_call(
        forward_kernel,
        out_shape=outs,
        in_specs=[in_smem()] + in_vmem(3) + in_place(18),
        out_specs=tuple(in_vmem(1) + in_place(7)),
        scratch_shapes=vmem_like(outs[1:])
        + [pltpu.VMEM((1, TOK, D), low)] * 2
        + [pltpu.VMEM((ROWS, D), full)] * 2
        + [
            pltpu.VMEM((D, DENSE), low),
            pltpu.SemaphoreType.DMA((16,)),
            pltpu.SemaphoreType.DMA((10,)),
            pltpu.VMEM((SLOTS, D), full),
        ],
        compiler_params=params(40),
        cost_estimate=pl.CostEstimate(
            flops=4 * 10**9, bytes_accessed=12 * 10**6, transcendentals=10**6
        ),
        name="token_forward",
    )(*args[:4], *pinned(args[4:]))


def experts_both_ways(got, weights):
    return pl.pallas_call(
        expert_kernel,
        grid=(GRP // 2,),
        out_shape=(
            pltpu.VMEM((EXPERTS, CAP, 2 * D), low),
            hbm(SLOTS, GRP * HID, dtype=low),
            hbm(SLOTS, GRP * HID, dtype=low),
            hbm(D, SLOTS, dtype=low),
            hbm(D, SLOTS, dtype=low),
        ),
        in_specs=[
            pl.BlockSpec(memory_space=pltpu.VMEM),
            pl.BlockSpec((2 * D, D), lambda i: (i, 0)),
        ],
        out_specs=(
            pl.BlockSpec(memory_space=pltpu.VMEM),
            pl.BlockSpec((SLOTS, 2 * HID), lambda i: (0, i)),
            pl.BlockSpec((SLOTS, 2 * HID), lambda i: (0, i)),
            pl.BlockSpec((D, SLOTS), lambda i: (0, 0)),
            pl.BlockSpec((D, SLOTS), lambda i: (0, 0)),
        ),
        scratch_shapes=[
            pltpu.VMEM((SLOTS, D), full),
            pltpu.VMEM((SLOTS, D), full),
            pltpu.VMEM((SLOTS, D), low),
            pltpu.VMEM((SLOTS, D), low),
        ],
        compiler_params=params(44),
        cost_estimate=pl.CostEstimate(
            flops=10 * 10**9, bytes_accessed=23 * 10**6, transcendentals=2 * 10**6
        ),
        name="experts",
    )(got, *pinned([weights]))


def expert_grads(half, xt, dzt, h, du):
    return pl.pallas_call(
        expert_grad_kernel,
        grid=(GRP // 2,),
        out_shape=hbm(GRP * HALF, D, dtype=low),
        in_specs=[
            pl.BlockSpec((HALF, SLOTS), lambda i: (half, 0)),
            pl.BlockSpec((HALF, SLOTS), lambda i: (half, 0)),
            pl.BlockSpec((SLOTS, 2 * HID), lambda i: (0, i)),
            pl.BlockSpec((SLOTS, 2 * HID), lambda i: (0, i)),
        ],
        out_specs=pl.BlockSpec((2 * HALF, D), lambda i: (i, 0)),
        compiler_params=params(32),
        cost_estimate=pl.CostEstimate(
            flops=3 * 10**9, bytes_accessed=13 * 10**6, transcendentals=0
        ),
        name="expert_grads",
    )(*pinned([xt, dzt, h, du]))


def token_backward(*args):
    outs = (
        hbm(1, TOK, D, dtype=low),
        hbm(1, TOK, D),
        hbm(16, 8, PIECE, WIDE, dtype=low),
        hbm(24, D),
    )
    return pl.pallas_call(
        backward_kernel,
        out_shape=outs,
        in_specs=[in_smem()] + in_vmem(4) + in_place(25),
        out_specs=tuple(in_place(4)),
        scratch_shapes=vmem_like(args[5:14])
        + vmem_like(outs)
        + [
            pltpu.VMEM((ROWS, D), full),
            pltpu.VMEM((ROWS, D), full),
            pltpu.VMEM((SLOTS, D), full),
            pltpu.VMEM((ROWS, 3 * D), low),
            pltpu.VMEM((D, DENSE), low),
            pltpu.SemaphoreType.DMA((16,)),
            pltpu.SemaphoreType.DMA((17,)),
        ],
        compiler_params=params(48),
        cost_estimate=pl.CostEstimate(
            flops=40 * 10**9, bytes_accessed=18 * 10**6, transcendentals=10**4
        ),
        name="token_backward",
    )(*args[:5], *pinned(args[5:]))


def owner_step(pieces, arrays):
    qkv = pl.BlockSpec((OWN, D), lambda i: (0, jnp.minimum(i, 2)))
    proj = pl.BlockSpec((OWN, D), lambda i: (0, 0))
    return pl.pallas_call(
        owner_kernel,
        grid=(4,),
        out_shape=tuple(hbm(*a.shape) for a in arrays),
        in_specs=[pl.BlockSpec((2, 2, PIECE, WIDE), lambda i: (0, i, 0, 0))]
        + [qkv] * 3
        + [proj] * 3,
        out_specs=(qkv,) * 3 + (proj,) * 3,
        compiler_params=params(16),
        cost_estimate=pl.CostEstimate(
            flops=10**7, bytes_accessed=8 * 10**6, transcendentals=10**6
        ),
        name="owner_step",
    )(pieces, *pinned(arrays))


def on_device(
    images,
    cotangent,
    expert_ids,
    kept_routes,
    qkv_master,
    qkv_first,
    qkv_second,
    proj_master,
    proj_first,
    proj_second,
    router_master,
    router_first,
    router_second,
    norm_master,
    norm_first,
    norm_second,
    inner_master,
    inner_first,
    inner_second,
    outer_master,
    outer_first,
    outer_second,
):
    pieces = dense_pieces(*pack(qkv_master, proj_master, router_master, norm_master))
    rows = piece_rows(lax.axis_index("grp"))
    mine = jnp.concatenate([inner_master[0].astype(low), outer_master[0].astype(low).T], axis=1)
    mine, *_ = lax.optimization_barrier((mine, pieces[2], pieces[5]))
    weights = lax.all_gather(mine, "grp", axis=0, tiled=True)

    ids = expert_ids.reshape(TOK, 2)
    kept = kept_routes.reshape(TOK, 2)
    flat = ids.reshape(-1)
    marks = (flat[:, None] == jnp.arange(EXPERTS, dtype=jnp.int32)[None, :]).astype(jnp.int32)
    slots = jnp.sum((jnp.cumsum(marks, axis=0) - marks) * marks, axis=1).reshape(TOK, 2)
    target = jnp.where(kept > 0, ids * CAP + slots, -1)
    padding = ((0, ROWS - TOK), (0, 0))
    target = jnp.pad(target, padding, constant_values=-1)
    ids = jnp.pad(ids, padding, constant_values=-1)
    keep = jnp.pad(kept.astype(full), padding)

    send, m, a, qkv, p, o, c, r = token_forward(
        rows, ids, keep, target.T, images, cotangent, *pieces
    )
    got = lax.all_to_all(send, "exp", split_axis=0, concat_axis=0, tiled=True)
    back, *kept_parts = experts_both_ways(got, weights)
    h, du, xt, dzt = kept_parts
    back = lax.all_to_all(back, "exp", split_axis=0, concat_axis=0, tiled=True)
    head = expert_grads(0, xt, dzt, h, du)
    tail = expert_grads(1, xt, dzt, h, du)
    head = lax.psum_scatter(head, "grp", scatter_dimension=0, tiled=True)
    result, image_grad, grads, extra = token_backward(
        rows, ids, target, keep, back, m, r, cotangent, c, o, qkv, p, a, images, *pieces
    )
    grads, head = lax.optimization_barrier((grads, head))
    grads = lax.psum_scatter(
        grads.reshape(GRP * 16 * PIECE, WIDE), "grp", scatter_dimension=0, tiled=True
    )
    experts = (
        inner_master,
        inner_first,
        inner_second,
        outer_master,
        outer_first,
        outer_second,
    )
    partial = expert_step(0, head, experts, ())

    extra = jnp.moveaxis(extra.reshape(24, GRP, OWN), 1, 0)
    extra = lax.all_to_all(extra, "grp", split_axis=0, concat_axis=0, tiled=True)
    extra = jnp.broadcast_to(jnp.sum(extra, axis=0)[None], (EXPERTS, 24, OWN))
    extra = lax.all_to_all(extra, "exp", split_axis=0, concat_axis=0, tiled=True)
    extra = jnp.sum(extra, axis=0).T
    grads, tail, extra = lax.optimization_barrier((grads, tail, extra))
    tail = lax.psum_scatter(tail, "grp", scatter_dimension=0, tiled=True)

    pieces = lax.all_to_all(
        grads.reshape(16, PIECE, WIDE), "exp", split_axis=0, concat_axis=0, tiled=True
    )
    piece = jnp.sum(pieces.astype(full), axis=0).astype(low)
    pieces = lax.all_to_all(
        jnp.broadcast_to(piece[None], (16, PIECE, WIDE)),
        "exp",
        split_axis=0,
        concat_axis=0,
        tiled=True,
    )
    qkv_moment, qkv_square, qkv_weight, proj_moment, proj_square, proj_weight = owner_step(
        pieces.reshape(2, 8, PIECE, WIDE),
        (qkv_master, qkv_first, qkv_second, proj_master, proj_first, proj_second),
    )
    router_moment, router_square, router_weight = adamw(
        router_master, router_first, router_second, extra[:, 0:16], 0.03
    )
    norm_moment, norm_square, norm_weight = adamw(
        norm_master, norm_first, norm_second, extra[:, 16:20], 0.3
    )
    (
        inner_moment,
        inner_square,
        inner_weight,
        outer_moment,
        outer_square,
        outer_weight,
    ) = expert_step(1, tail, experts, partial)
    return (
        result,
        image_grad,
        qkv_moment,
        qkv_square,
        qkv_weight,
        proj_moment,
        proj_square,
        proj_weight,
        router_moment,
        router_square,
        router_weight,
        norm_moment,
        norm_square,
        norm_weight,
        inner_moment,
        inner_square,
        inner_weight,
        outer_moment,
        outer_square,
        outer_weight,
    )


def solution(mesh):
    in_specs = (
        P(("grp", "exp"), None, None),
        P(("grp", "exp"), None, None),
        P(("grp", "exp"), None, None),
        P(("grp", "exp"), None, None),
        P("grp", None),
        P("grp", None),
        P("grp", None),
        P("grp", None),
        P("grp", None),
        P("grp", None),
        P("grp", None),
        P("grp", None),
        P("grp", None),
        P("grp", None),
        P("grp", None),
        P("grp", None),
        P("exp", None, "grp"),
        P("exp", None, "grp"),
        P("exp", None, "grp"),
        P("exp", "grp", None),
        P("exp", "grp", None),
        P("exp", "grp", None),
    )
    out_specs = (
        P(("grp", "exp"), None, None),
        P(("grp", "exp"), None, None),
        P("grp", None),
        P("grp", None),
        P("grp", None),
        P("grp", None),
        P("grp", None),
        P("grp", None),
        P("grp", None),
        P("grp", None),
        P("grp", None),
        P("grp", None),
        P("grp", None),
        P("grp", None),
        P("exp", None, "grp"),
        P("exp", None, "grp"),
        P("exp", None, "grp"),
        P("exp", "grp", None),
        P("exp", "grp", None),
        P("exp", "grp", None),
    )
    return jax.shard_map(
        on_device, mesh=mesh, in_specs=in_specs, out_specs=out_specs, check_vma=False
    )
```

```python
import jax
import jax.numpy as jnp
from jax import lax
from jax.experimental import pallas as pl
from jax.experimental.pallas import tpu as pltpu
from jax.sharding import PartitionSpec as P

HEADS = 12
HEAD_DIM = 64
STEP = 10
D = 768
TOK = 197
ROWS = 208
EXPERTS = 16
CAP = 33
SLOTS = EXPERTS * CAP
DENSE = 3200
GRP = 8
OWN = D // GRP
PIECE = 48
WIDE = 384
HID = 384
BLOCK = 4 * PIECE + 16

norm_epsilon = 1e-06
beta_first = 0.9
beta_second = 0.999
adam_epsilon = 1e-08
weight_decay = 0.1
score_scale = HEAD_DIM ** (-0.5)
low = jnp.bfloat16
full = jnp.float32


def dot(a, b, dims=((1,), (0,))):
    return lax.dot_general(a, b, (dims, ((), ())), preferred_element_type=jnp.float32)


NT = ((1,), (1,))
TN = ((0,), (0,))


def unit_rows(values):
    centered = values - jnp.mean(values, axis=-1, keepdims=True)
    variance = jnp.mean(centered * centered, axis=-1, keepdims=True)
    scale = lax.rsqrt(variance + norm_epsilon)
    return centered * scale, scale


def norm_rows(w_ref):
    return w_ref[:, 3072:3200].astype(full).T[16:24]


def pack_kernel(qkv_ref, proj_ref, router_ref, norm_ref, *refs):
    first_out, second_out, qkv_in, proj_in, router_in, norm_in, sem = refs
    sources = (qkv_ref, proj_ref, router_ref, norm_ref)
    loads = [
        pltpu.make_async_copy(source, target, sem.at[i])
        for i, (source, target) in enumerate(zip(sources, refs[2:6]))
    ]
    for load in loads:
        load.start()
    for load in loads[2:]:
        load.wait()
    rest = [router_in[...], norm_in[...], jnp.zeros((DENSE - 3092, OWN), full)]
    rest = jnp.concatenate(rest, axis=0).T.astype(low)
    for load in loads[:2]:
        load.wait()
    for i, out_ref in enumerate((first_out, second_out)):
        rows = slice(i * PIECE, (i + 1) * PIECE)
        out_ref[:, 0:2304] = qkv_in[rows, :].astype(low)
        out_ref[:, 2304:3072] = proj_in[rows, :].astype(low)
        out_ref[:, 3072:3200] = rest[rows, :]


def dense_pieces(first, second):
    def along(step, value):
        hops = [(2 * x + c, 2 * ((x + step) % 4) + c) for x in range(4) for c in range(2)]
        return lax.ppermute(value, "grp", hops)

    def across(value):
        return lax.ppermute(value, "grp", [(i, i ^ 1) for i in range(GRP)])

    up_first, down_second = along(1, first), along(3, second)
    up_first, down_second, again, other = lax.optimization_barrier(
        (up_first, down_second, second, first)
    )
    up_second, down_first = along(1, again), along(3, other)
    far_first, far_second = along(1, up_first), along(3, down_second)
    here = [first, second, up_first, up_second, down_first, down_second, far_first, far_second]
    return here + [across(piece) for piece in here]


def piece_rows(place):
    x, c = place // 2, place % 2
    rows = []
    for core in (c, 1 - c):
        for step in (0, 3, 1, 2):
            near = OWN * (2 * ((x + step) % 4) + core)
            rows += [near, near + PIECE]
    return jnp.stack(rows + [x, c]).astype(jnp.int32)


def dense_copies(rows_ref, pieces, w_ref, sem):
    copies = []
    for i, piece in enumerate(pieces):
        at = pl.multiple_of(rows_ref[i], PIECE)
        copies.append(pltpu.make_async_copy(piece, w_ref.at[pl.ds(at, PIECE), :], sem.at[i]))
        copies[-1].start()
    return copies


class Moves:
    def __init__(self, sem):
        self.sem, self.open = sem, {}

    def start(self, name, source, target):
        self.open[name] = pltpu.make_async_copy(source, target, self.sem.at[len(self.open)])
        self.open[name].start()

    def wait(self, *names):
        for name in names:
            self.open[name].wait()


def slot_rows(e):
    return slice(e * CAP, (e + 1) * CAP)


def padded(ref, pad_ref):
    pad_ref[192:ROWS, :] = jnp.zeros((ROWS - 192, D), full)
    pad_ref[0:TOK, :] = ref[0].astype(full)
    return pad_ref[...]


def lanes(shape):
    return lax.broadcasted_iota(jnp.int32, shape, 1)


def half_masks():
    lane = lanes((1, 128))
    first = (lane < HEAD_DIM).astype(full)
    return first.astype(low), (1.0 - first).astype(low)


def forward_kernel(rows_ref, ids_ref, keep_ref, trow_ref, x_hbm, g_hbm, *refs):
    pieces, refs = refs[:16], refs[16:]
    outs, refs = refs[:8], refs[8:]
    send_ref = outs[0]
    m_ref, a_ref, qkv_ref, p_ref, o_ref, c_ref, r_ref = refs[:7]
    x_ref, g_ref, x_pad, g_pad, w_ref, w_sem, sem, spare = refs[7:]
    moves = Moves(sem)
    moves.start("x", x_hbm, x_ref)
    copies = dense_copies(rows_ref, pieces, w_ref, w_sem)
    moves.start("g", g_hbm, g_ref)
    moves.wait("x")
    x = padded(x_ref, x_pad)
    unit = unit_rows(x)[0]
    moves.wait("g")
    g = padded(g_ref, g_pad)
    for copy in copies:
        copy.wait()
    norms = norm_rows(w_ref)
    a = (unit * norms[0:1] + norms[1:2]).astype(low)
    a_ref[...] = a
    moves.start("a", a_ref, outs[2])
    for part in range(3):
        cols = slice(part * D, part * D + D)
        qkv_ref[:, cols] = dot(a, w_ref[:, cols]).astype(low)
    moves.start("qkv", qkv_ref, outs[3])
    first, second = half_masks()
    seen = lanes((ROWS, ROWS)) < TOK
    low_half = lanes((ROWS, 128)) < HEAD_DIM
    for pair in range(HEADS // 2):
        at = pair * 128
        q = qkv_ref[:, at : at + 128]
        k = qkv_ref[:, D + at : D + at + 128]
        v = qkv_ref[:, 2 * D + at : 2 * D + at + 128]
        mixed = []
        for side, mask in enumerate((first, second)):
            s = dot(q * mask, k, NT) * score_scale
            s = jnp.where(seen, s, -1e30)
            e = jnp.exp(s - jnp.max(s, axis=1, keepdims=True))
            p = (e / jnp.sum(e, axis=1, keepdims=True)).astype(low)
            p_ref[2 * pair + side] = p
            mixed.append(dot(p, v))
        o_ref[:, at : at + 128] = jnp.where(low_half, mixed[0], mixed[1]).astype(low)
    moves.start("p", p_ref, outs[4])
    moves.start("o", o_ref, outs[5])
    m = x + dot(o_ref[...], w_ref[:, 2304:3072])
    m_ref[...] = m
    moves.start("m", m_ref, outs[1])
    c = (unit_rows(m)[0] * norms[2:3] + norms[3:4]).astype(low)
    c_ref[...] = c
    moves.start("c", c_ref, outs[6])
    lane = lanes((ROWS, 128))
    logits = jnp.where(lane < EXPERTS, dot(c, w_ref[:, 3072:3200]), -1e30)
    e = jnp.exp(logits - jnp.max(logits, axis=1, keepdims=True))
    r = e / jnp.sum(e, axis=1, keepdims=True)
    r_ref[...] = r
    moves.start("r", r_ref, outs[7])
    slot = lax.broadcasted_iota(jnp.int32, (SLOTS, ROWS), 0)
    picks, grads = [], []
    for j in range(2):
        chosen = lane == ids_ref[:, j : j + 1]
        gate = jnp.sum(jnp.where(chosen, r, 0.0), axis=1, keepdims=True) * keep_ref[:, j : j + 1]
        picks.append((slot == trow_ref[j : j + 1, :]).astype(full).astype(low))
        grads.append((gate * g).astype(low))
    for part, value in enumerate(
        (dot(picks[0] + picks[1], c), dot(picks[0], grads[0]) + dot(picks[1], grads[1]))
    ):
        spare[...] = value
        for e in range(EXPERTS):
            send_ref[e, :, part * D : (part + 1) * D] = spare[slot_rows(e), :].astype(low)
    moves.wait("a", "qkv", "p", "o", "m", "c", "r")


def expert_kernel(
    got_ref, w_ref, back_ref, h_ref, du_ref, xt_ref, dzt_ref, z_sum, dx_sum, xs, dzs
):
    step = pl.program_id(0)

    @pl.when(step == 0)
    def _():
        for e in range(EXPERTS):
            rows = slice(e * CAP, (e + 1) * CAP)
            z_sum[rows, :] = got_ref[e, :, 0:D].astype(full)
            dx_sum[rows, :] = got_ref[e, :, D:].astype(full)
        xs[...] = z_sum[...].astype(low)
        dzs[...] = dx_sum[...].astype(low)
        xt_ref[...] = xs[...].T
        dzt_ref[...] = dzs[...].T
        z_sum[...] = jnp.zeros_like(z_sum)
        dx_sum[...] = jnp.zeros_like(dx_sum)

    wi = jnp.concatenate([w_ref[0:D, 0:HID], w_ref[D:, 0:HID]], axis=1)
    wot = jnp.concatenate([w_ref[0:D, HID:], w_ref[D:, HID:]], axis=1)
    u = dot(xs[...], wi)
    dh = dot(dzs[...], wot)
    square = u * u
    inner = u * (0.7978845608028654 + (0.7978845608028654 * 0.044715) * square)
    t = jnp.tanh(inner)
    half = 0.5 * t + 0.5
    h = (u * half).astype(low)
    slope = (0.5 * u) * (1.0 - t * t)
    slope = slope * (0.7978845608028654 + (3 * 0.7978845608028654 * 0.044715) * square) + half
    du = (slope * dh).astype(low)
    h_ref[...] = h
    du_ref[...] = du
    z_sum[...] += dot(h, wot, NT)
    dx_sum[...] += dot(du, wi, NT)

    @pl.when(step == pl.num_programs(0) - 1)
    def _():
        for e in range(EXPERTS):
            rows = slice(e * CAP, (e + 1) * CAP)
            back_ref[e, :, 0:D] = z_sum[rows, :].astype(low)
            back_ref[e, :, D:] = dx_sum[rows, :].astype(low)


def expert_grad_kernel(h_ref, du_ref, xt_ref, dzt_ref, out_ref):
    gi = dot(xt_ref[...], du_ref[...]).astype(low)
    go = dot(dzt_ref[...], h_ref[...]).astype(low)
    for i in range(2):
        cols = slice(i * HID, (i + 1) * HID)
        out_ref[i * D : (i + 1) * D, 0:HID] = gi[:, cols]
        out_ref[i * D : (i + 1) * D, HID:] = go[:, cols]


def owner_place(rows_ref, g):
    return (g % 2 + rows_ref[17]) % 2, (g // 2 + 4 - rows_ref[16]) % 4


def spread(rows_ref, grad, part, grads_ref):
    for g in range(GRP):
        side, step = owner_place(rows_ref, g)
        at = pl.multiple_of(step * PIECE, PIECE)
        for r in range(2):
            rows = slice(g * OWN + r * PIECE, g * OWN + (r + 1) * PIECE)
            for k in range(2):
                cols = slice(k * WIDE, (k + 1) * WIDE)
                grads_ref[side, r * 8 + part * 2 + k, pl.ds(at, PIECE), :] = grad[rows, cols]


def spread_extra(rows_ref, extra, rest_ref, grads_ref):
    empty = jnp.zeros((16, 128 - OWN), full)
    for g in range(GRP):
        side, step = owner_place(rows_ref, g)
        cols = slice(g * OWN, (g + 1) * OWN)
        parts = [extra[0:16, cols], empty, extra[16:32, cols], empty, jnp.zeros((16, 128), full)]
        rest_ref[side, step] = jnp.concatenate(parts, axis=1)
    unused = jnp.zeros((12, WIDE), full)
    for side in range(2):
        for e in range(16):
            rows = [rest_ref[side, step, e : e + 1, :] for step in range(4)]
            rows = jnp.concatenate(rows + [unused], axis=0)
            grads_ref[side, e, 4 * PIECE :, :] = rows.astype(low)


def backward_kernel(rows_ref, ids_ref, tcol_ref, keep_ref, back_ref, *refs):
    ins, pieces, refs = refs[:9], refs[9:25], refs[25:]
    outs, refs = refs[:4], refs[4:]
    m_ref, r_ref, g_ref, c_ref, o_ref, qkv_ref, p_ref, a_ref, x_ref = refs[:9]
    result_ref, image_ref = refs[9:11]
    x_pad, g_pad, spare, dqkv, w_ref, w_sem, sem, grads_ref, rest_ref = refs[11:]
    moves = Moves(sem)
    for name in range(1, 5):
        moves.start(name, ins[name - 1], refs[name - 1])
    copies = dense_copies(rows_ref, pieces, w_ref, w_sem)
    for name in range(5, 10):
        moves.start(name, ins[name - 1], refs[name - 1])

    def rows_of(part):
        for e in range(EXPERTS):
            spare[slot_rows(e), :] = back_ref[e, :, part * D : (part + 1) * D].astype(full)
        return spare[...].astype(low)

    def send_grads(part):
        rows = pl.ds(0, 4 * PIECE)
        for r in range(2):
            some = pl.ds(r * 8 + part * 2, 2)
            for side in (1, 0):
                moves.start(
                    (part, r, side),
                    grads_ref.at[side, some, rows],
                    outs[2 + side].at[some, rows],
                )

    moves.wait(1, 2, 3)
    g = padded(g_ref, g_pad)
    m = m_ref[...]
    r = r_ref[...]
    lane = lanes((ROWS, 128))
    slot = lanes((ROWS, SLOTS))
    z = rows_of(0)
    total = m
    dr = jnp.zeros((ROWS, 128), full)
    picks = []
    for j in range(2):
        pick = (slot == tcol_ref[:, j : j + 1]).astype(full).astype(low)
        picks.append(pick)
        keep = keep_ref[:, j : j + 1]
        chosen = lane == ids_ref[:, j : j + 1]
        gate = jnp.sum(jnp.where(chosen, r, 0.0), axis=1, keepdims=True) * keep
        zj = dot(pick, z)
        total = total + gate * zj
        dgate = jnp.sum(g * zj, axis=1, keepdims=True) * keep
        dr = dr + jnp.where(chosen, dgate, 0.0)
    result_ref[0] = total[0:TOK].astype(low)
    moves.start("result", result_ref, outs[0])
    for copy in copies:
        copy.wait()
    norms = norm_rows(w_ref)
    moves.wait(4)
    dl = (r * (dr - jnp.sum(dr * r, axis=1, keepdims=True))).astype(low)
    c = c_ref[...]
    gr = dot(dl, c, TN)[0:16]
    dc = dot(dl, w_ref[:, 3072:3200], NT) + dot(picks[0] + picks[1], rows_of(1))
    xh, scale = unit_rows(m)
    dn2 = jnp.sum(dc * xh, axis=0, keepdims=True)
    dn3 = jnp.sum(dc, axis=0, keepdims=True)
    dxh = dc * norms[2:3]
    dm = g + scale * (
        dxh
        - jnp.mean(dxh, axis=1, keepdims=True)
        - xh * jnp.mean(dxh * xh, axis=1, keepdims=True)
    )
    dmb = dm.astype(low)
    moves.wait(5)
    spread(rows_ref, dot(o_ref[...].T, dmb).astype(low), 3, grads_ref)
    send_grads(3)
    do = dot(dmb, w_ref[:, 2304:3072], NT).astype(low)
    first, second = half_masks()
    low_half = lane < HEAD_DIM
    moves.wait(6, 7)
    for pair in range(HEADS // 2):
        at = pair * 128
        q = qkv_ref[:, at : at + 128]
        k = qkv_ref[:, D + at : D + at + 128]
        v = qkv_ref[:, 2 * D + at : 2 * D + at + 128]
        dop = do[:, at : at + 128]
        parts = []
        for side, mask in enumerate((first, second)):
            p_low = p_ref[2 * pair + side]
            p = p_low.astype(full)
            dp = dot(dop * mask, v, NT)
            ds = (p * (dp - jnp.sum(dp * p, axis=1, keepdims=True))).astype(low)
            parts.append((dot(ds, k), dot(ds, q, TN), dot(p_low, dop, TN)))
        for which, factor in enumerate((score_scale, score_scale, 1.0)):
            both = jnp.where(low_half, parts[0][which], parts[1][which]) * factor
            dqkv[:, which * D + at : which * D + at + 128] = both.astype(low)
    moves.wait(8, 9)
    at_rows = a_ref[...].T
    da = jnp.zeros((ROWS, D), full)
    for part in range(3):
        cols = slice(part * D, part * D + D)
        spread(rows_ref, dot(at_rows, dqkv[:, cols]).astype(low), part, grads_ref)
        send_grads(part)
        da = da + dot(dqkv[:, cols], w_ref[:, cols], NT)
    xh, scale = unit_rows(padded(x_ref, x_pad))
    extra = [
        gr,
        jnp.sum(da * xh, axis=0, keepdims=True),
        jnp.sum(da, axis=0, keepdims=True),
        dn2,
        dn3,
        jnp.zeros((12, D), full),
    ]
    spread_extra(rows_ref, jnp.concatenate(extra, axis=0), rest_ref, grads_ref)
    for side in (1, 0):
        rows = pl.ds(4 * PIECE, 16)
        moves.start(("rest", side), grads_ref.at[side, :, rows], outs[2 + side].at[:, rows])
    dxh = da * norms[0:1]
    dx = dm + scale * (
        dxh
        - jnp.mean(dxh, axis=1, keepdims=True)
        - xh * jnp.mean(dxh * xh, axis=1, keepdims=True)
    )
    image_ref[0] = dx[0:TOK]
    moves.start("image", image_ref, outs[1])
    moves.wait(*[name for name in moves.open if name not in range(1, 10)])


def adamw(master, first, second, gradient, rate):
    first = beta_first * first + (1.0 - beta_first) * gradient
    second = beta_second * second + (1.0 - beta_second) * gradient * gradient
    corrected = first / (1.0 - beta_first**STEP)
    scaled = jnp.sqrt(second / (1.0 - beta_second**STEP)) + adam_epsilon
    return (first, second, master - rate * (corrected / scaled + weight_decay * master))


def owner_kernel(pieces_ref, rest_ref, *refs):
    inputs, outputs = refs[:12], refs[12:]

    def update(side, rate):
        for r in range(2):
            rows = slice(r * PIECE, (r + 1) * PIECE)
            for k in range(2):
                cols = slice(k * WIDE, (k + 1) * WIDE)
                grad = pieces_ref[r, k, 0:PIECE, :].astype(full)
                new = adamw(*[ref[rows, cols] for ref in inputs[side : side + 3]], grad, rate)
                for ref, value in zip(outputs[side : side + 3], new):
                    ref[rows, cols] = value

    last = pl.program_id(0) == 3
    pl.when(jnp.logical_not(last))(lambda: update(0, 0.04))
    pl.when(last)(lambda: update(3, 0.2))

    @pl.when(last)
    def _():
        rest = jnp.concatenate(
            [rest_ref[r, k, PIECE :, :] for r in range(2) for k in range(8)], axis=0
        ).astype(full)
        for side, grad, rate in (
            (6, rest[:, 0:OWN], 0.03),
            (9, rest[0:4, 128 : 128 + OWN], 0.3),
        ):
            new = adamw(*[ref[...] for ref in inputs[side : side + 3]], grad, rate)
            for ref, value in zip(outputs[side : side + 3], new):
                ref[...] = value


def expert_step_kernel(grad_ref, *refs):
    inputs, outputs = refs[:6], refs[-6:]
    grad = grad_ref[...].astype(full)
    new = adamw(*[ref[0] for ref in inputs[:3]], grad[:, 0:HID], 0.04)
    new = new + adamw(*[ref[0] for ref in inputs[3:]], grad[:, HID:].T, 0.15)
    for ref, value in zip(outputs, new):
        ref[0] = value


def expert_step(grad, arrays):
    inner = pl.BlockSpec((1, 128, HID), lambda i: (0, i, 0))
    outer = pl.BlockSpec((1, HID, 128), lambda i: (0, 0, i))
    return pl.pallas_call(
        expert_step_kernel,
        grid=(D // 128,),
        out_shape=tuple(hbm(*a.shape) for a in arrays),
        in_specs=[pl.BlockSpec((128, D), lambda i: (i, 0))]
        + [inner] * 3
        + [outer] * 3,
        out_specs=(inner,) * 3 + (outer,) * 3,
        compiler_params=params(16),
        cost_estimate=pl.CostEstimate(
            flops=10**7, bytes_accessed=8 * 10**6, transcendentals=10**6
        ),
        name="expert_step",
    )(*pinned([grad, *arrays]))


def shape(*dims, dtype=jnp.float32):
    return jax.ShapeDtypeStruct(dims, dtype)


def in_vmem(count):
    return [pl.BlockSpec(memory_space=pltpu.VMEM)] * count


def pinned(values):
    return [pltpu.with_memory_space_constraint(v, pltpu.HBM) for v in values]


def hbm(*dims, dtype=jnp.float32):
    return pltpu.HBM(dims, dtype)


def in_smem():
    return pl.BlockSpec(memory_space=pltpu.SMEM)


def in_place(count):
    return [pl.BlockSpec(memory_space=pl.ANY)] * count


def params(mib):
    return pltpu.CompilerParams(vmem_limit_bytes=mib * 2**20)


def pack(qkv, proj, router, norm):
    return pl.pallas_call(
        pack_kernel,
        out_shape=(shape(PIECE, DENSE, dtype=low),) * 2,
        in_specs=in_place(4),
        out_specs=tuple(in_vmem(2)),
        scratch_shapes=vmem_like((qkv, proj, router.T, norm.T)) + [pltpu.SemaphoreType.DMA((4,))],
        compiler_params=params(16),
        cost_estimate=pl.CostEstimate(flops=10**5, bytes_accessed=2 * 10**6, transcendentals=0),
        name="pack",
    )(*pinned((qkv, proj, router.T, norm.T)))


def flat_type(value):
    return value.inner_aval if hasattr(value, "inner_aval") else value


def vmem_like(shapes):
    return [pltpu.VMEM(s.shape, s.dtype) for s in map(flat_type, shapes)]


def token_forward(*args):
    outs = (
        pltpu.VMEM((EXPERTS, CAP, 2 * D), low),
        hbm(ROWS, D),
        hbm(ROWS, D, dtype=low),
        hbm(ROWS, 3 * D, dtype=low),
        hbm(HEADS, ROWS, ROWS, dtype=low),
        hbm(ROWS, D, dtype=low),
        hbm(ROWS, D, dtype=low),
        hbm(ROWS, 128),
    )
    return pl.pallas_call(
        forward_kernel,
        out_shape=outs,
        in_specs=[in_smem()] + in_vmem(3) + in_place(18),
        out_specs=tuple(in_vmem(1) + in_place(7)),
        scratch_shapes=vmem_like(outs[1:])
        + [pltpu.VMEM((1, TOK, D), low)] * 2
        + [pltpu.VMEM((ROWS, D), full)] * 2
        + [
            pltpu.VMEM((D, DENSE), low),
            pltpu.SemaphoreType.DMA((16,)),
            pltpu.SemaphoreType.DMA((10,)),
            pltpu.VMEM((SLOTS, D), full),
        ],
        compiler_params=params(40),
        cost_estimate=pl.CostEstimate(
            flops=4 * 10**9, bytes_accessed=12 * 10**6, transcendentals=10**6
        ),
        name="token_forward",
    )(*args[:4], *pinned(args[4:]))


PAIR = pl.BlockSpec((2 * D, D), lambda i: (i, 0))
HIDDEN = pl.BlockSpec((SLOTS, 2 * HID), lambda i: (0, i))
TURNED = pl.BlockSpec((D, SLOTS), lambda i: (0, 0))


def experts_both_ways(got, weights):
    hidden, turned = hbm(SLOTS, GRP * HID, dtype=low), hbm(D, SLOTS, dtype=low)
    return pl.pallas_call(
        expert_kernel,
        grid=(GRP // 2,),
        out_shape=(
            pltpu.VMEM((EXPERTS, CAP, 2 * D), low),
            hidden,
            hidden,
            turned,
            turned,
        ),
        in_specs=in_vmem(1) + [PAIR],
        out_specs=(*in_vmem(1), HIDDEN, HIDDEN, TURNED, TURNED),
        scratch_shapes=[pltpu.VMEM((SLOTS, D), full)] * 2 + [pltpu.VMEM((SLOTS, D), low)] * 2,
        compiler_params=params(44),
        cost_estimate=pl.CostEstimate(
            flops=10 * 10**9, bytes_accessed=23 * 10**6, transcendentals=2 * 10**6
        ),
        name="experts",
    )(got, *pinned([weights]))


def expert_grads(*args):
    return pl.pallas_call(
        expert_grad_kernel,
        grid=(GRP // 2,),
        out_shape=hbm(GRP * D, D, dtype=low),
        in_specs=[HIDDEN, HIDDEN, TURNED, TURNED],
        out_specs=PAIR,
        compiler_params=params(28),
        cost_estimate=pl.CostEstimate(
            flops=6 * 10**9, bytes_accessed=18 * 10**6, transcendentals=0
        ),
        name="expert_grads",
    )(*pinned(args))


def token_backward(*args):
    outs = (
        hbm(1, TOK, D, dtype=low),
        hbm(1, TOK, D),
        hbm(16, BLOCK, WIDE, dtype=low),
        hbm(16, BLOCK, WIDE, dtype=low),
    )
    return pl.pallas_call(
        backward_kernel,
        out_shape=outs,
        in_specs=[in_smem()] + in_vmem(4) + in_place(25),
        out_specs=tuple(in_place(4)),
        scratch_shapes=vmem_like(args[5:14])
        + vmem_like(outs[:2])
        + [
            pltpu.VMEM((ROWS, D), full),
            pltpu.VMEM((ROWS, D), full),
            pltpu.VMEM((SLOTS, D), full),
            pltpu.VMEM((ROWS, 3 * D), low),
            pltpu.VMEM((D, DENSE), low),
            pltpu.SemaphoreType.DMA((16,)),
            pltpu.SemaphoreType.DMA((29,)),
            pltpu.VMEM((2, 16, BLOCK, WIDE), low),
            pltpu.VMEM((2, 4, 16, WIDE), full),
        ],
        compiler_params=params(48),
        cost_estimate=pl.CostEstimate(
            flops=400 * 10**9, bytes_accessed=18 * 10**6, transcendentals=10**4
        ),
        name="token_backward",
    )(*args[:5], *pinned(args[5:]))


def owner_step(pieces, arrays, small):
    qkv = pl.BlockSpec((OWN, D), lambda i: (0, jnp.minimum(i, 2)))
    proj = pl.BlockSpec((OWN, D), lambda i: (0, 0))
    whole = [pl.BlockSpec(a.shape, lambda i: (0, 0)) for a in small]
    return pl.pallas_call(
        owner_kernel,
        grid=(4,),
        out_shape=tuple([hbm(*a.shape) for a in arrays] + [shape(*a.shape) for a in small]),
        in_specs=[
            pl.BlockSpec((2, 2, PIECE + 1, WIDE), lambda i: (0, i, 0, 0)),
            pl.BlockSpec((2, 8, PIECE + 1, WIDE), lambda i: (0, 0, 0, 0)),
        ]
        + [qkv] * 3
        + [proj] * 3
        + whole,
        out_specs=tuple([qkv] * 3 + [proj] * 3 + whole),
        compiler_params=params(24),
        cost_estimate=pl.CostEstimate(
            flops=10**7, bytes_accessed=8 * 10**6, transcendentals=10**6
        ),
        name="owner_step",
    )(pieces, pieces, *pinned(arrays), *small)


def exchange(value):
    return lax.all_to_all(value, "exp", split_axis=0, concat_axis=0, tiled=True)


def dense_sum(keep, give):
    def along(step, value):
        hops = [(2 * x + c, 2 * ((x + step) % 4) + c) for x in range(4) for c in range(2)]
        return lax.ppermute(value, "grp", hops)

    got = lax.ppermute(give, "grp", [(i, i ^ 1) for i in range(GRP)])
    pieces = exchange((keep.astype(full) + got.astype(full)).astype(low))
    total = jnp.sum(pieces.astype(full), axis=0)
    main, rest = total[: 4 * PIECE].reshape(4, PIECE, WIDE), total[4 * PIECE :][:4, None]
    total = jnp.concatenate([main, rest], axis=1)
    sent = [along(step, total[step].astype(low)).astype(full) for step in (1, 2, 3)]
    return total[0] + sent[0] + sent[1] + sent[2]


def on_device(
    images,
    cotangent,
    expert_ids,
    kept_routes,
    qkv_master,
    qkv_first,
    qkv_second,
    proj_master,
    proj_first,
    proj_second,
    router_master,
    router_first,
    router_second,
    norm_master,
    norm_first,
    norm_second,
    inner_master,
    inner_first,
    inner_second,
    outer_master,
    outer_first,
    outer_second,
):
    pieces = dense_pieces(*pack(qkv_master, proj_master, router_master, norm_master))
    rows = piece_rows(lax.axis_index("grp"))
    mine = jnp.concatenate([inner_master[0].astype(low), outer_master[0].astype(low).T], axis=1)
    mine, *_ = lax.optimization_barrier((mine, pieces[3], pieces[4]))
    weights = lax.all_gather(mine, "grp", axis=0, tiled=True)

    ids = expert_ids.reshape(TOK, 2)
    kept = kept_routes.reshape(TOK, 2)
    flat = ids.reshape(-1)
    marks = (flat[:, None] == jnp.arange(EXPERTS, dtype=jnp.int32)[None, :]).astype(jnp.int32)
    slots = jnp.sum((jnp.cumsum(marks, axis=0) - marks) * marks, axis=1).reshape(TOK, 2)
    target = jnp.where(kept > 0, ids * CAP + slots, -1)
    padding = ((0, ROWS - TOK), (0, 0))
    target = jnp.pad(target, padding, constant_values=-1)
    ids = jnp.pad(ids, padding, constant_values=-1)
    keep = jnp.pad(kept.astype(full), padding)

    send, m, a, qkv, p, o, c, r = token_forward(
        rows, ids, keep, target.T, images, cotangent, *pieces
    )
    back, *hidden = experts_both_ways(exchange(send), weights)
    back = exchange(back)
    grad = lax.psum_scatter(expert_grads(*hidden), "grp", scatter_dimension=0, tiled=True)
    result, image_grad, keep_grads, give_grads = token_backward(
        rows, ids, target, keep, back, m, r, cotangent, c, o, qkv, p, a, images, *pieces
    )
    (
        inner_moment,
        inner_square,
        inner_weight,
        outer_moment,
        outer_square,
        outer_weight,
    ) = expert_step(
        grad,
        (inner_master, inner_first, inner_second, outer_master, outer_first, outer_second),
    )
    block = dense_sum(keep_grads, give_grads).astype(low)
    block = exchange(jnp.broadcast_to(block[None], (16, PIECE + 1, WIDE)))
    block, inner_weight = lax.optimization_barrier((block, inner_weight))
    small = (router_master, router_first, router_second, norm_master, norm_first, norm_second)
    new = owner_step(
        block.reshape(2, 8, PIECE + 1, WIDE),
        (qkv_master, qkv_first, qkv_second, proj_master, proj_first, proj_second),
        [value.T for value in small],
    )
    qkv_moment, qkv_square, qkv_weight, proj_moment, proj_square, proj_weight = new[:6]
    router_moment, router_square, router_weight = [value.T for value in new[6:9]]
    norm_moment, norm_square, norm_weight = [value.T for value in new[9:]]
    return (
        result,
        image_grad,
        qkv_moment,
        qkv_square,
        qkv_weight,
        proj_moment,
        proj_square,
        proj_weight,
        router_moment,
        router_square,
        router_weight,
        norm_moment,
        norm_square,
        norm_weight,
        inner_moment,
        inner_square,
        inner_weight,
        outer_moment,
        outer_square,
        outer_weight,
    )


def solution(mesh):
    in_specs = (
        P(("grp", "exp"), None, None),
        P(("grp", "exp"), None, None),
        P(("grp", "exp"), None, None),
        P(("grp", "exp"), None, None),
        P("grp", None),
        P("grp", None),
        P("grp", None),
        P("grp", None),
        P("grp", None),
        P("grp", None),
        P("grp", None),
        P("grp", None),
        P("grp", None),
        P("grp", None),
        P("grp", None),
        P("grp", None),
        P("exp", None, "grp"),
        P("exp", None, "grp"),
        P("exp", None, "grp"),
        P("exp", "grp", None),
        P("exp", "grp", None),
        P("exp", "grp", None),
    )
    out_specs = (
        P(("grp", "exp"), None, None),
        P(("grp", "exp"), None, None),
        P("grp", None),
        P("grp", None),
        P("grp", None),
        P("grp", None),
        P("grp", None),
        P("grp", None),
        P("grp", None),
        P("grp", None),
        P("grp", None),
        P("grp", None),
        P("grp", None),
        P("grp", None),
        P("exp", None, "grp"),
        P("exp", None, "grp"),
        P("exp", None, "grp"),
        P("exp", "grp", None),
        P("exp", "grp", None),
        P("exp", "grp", None),
    )
    return jax.shard_map(
        on_device, mesh=mesh, in_specs=in_specs, out_specs=out_specs, check_vma=False
    )
```

```python
import jax
import jax.numpy as jnp
from jax import lax
from jax.experimental import pallas as pl
from jax.experimental.pallas import tpu as pltpu
from jax.sharding import PartitionSpec as P

HEADS = 12
HEAD_DIM = 64
STEP = 10
D = 768
TOK = 197
ROWS = 208
EXPERTS = 16
CAP = 33
SLOTS = EXPERTS * CAP
DENSE = 3200
GRP = 8
OWN = D // GRP
PIECE = 48
WIDE = 384
HID = 384
LAST = EXPERTS * 32
BLOCK = 4 * PIECE + 16

norm_epsilon = 1e-06
beta_first = 0.9
beta_second = 0.999
adam_epsilon = 1e-08
weight_decay = 0.1
score_scale = HEAD_DIM ** (-0.5)
low = jnp.bfloat16
full = jnp.float32


def dot(a, b, dims=((1,), (0,))):
    return lax.dot_general(a, b, (dims, ((), ())), preferred_element_type=jnp.float32)


NT = ((1,), (1,))
TN = ((0,), (0,))


def unit_rows(values):
    centered = values - jnp.mean(values, axis=-1, keepdims=True)
    variance = jnp.mean(centered * centered, axis=-1, keepdims=True)
    scale = lax.rsqrt(variance + norm_epsilon)
    return centered * scale, scale


def norm_rows(w_ref):
    return w_ref[:, 3072:3200].astype(full).T[16:24]


def pack_kernel(qkv_ref, proj_ref, router_ref, norm_ref, *refs):
    first_out, second_out, qkv_in, proj_in, router_in, norm_in, sem = refs
    sources = (qkv_ref, proj_ref, router_ref, norm_ref)
    loads = [
        pltpu.make_async_copy(source, target, sem.at[i])
        for i, (source, target) in enumerate(zip(sources, refs[2:6]))
    ]
    for load in loads:
        load.start()
    for load in loads[2:]:
        load.wait()
    rest = [router_in[...], norm_in[...], jnp.zeros((DENSE - 3092, OWN), full)]
    rest = jnp.concatenate(rest, axis=0).T.astype(low)
    for load in loads[:2]:
        load.wait()
    for i, out_ref in enumerate((first_out, second_out)):
        rows = slice(i * PIECE, (i + 1) * PIECE)
        out_ref[:, 0:2304] = qkv_in[rows, :].astype(low)
        out_ref[:, 2304:3072] = proj_in[rows, :].astype(low)
        out_ref[:, 3072:3200] = rest[rows, :]


def dense_pieces(first, second):
    def along(step, value):
        hops = [(2 * x + c, 2 * ((x + step) % 4) + c) for x in range(4) for c in range(2)]
        return lax.ppermute(value, "grp", hops)

    def across(value):
        return lax.ppermute(value, "grp", [(i, i ^ 1) for i in range(GRP)])

    up_first, down_second = along(1, first), along(3, second)
    up_first, down_second, again, other = lax.optimization_barrier(
        (up_first, down_second, second, first)
    )
    up_second, down_first = along(1, again), along(3, other)
    far_first, far_second = along(1, up_first), along(3, down_second)
    here = [first, second, up_first, up_second, down_first, down_second, far_first, far_second]
    return here + [across(piece) for piece in here]


def piece_rows(place):
    x, c = place // 2, place % 2
    rows = []
    for core in (c, 1 - c):
        for step in (0, 3, 1, 2):
            near = OWN * (2 * ((x + step) % 4) + core)
            rows += [near, near + PIECE]
    return jnp.stack(rows + [x, c]).astype(jnp.int32)


def dense_copies(rows_ref, pieces, w_ref, sem):
    copies = []
    for i, piece in enumerate(pieces):
        at = pl.multiple_of(rows_ref[i], PIECE)
        copies.append(pltpu.make_async_copy(piece, w_ref.at[pl.ds(at, PIECE), :], sem.at[i]))
        copies[-1].start()
    return copies


class Moves:
    def __init__(self, sem):
        self.sem, self.open = sem, {}

    def start(self, name, source, target):
        self.open[name] = pltpu.make_async_copy(source, target, self.sem.at[len(self.open)])
        self.open[name].start()

    def wait(self, *names):
        for name in names:
            self.open[name].wait()


def pack_slots(totals, out_ref):
    unused = jnp.zeros((4, 128), full)
    for e in range(EXPERTS):
        last = []
        for part, total in enumerate(totals):
            for j in range(6):
                cols, at = slice(j * 128, (j + 1) * 128), (part * 6 + j) * 32
                out_ref[e, at : at + 32, :] = total[e * 32 : (e + 1) * 32, cols].astype(low)
                last.append(total[LAST + e : LAST + e + 1, cols])
        out_ref[e, 384:400, :] = jnp.concatenate(last + [unused], axis=0).astype(low)


def unpack_slots(got_ref, part, rows_ref):
    last = []
    for e in range(EXPERTS):
        for j in range(6):
            cols, at = slice(j * 128, (j + 1) * 128), (part * 6 + j) * 32
            rows_ref[e * 32 : (e + 1) * 32, cols] = got_ref[e, at : at + 32, :]
        block = got_ref[e, 384:400, :].astype(full)
        rows = [block[part * 6 + j : part * 6 + j + 1] for j in range(6)]
        last.append(jnp.concatenate(rows, axis=1))
    rows_ref[LAST:SLOTS, :] = jnp.concatenate(last, axis=0).astype(low)


def padded(ref, pad_ref):
    pad_ref[192:ROWS, :] = jnp.zeros((ROWS - 192, D), full)
    pad_ref[0:TOK, :] = ref[0].astype(full)
    return pad_ref[...]


def lanes(shape):
    return lax.broadcasted_iota(jnp.int32, shape, 1)


def half_masks():
    lane = lanes((1, 128))
    first = (lane < HEAD_DIM).astype(full)
    return first.astype(low), (1.0 - first).astype(low)


def forward_kernel(rows_ref, ids_ref, keep_ref, trow_ref, x_hbm, g_hbm, *refs):
    pieces, refs = refs[:16], refs[16:]
    outs, refs = refs[:8], refs[8:]
    send_ref = outs[0]
    m_ref, a_ref, qkv_ref, p_ref, o_ref, c_ref, r_ref = refs[:7]
    x_ref, g_ref, x_pad, g_pad, w_ref, w_sem, sem, spare, spare2 = refs[7:]
    moves = Moves(sem)
    moves.start("x", x_hbm, x_ref)
    copies = dense_copies(rows_ref, pieces, w_ref, w_sem)
    moves.start("g", g_hbm, g_ref)
    moves.wait("x")
    x = padded(x_ref, x_pad)
    unit = unit_rows(x)[0]
    moves.wait("g")
    g = padded(g_ref, g_pad)
    for copy in copies:
        copy.wait()
    norms = norm_rows(w_ref)
    a = (unit * norms[0:1] + norms[1:2]).astype(low)
    a_ref[...] = a
    moves.start("a", a_ref, outs[2])
    for part in range(3):
        cols = slice(part * D, part * D + D)
        qkv_ref[:, cols] = dot(a, w_ref[:, cols]).astype(low)
    moves.start("qkv", qkv_ref, outs[3])
    first, second = half_masks()
    seen = lanes((ROWS, ROWS)) < TOK
    low_half = lanes((ROWS, 128)) < HEAD_DIM
    for pair in range(HEADS // 2):
        at = pair * 128
        q = qkv_ref[:, at : at + 128]
        k = qkv_ref[:, D + at : D + at + 128]
        v = qkv_ref[:, 2 * D + at : 2 * D + at + 128]
        mixed = []
        for side, mask in enumerate((first, second)):
            s = dot(q * mask, k, NT) * score_scale
            s = jnp.where(seen, s, -1e30)
            e = jnp.exp(s - jnp.max(s, axis=1, keepdims=True))
            p = (e / jnp.sum(e, axis=1, keepdims=True)).astype(low)
            p_ref[2 * pair + side] = p
            mixed.append(dot(p, v))
        o_ref[:, at : at + 128] = jnp.where(low_half, mixed[0], mixed[1]).astype(low)
    moves.start("p", p_ref, outs[4])
    moves.start("o", o_ref, outs[5])
    m = x + dot(o_ref[...], w_ref[:, 2304:3072])
    m_ref[...] = m
    moves.start("m", m_ref, outs[1])
    c = (unit_rows(m)[0] * norms[2:3] + norms[3:4]).astype(low)
    c_ref[...] = c
    moves.start("c", c_ref, outs[6])
    lane = lanes((ROWS, 128))
    logits = jnp.where(lane < EXPERTS, dot(c, w_ref[:, 3072:3200]), -1e30)
    e = jnp.exp(logits - jnp.max(logits, axis=1, keepdims=True))
    r = e / jnp.sum(e, axis=1, keepdims=True)
    r_ref[...] = r
    moves.start("r", r_ref, outs[7])
    slot = lax.broadcasted_iota(jnp.int32, (SLOTS, ROWS), 0)
    picks, grads = [], []
    for j in range(2):
        chosen = lane == ids_ref[:, j : j + 1]
        gate = jnp.sum(jnp.where(chosen, r, 0.0), axis=1, keepdims=True) * keep_ref[:, j : j + 1]
        picks.append((slot == trow_ref[j : j + 1, :]).astype(full).astype(low))
        grads.append((gate * g).astype(low))
    spare[...] = dot(picks[0] + picks[1], c)
    spare2[...] = dot(picks[0], grads[0]) + dot(picks[1], grads[1])
    pack_slots((spare, spare2), send_ref)
    moves.wait("a", "qkv", "p", "o", "m", "c", "r")


def expert_kernel(
    got_ref, w_ref, back_ref, h_ref, du_ref, xt_ref, dzt_ref, z_sum, dx_sum, xs, dzs
):
    step = pl.program_id(0)

    @pl.when(step == 0)
    def _():
        unpack_slots(got_ref, 0, xs)
        unpack_slots(got_ref, 1, dzs)
        xt_ref[...] = xs[...].T
        dzt_ref[...] = dzs[...].T
        z_sum[...] = jnp.zeros_like(z_sum)
        dx_sum[...] = jnp.zeros_like(dx_sum)

    wi = jnp.concatenate([w_ref[0:D, 0:HID], w_ref[D:, 0:HID]], axis=1)
    wot = jnp.concatenate([w_ref[0:D, HID:], w_ref[D:, HID:]], axis=1)
    u = dot(xs[...], wi)
    dh = dot(dzs[...], wot)
    square = u * u
    inner = u * (0.7978845608028654 + (0.7978845608028654 * 0.044715) * square)
    t = jnp.tanh(inner)
    half = 0.5 * t + 0.5
    h = (u * half).astype(low)
    slope = (0.5 * u) * (1.0 - t * t)
    slope = slope * (0.7978845608028654 + (3 * 0.7978845608028654 * 0.044715) * square) + half
    du = (slope * dh).astype(low)
    h_ref[...] = h
    du_ref[...] = du
    z_sum[...] += dot(h, wot, NT)
    dx_sum[...] += dot(du, wi, NT)

    @pl.when(step == pl.num_programs(0) - 1)
    def _():
        pack_slots((z_sum, dx_sum), back_ref)


def expert_grad_kernel(h_ref, du_ref, xt_ref, dzt_ref, out_ref):
    gi = dot(xt_ref[...], du_ref[...]).astype(low)
    go = dot(dzt_ref[...], h_ref[...]).astype(low)
    for i in range(2):
        cols = slice(i * HID, (i + 1) * HID)
        out_ref[i * D : (i + 1) * D, 0:HID] = gi[:, cols]
        out_ref[i * D : (i + 1) * D, HID:] = go[:, cols]


def owner_place(rows_ref, g):
    return (g % 2 + rows_ref[17]) % 2, (g // 2 + 4 - rows_ref[16]) % 4


def spread(rows_ref, grad, part, grads_ref):
    for g in range(GRP):
        side, step = owner_place(rows_ref, g)
        at = pl.multiple_of(step * PIECE, PIECE)
        for r in range(2):
            rows = slice(g * OWN + r * PIECE, g * OWN + (r + 1) * PIECE)
            for k in range(2):
                cols = slice(k * WIDE, (k + 1) * WIDE)
                grads_ref[side, r * 8 + part * 2 + k, pl.ds(at, PIECE), :] = grad[rows, cols]


def spread_extra(rows_ref, extra, rest_ref, grads_ref):
    empty = jnp.zeros((16, 128 - OWN), full)
    for g in range(GRP):
        side, step = owner_place(rows_ref, g)
        cols = slice(g * OWN, (g + 1) * OWN)
        parts = [extra[0:16, cols], empty, extra[16:32, cols], empty, jnp.zeros((16, 128), full)]
        rest_ref[side, step] = jnp.concatenate(parts, axis=1)
    unused = jnp.zeros((12, WIDE), full)
    for side in range(2):
        for e in range(16):
            rows = [rest_ref[side, step, e : e + 1, :] for step in range(4)]
            rows = jnp.concatenate(rows + [unused], axis=0)
            grads_ref[side, e, 4 * PIECE :, :] = rows.astype(low)


def backward_kernel(rows_ref, ids_ref, tcol_ref, keep_ref, back_ref, *refs):
    ins, pieces, refs = refs[:9], refs[9:25], refs[25:]
    outs, refs = refs[:4], refs[4:]
    m_ref, r_ref, g_ref, c_ref, o_ref, qkv_ref, p_ref, a_ref, x_ref = refs[:9]
    result_ref, image_ref = refs[9:11]
    x_pad, g_pad, spare, dqkv, w_ref, w_sem, sem, grads_ref, rest_ref = refs[11:]
    moves = Moves(sem)
    for name in range(1, 5):
        moves.start(name, ins[name - 1], refs[name - 1])
    copies = dense_copies(rows_ref, pieces, w_ref, w_sem)
    for name in range(5, 10):
        moves.start(name, ins[name - 1], refs[name - 1])

    def rows_of(part):
        unpack_slots(back_ref, part, spare)
        return spare[...]

    def send_grads(part):
        rows = pl.ds(0, 4 * PIECE)
        for r in range(2):
            some = pl.ds(r * 8 + part * 2, 2)
            for side in (1, 0):
                moves.start(
                    (part, r, side),
                    grads_ref.at[side, some, rows],
                    outs[2 + side].at[some, rows],
                )

    moves.wait(1, 2, 3)
    g = padded(g_ref, g_pad)
    m = m_ref[...]
    r = r_ref[...]
    lane = lanes((ROWS, 128))
    slot = lanes((ROWS, SLOTS))
    z = rows_of(0)
    total = m
    dr = jnp.zeros((ROWS, 128), full)
    picks = []
    for j in range(2):
        pick = (slot == tcol_ref[:, j : j + 1]).astype(full).astype(low)
        picks.append(pick)
        keep = keep_ref[:, j : j + 1]
        chosen = lane == ids_ref[:, j : j + 1]
        gate = jnp.sum(jnp.where(chosen, r, 0.0), axis=1, keepdims=True) * keep
        zj = dot(pick, z)
        total = total + gate * zj
        dgate = jnp.sum(g * zj, axis=1, keepdims=True) * keep
        dr = dr + jnp.where(chosen, dgate, 0.0)
    result_ref[0] = total[0:TOK].astype(low)
    moves.start("result", result_ref, outs[0])
    for copy in copies:
        copy.wait()
    norms = norm_rows(w_ref)
    moves.wait(4)
    dl = (r * (dr - jnp.sum(dr * r, axis=1, keepdims=True))).astype(low)
    c = c_ref[...]
    gr = dot(dl, c, TN)[0:16]
    dc = dot(dl, w_ref[:, 3072:3200], NT) + dot(picks[0] + picks[1], rows_of(1))
    xh, scale = unit_rows(m)
    dn2 = jnp.sum(dc * xh, axis=0, keepdims=True)
    dn3 = jnp.sum(dc, axis=0, keepdims=True)
    dxh = dc * norms[2:3]
    dm = g + scale * (
        dxh
        - jnp.mean(dxh, axis=1, keepdims=True)
        - xh * jnp.mean(dxh * xh, axis=1, keepdims=True)
    )
    dmb = dm.astype(low)
    moves.wait(5)
    spread(rows_ref, dot(o_ref[...].T, dmb).astype(low), 3, grads_ref)
    send_grads(3)
    do = dot(dmb, w_ref[:, 2304:3072], NT).astype(low)
    first, second = half_masks()
    low_half = lane < HEAD_DIM
    moves.wait(6, 7)
    for pair in range(HEADS // 2):
        at = pair * 128
        q = qkv_ref[:, at : at + 128]
        k = qkv_ref[:, D + at : D + at + 128]
        v = qkv_ref[:, 2 * D + at : 2 * D + at + 128]
        dop = do[:, at : at + 128]
        parts = []
        for side, mask in enumerate((first, second)):
            p_low = p_ref[2 * pair + side]
            p = p_low.astype(full)
            dp = dot(dop * mask, v, NT)
            ds = (p * (dp - jnp.sum(dp * p, axis=1, keepdims=True))).astype(low)
            parts.append((dot(ds, k), dot(ds, q, TN), dot(p_low, dop, TN)))
        for which, factor in enumerate((score_scale, score_scale, 1.0)):
            both = jnp.where(low_half, parts[0][which], parts[1][which]) * factor
            dqkv[:, which * D + at : which * D + at + 128] = both.astype(low)
    moves.wait(8, 9)
    at_rows = a_ref[...].T
    da = jnp.zeros((ROWS, D), full)
    for part in range(3):
        cols = slice(part * D, part * D + D)
        spread(rows_ref, dot(at_rows, dqkv[:, cols]).astype(low), part, grads_ref)
        send_grads(part)
        da = da + dot(dqkv[:, cols], w_ref[:, cols], NT)
    xh, scale = unit_rows(padded(x_ref, x_pad))
    extra = [
        gr,
        jnp.sum(da * xh, axis=0, keepdims=True),
        jnp.sum(da, axis=0, keepdims=True),
        dn2,
        dn3,
        jnp.zeros((12, D), full),
    ]
    spread_extra(rows_ref, jnp.concatenate(extra, axis=0), rest_ref, grads_ref)
    for side in (1, 0):
        rows = pl.ds(4 * PIECE, 16)
        moves.start(("rest", side), grads_ref.at[side, :, rows], outs[2 + side].at[:, rows])
    dxh = da * norms[0:1]
    dx = dm + scale * (
        dxh
        - jnp.mean(dxh, axis=1, keepdims=True)
        - xh * jnp.mean(dxh * xh, axis=1, keepdims=True)
    )
    image_ref[0] = dx[0:TOK]
    moves.start("image", image_ref, outs[1])
    moves.wait(*[name for name in moves.open if name not in range(1, 10)])


def adamw(master, first, second, gradient, rate):
    first = beta_first * first + (1.0 - beta_first) * gradient
    second = beta_second * second + (1.0 - beta_second) * gradient * gradient
    corrected = first / (1.0 - beta_first**STEP)
    scaled = jnp.sqrt(second / (1.0 - beta_second**STEP)) + adam_epsilon
    return (first, second, master - rate * (corrected / scaled + weight_decay * master))


def owner_kernel(pieces_ref, rest_ref, *refs):
    inputs, outputs = refs[:12], refs[12:]

    def update(side, rate):
        for r in range(2):
            rows = slice(r * PIECE, (r + 1) * PIECE)
            for k in range(2):
                cols = slice(k * WIDE, (k + 1) * WIDE)
                grad = pieces_ref[r, k, 0:PIECE, :].astype(full)
                new = adamw(*[ref[rows, cols] for ref in inputs[side : side + 3]], grad, rate)
                for ref, value in zip(outputs[side : side + 3], new):
                    ref[rows, cols] = value

    last = pl.program_id(0) == 3
    pl.when(jnp.logical_not(last))(lambda: update(0, 0.04))
    pl.when(last)(lambda: update(3, 0.2))

    @pl.when(last)
    def _():
        rest = jnp.concatenate(
            [rest_ref[r, k, PIECE :, :] for r in range(2) for k in range(8)], axis=0
        ).astype(full)
        for side, grad, rate in (
            (6, rest[:, 0:OWN], 0.03),
            (9, rest[0:4, 128 : 128 + OWN], 0.3),
        ):
            new = adamw(*[ref[...] for ref in inputs[side : side + 3]], grad, rate)
            for ref, value in zip(outputs[side : side + 3], new):
                ref[...] = value


def expert_step_kernel(grad_ref, *refs):
    inputs, outputs = refs[:6], refs[-6:]
    grad = grad_ref[...].astype(full)
    new = adamw(*[ref[0] for ref in inputs[:3]], grad[:, 0:HID], 0.04)
    new = new + adamw(*[ref[0] for ref in inputs[3:]], grad[:, HID:].T, 0.15)
    for ref, value in zip(outputs, new):
        ref[0] = value


def expert_step(grad, arrays):
    inner = pl.BlockSpec((1, 128, HID), lambda i: (0, i, 0))
    outer = pl.BlockSpec((1, HID, 128), lambda i: (0, 0, i))
    return pl.pallas_call(
        expert_step_kernel,
        grid=(D // 128,),
        out_shape=tuple(hbm(*a.shape) for a in arrays),
        in_specs=[pl.BlockSpec((128, D), lambda i: (i, 0))]
        + [inner] * 3
        + [outer] * 3,
        out_specs=(inner,) * 3 + (outer,) * 3,
        compiler_params=params(16),
        cost_estimate=pl.CostEstimate(
            flops=10**7, bytes_accessed=8 * 10**6, transcendentals=10**6
        ),
        name="expert_step",
    )(*pinned([grad, *arrays]))


def shape(*dims, dtype=jnp.float32):
    return jax.ShapeDtypeStruct(dims, dtype)


def in_vmem(count):
    return [pl.BlockSpec(memory_space=pltpu.VMEM)] * count


def pinned(values):
    return [pltpu.with_memory_space_constraint(v, pltpu.HBM) for v in values]


def hbm(*dims, dtype=jnp.float32):
    return pltpu.HBM(dims, dtype)


def in_smem():
    return pl.BlockSpec(memory_space=pltpu.SMEM)


def in_place(count):
    return [pl.BlockSpec(memory_space=pl.ANY)] * count


def params(mib):
    return pltpu.CompilerParams(vmem_limit_bytes=mib * 2**20)


def pack(qkv, proj, router, norm):
    return pl.pallas_call(
        pack_kernel,
        out_shape=(shape(PIECE, DENSE, dtype=low),) * 2,
        in_specs=in_place(4),
        out_specs=tuple(in_vmem(2)),
        scratch_shapes=vmem_like((qkv, proj, router.T, norm.T)) + [pltpu.SemaphoreType.DMA((4,))],
        compiler_params=params(16),
        cost_estimate=pl.CostEstimate(flops=10**5, bytes_accessed=2 * 10**6, transcendentals=0),
        name="pack",
    )(*pinned((qkv, proj, router.T, norm.T)))


def flat_type(value):
    return value.inner_aval if hasattr(value, "inner_aval") else value


def vmem_like(shapes):
    return [pltpu.VMEM(s.shape, s.dtype) for s in map(flat_type, shapes)]


def token_forward(*args):
    outs = (
        pltpu.VMEM((EXPERTS, 400, 128), low),
        hbm(ROWS, D),
        hbm(ROWS, D, dtype=low),
        hbm(ROWS, 3 * D, dtype=low),
        hbm(HEADS, ROWS, ROWS, dtype=low),
        hbm(ROWS, D, dtype=low),
        hbm(ROWS, D, dtype=low),
        hbm(ROWS, 128),
    )
    return pl.pallas_call(
        forward_kernel,
        out_shape=outs,
        in_specs=[in_smem()] + in_vmem(3) + in_place(18),
        out_specs=tuple(in_vmem(1) + in_place(7)),
        scratch_shapes=vmem_like(outs[1:])
        + [pltpu.VMEM((1, TOK, D), low)] * 2
        + [pltpu.VMEM((ROWS, D), full)] * 2
        + [
            pltpu.VMEM((D, DENSE), low),
            pltpu.SemaphoreType.DMA((16,)),
            pltpu.SemaphoreType.DMA((10,)),
            pltpu.VMEM((SLOTS, D), full),
            pltpu.VMEM((SLOTS, D), full),
        ],
        compiler_params=params(40),
        cost_estimate=pl.CostEstimate(
            flops=4 * 10**9, bytes_accessed=12 * 10**6, transcendentals=10**6
        ),
        name="token_forward",
    )(*args[:4], *pinned(args[4:]))


PAIR = pl.BlockSpec((2 * D, D), lambda i: (i, 0))
HIDDEN = pl.BlockSpec((SLOTS, 2 * HID), lambda i: (0, i))
TURNED = pl.BlockSpec((D, SLOTS), lambda i: (0, 0))


def experts_both_ways(got, weights):
    hidden, turned = hbm(SLOTS, GRP * HID, dtype=low), hbm(D, SLOTS, dtype=low)
    return pl.pallas_call(
        expert_kernel,
        grid=(GRP // 2,),
        out_shape=(
            pltpu.VMEM((EXPERTS, 400, 128), low),
            hidden,
            hidden,
            turned,
            turned,
        ),
        in_specs=in_vmem(1) + [PAIR],
        out_specs=(*in_vmem(1), HIDDEN, HIDDEN, TURNED, TURNED),
        scratch_shapes=[pltpu.VMEM((SLOTS, D), full)] * 2 + [pltpu.VMEM((SLOTS, D), low)] * 2,
        compiler_params=params(44),
        cost_estimate=pl.CostEstimate(
            flops=10 * 10**9, bytes_accessed=23 * 10**6, transcendentals=2 * 10**6
        ),
        name="experts",
    )(got, *pinned([weights]))


def expert_grads(*args):
    return pl.pallas_call(
        expert_grad_kernel,
        grid=(GRP // 2,),
        out_shape=hbm(GRP * D, D, dtype=low),
        in_specs=[HIDDEN, HIDDEN, TURNED, TURNED],
        out_specs=PAIR,
        compiler_params=params(28),
        cost_estimate=pl.CostEstimate(
            flops=6 * 10**9, bytes_accessed=18 * 10**6, transcendentals=0
        ),
        name="expert_grads",
    )(*pinned(args))


def token_backward(*args):
    outs = (
        hbm(1, TOK, D, dtype=low),
        hbm(1, TOK, D),
        hbm(16, BLOCK, WIDE, dtype=low),
        hbm(16, BLOCK, WIDE, dtype=low),
    )
    return pl.pallas_call(
        backward_kernel,
        out_shape=outs,
        in_specs=[in_smem()] + in_vmem(4) + in_place(25),
        out_specs=tuple(in_place(4)),
        scratch_shapes=vmem_like(args[5:14])
        + vmem_like(outs[:2])
        + [
            pltpu.VMEM((ROWS, D), full),
            pltpu.VMEM((ROWS, D), full),
            pltpu.VMEM((SLOTS, D), low),
            pltpu.VMEM((ROWS, 3 * D), low),
            pltpu.VMEM((D, DENSE), low),
            pltpu.SemaphoreType.DMA((16,)),
            pltpu.SemaphoreType.DMA((29,)),
            pltpu.VMEM((2, 16, BLOCK, WIDE), low),
            pltpu.VMEM((2, 4, 16, WIDE), full),
        ],
        compiler_params=params(48),
        cost_estimate=pl.CostEstimate(
            flops=400 * 10**9, bytes_accessed=18 * 10**6, transcendentals=10**4
        ),
        name="token_backward",
    )(*args[:5], *pinned(args[5:]))


def owner_step(pieces, arrays, small):
    qkv = pl.BlockSpec((OWN, D), lambda i: (0, jnp.minimum(i, 2)))
    proj = pl.BlockSpec((OWN, D), lambda i: (0, 0))
    whole = [pl.BlockSpec(a.shape, lambda i: (0, 0)) for a in small]
    return pl.pallas_call(
        owner_kernel,
        grid=(4,),
        out_shape=tuple([hbm(*a.shape) for a in arrays] + [shape(*a.shape) for a in small]),
        in_specs=[
            pl.BlockSpec((2, 2, PIECE + 1, WIDE), lambda i: (0, i, 0, 0)),
            pl.BlockSpec((2, 8, PIECE + 1, WIDE), lambda i: (0, 0, 0, 0)),
        ]
        + [qkv] * 3
        + [proj] * 3
        + whole,
        out_specs=tuple([qkv] * 3 + [proj] * 3 + whole),
        compiler_params=params(24),
        cost_estimate=pl.CostEstimate(
            flops=10**7, bytes_accessed=8 * 10**6, transcendentals=10**6
        ),
        name="owner_step",
    )(pieces, pieces, *pinned(arrays), *small)


def exchange(value):
    return lax.all_to_all(value, "exp", split_axis=0, concat_axis=0, tiled=True)


def dense_sum(keep, give):
    def along(step, value):
        hops = [(2 * x + c, 2 * ((x + step) % 4) + c) for x in range(4) for c in range(2)]
        return lax.ppermute(value, "grp", hops)

    got = lax.ppermute(give, "grp", [(i, i ^ 1) for i in range(GRP)])
    pieces = exchange((keep.astype(full) + got.astype(full)).astype(low))
    total = jnp.sum(pieces.astype(full), axis=0)
    main, rest = total[: 4 * PIECE].reshape(4, PIECE, WIDE), total[4 * PIECE :][:4, None]
    total = jnp.concatenate([main, rest], axis=1)
    sent = [along(step, total[step].astype(low)).astype(full) for step in (1, 2, 3)]
    return total[0] + sent[0] + sent[1] + sent[2]


def on_device(
    images,
    cotangent,
    expert_ids,
    kept_routes,
    qkv_master,
    qkv_first,
    qkv_second,
    proj_master,
    proj_first,
    proj_second,
    router_master,
    router_first,
    router_second,
    norm_master,
    norm_first,
    norm_second,
    inner_master,
    inner_first,
    inner_second,
    outer_master,
    outer_first,
    outer_second,
):
    pieces = dense_pieces(*pack(qkv_master, proj_master, router_master, norm_master))
    rows = piece_rows(lax.axis_index("grp"))
    mine = jnp.concatenate([inner_master[0].astype(low), outer_master[0].astype(low).T], axis=1)
    mine, *_ = lax.optimization_barrier((mine, pieces[3], pieces[4]))
    weights = lax.all_gather(mine, "grp", axis=0, tiled=True)

    ids = expert_ids.reshape(TOK, 2)
    kept = kept_routes.reshape(TOK, 2)
    flat = ids.reshape(-1)
    marks = (flat[:, None] == jnp.arange(EXPERTS, dtype=jnp.int32)[None, :]).astype(jnp.int32)
    slots = jnp.sum((jnp.cumsum(marks, axis=0) - marks) * marks, axis=1).reshape(TOK, 2)
    places = jnp.where(slots < CAP - 1, ids * 32 + slots, LAST + ids)
    target = jnp.where(kept > 0, places, -1)
    padding = ((0, ROWS - TOK), (0, 0))
    target = jnp.pad(target, padding, constant_values=-1)
    ids = jnp.pad(ids, padding, constant_values=-1)
    keep = jnp.pad(kept.astype(full), padding)

    send, m, a, qkv, p, o, c, r = token_forward(
        rows, ids, keep, target.T, images, cotangent, *pieces
    )
    back, *hidden = experts_both_ways(exchange(send), weights)
    back = exchange(back)
    grad = lax.psum_scatter(expert_grads(*hidden), "grp", scatter_dimension=0, tiled=True)
    result, image_grad, keep_grads, give_grads = token_backward(
        rows, ids, target, keep, back, m, r, cotangent, c, o, qkv, p, a, images, *pieces
    )
    (
        inner_moment,
        inner_square,
        inner_weight,
        outer_moment,
        outer_square,
        outer_weight,
    ) = expert_step(
        grad,
        (inner_master, inner_first, inner_second, outer_master, outer_first, outer_second),
    )
    block = dense_sum(keep_grads, give_grads).astype(low)
    block = exchange(jnp.broadcast_to(block[None], (16, PIECE + 1, WIDE)))
    block, inner_weight = lax.optimization_barrier((block, inner_weight))
    small = (router_master, router_first, router_second, norm_master, norm_first, norm_second)
    new = owner_step(
        block.reshape(2, 8, PIECE + 1, WIDE),
        (qkv_master, qkv_first, qkv_second, proj_master, proj_first, proj_second),
        [value.T for value in small],
    )
    qkv_moment, qkv_square, qkv_weight, proj_moment, proj_square, proj_weight = new[:6]
    router_moment, router_square, router_weight = [value.T for value in new[6:9]]
    norm_moment, norm_square, norm_weight = [value.T for value in new[9:]]
    return (
        result,
        image_grad,
        qkv_moment,
        qkv_square,
        qkv_weight,
        proj_moment,
        proj_square,
        proj_weight,
        router_moment,
        router_square,
        router_weight,
        norm_moment,
        norm_square,
        norm_weight,
        inner_moment,
        inner_square,
        inner_weight,
        outer_moment,
        outer_square,
        outer_weight,
    )


def solution(mesh):
    in_specs = (
        P(("grp", "exp"), None, None),
        P(("grp", "exp"), None, None),
        P(("grp", "exp"), None, None),
        P(("grp", "exp"), None, None),
        P("grp", None),
        P("grp", None),
        P("grp", None),
        P("grp", None),
        P("grp", None),
        P("grp", None),
        P("grp", None),
        P("grp", None),
        P("grp", None),
        P("grp", None),
        P("grp", None),
        P("grp", None),
        P("exp", None, "grp"),
        P("exp", None, "grp"),
        P("exp", None, "grp"),
        P("exp", "grp", None),
        P("exp", "grp", None),
        P("exp", "grp", None),
    )
    out_specs = (
        P(("grp", "exp"), None, None),
        P(("grp", "exp"), None, None),
        P("grp", None),
        P("grp", None),
        P("grp", None),
        P("grp", None),
        P("grp", None),
        P("grp", None),
        P("grp", None),
        P("grp", None),
        P("grp", None),
        P("grp", None),
        P("grp", None),
        P("grp", None),
        P("exp", None, "grp"),
        P("exp", None, "grp"),
        P("exp", None, "grp"),
        P("exp", "grp", None),
        P("exp", "grp", None),
        P("exp", "grp", None),
    )
    return jax.shard_map(
        on_device, mesh=mesh, in_specs=in_specs, out_specs=out_specs, check_vma=False
    )
```

```python
import jax
import jax.numpy as jnp
from jax import lax
from jax.experimental import pallas as pl
from jax.experimental.pallas import tpu as pltpu
from jax.sharding import PartitionSpec as P

HEADS = 12
HEAD_DIM = 64
STEP = 10
D = 768
TOK = 197
ROWS = 208
EXPERTS = 16
CAP = 33
SLOTS = EXPERTS * CAP
DENSE = 3200
GRP = 8
OWN = D // GRP
PIECE = 48
WIDE = 384
HID = 384
LAST = EXPERTS * 32
BLOCK = 4 * PIECE + 16

norm_epsilon = 1e-06
beta_first = 0.9
beta_second = 0.999
adam_epsilon = 1e-08
weight_decay = 0.1
score_scale = HEAD_DIM ** (-0.5)
low = jnp.bfloat16
full = jnp.float32


def dot(a, b, dims=((1,), (0,))):
    return lax.dot_general(a, b, (dims, ((), ())), preferred_element_type=jnp.float32)


NT = ((1,), (1,))
TN = ((0,), (0,))


def unit_rows(values):
    centered = values - jnp.mean(values, axis=-1, keepdims=True)
    variance = jnp.mean(centered * centered, axis=-1, keepdims=True)
    scale = lax.rsqrt(variance + norm_epsilon)
    return centered * scale, scale


def norm_rows(w_ref):
    return w_ref[:, 3072:3200].astype(full).T[16:24]


def pack_kernel(qkv_ref, proj_ref, router_ref, norm_ref, *refs):
    first_out, second_out, qkv_in, proj_in, router_in, norm_in, sem = refs
    sources = (qkv_ref, proj_ref, router_ref, norm_ref)
    loads = [
        pltpu.make_async_copy(source, target, sem.at[i])
        for i, (source, target) in enumerate(zip(sources, refs[2:6]))
    ]
    for load in loads:
        load.start()
    for load in loads[2:]:
        load.wait()
    rest = [router_in[...], norm_in[...], jnp.zeros((DENSE - 3092, OWN), full)]
    rest = jnp.concatenate(rest, axis=0).T.astype(low)
    for load in loads[:2]:
        load.wait()
    for i, out_ref in enumerate((first_out, second_out)):
        rows = slice(i * PIECE, (i + 1) * PIECE)
        out_ref[:, 0:2304] = qkv_in[rows, :].astype(low)
        out_ref[:, 2304:3072] = proj_in[rows, :].astype(low)
        out_ref[:, 3072:3200] = rest[rows, :]


def dense_pieces(first, second):
    def along(step, value):
        hops = [(2 * x + c, 2 * ((x + step) % 4) + c) for x in range(4) for c in range(2)]
        return lax.ppermute(value, "grp", hops)

    def across(value):
        return lax.ppermute(value, "grp", [(i, i ^ 1) for i in range(GRP)])

    up_first, down_second = along(1, first), along(3, second)
    up_first, down_second, again, other = lax.optimization_barrier(
        (up_first, down_second, second, first)
    )
    up_second, down_first = along(1, again), along(3, other)
    far_first, far_second = along(1, up_first), along(3, down_second)
    here = [first, second, up_first, up_second, down_first, down_second, far_first, far_second]
    return here + [across(piece) for piece in here]


def piece_rows(place):
    x, c = place // 2, place % 2
    rows = []
    for core in (c, 1 - c):
        for step in (0, 3, 1, 2):
            near = OWN * (2 * ((x + step) % 4) + core)
            rows += [near, near + PIECE]
    return jnp.stack(rows + [x, c]).astype(jnp.int32)


def dense_copies(rows_ref, pieces, w_ref, sem):
    copies = []
    for i, piece in enumerate(pieces):
        at = pl.multiple_of(rows_ref[i], PIECE)
        copies.append(pltpu.make_async_copy(piece, w_ref.at[pl.ds(at, PIECE), :], sem.at[i]))
        copies[-1].start()
    return copies


class Moves:
    def __init__(self, sem):
        self.sem, self.open = sem, {}

    def start(self, name, source, target):
        self.open[name] = pltpu.make_async_copy(source, target, self.sem.at[len(self.open)])
        self.open[name].start()

    def wait(self, *names):
        for name in names:
            self.open[name].wait()


def pack_slots(totals, out_ref):
    unused = jnp.zeros((4, 128), full)
    for e in range(EXPERTS):
        last = []
        for part, total in enumerate(totals):
            for j in range(6):
                cols, at = slice(j * 128, (j + 1) * 128), (part * 6 + j) * 32
                out_ref[e, at : at + 32, :] = total[e * 32 : (e + 1) * 32, cols].astype(low)
                last.append(total[LAST + e : LAST + e + 1, cols])
        out_ref[e, 384:400, :] = jnp.concatenate(last + [unused], axis=0).astype(low)


def unpack_slots(got_ref, part, rows_ref):
    last = []
    for e in range(EXPERTS):
        for j in range(6):
            cols, at = slice(j * 128, (j + 1) * 128), (part * 6 + j) * 32
            rows_ref[e * 32 : (e + 1) * 32, cols] = got_ref[e, at : at + 32, :]
        block = got_ref[e, 384:400, :].astype(full)
        rows = [block[part * 6 + j : part * 6 + j + 1] for j in range(6)]
        last.append(jnp.concatenate(rows, axis=1))
    rows_ref[LAST:SLOTS, :] = jnp.concatenate(last, axis=0).astype(low)


def padded(ref, pad_ref):
    pad_ref[192:ROWS, :] = jnp.zeros((ROWS - 192, D), full)
    pad_ref[0:TOK, :] = ref[0].astype(full)
    return pad_ref[...]


def lanes(shape):
    return lax.broadcasted_iota(jnp.int32, shape, 1)


def half_masks():
    lane = lanes((1, 128))
    first = (lane < HEAD_DIM).astype(full)
    return first.astype(low), (1.0 - first).astype(low)


def forward_kernel(rows_ref, ids_ref, keep_ref, trow_ref, x_hbm, g_hbm, *refs):
    pieces, refs = refs[:16], refs[16:]
    outs, refs = refs[:8], refs[8:]
    send_ref = outs[0]
    m_ref, a_ref, qkv_ref, p_ref, o_ref, c_ref, r_ref = refs[:7]
    x_ref, g_ref, x_pad, g_pad, w_ref, w_sem, sem, spare, spare2 = refs[7:]
    moves = Moves(sem)
    moves.start("x", x_hbm, x_ref)
    copies = dense_copies(rows_ref, pieces, w_ref, w_sem)
    moves.start("g", g_hbm, g_ref)
    moves.wait("x")
    x = padded(x_ref, x_pad)
    unit = unit_rows(x)[0]
    moves.wait("g")
    g = padded(g_ref, g_pad)
    for copy in copies:
        copy.wait()
    norms = norm_rows(w_ref)
    a = (unit * norms[0:1] + norms[1:2]).astype(low)
    a_ref[...] = a
    moves.start("a", a_ref, outs[2])
    for part in range(3):
        cols = slice(part * D, part * D + D)
        qkv_ref[:, cols] = dot(a, w_ref[:, cols]).astype(low)
    moves.start("qkv", qkv_ref, outs[3])
    first, second = half_masks()
    seen = lanes((ROWS, ROWS)) < TOK
    low_half = lanes((ROWS, 128)) < HEAD_DIM
    for pair in range(HEADS // 2):
        at = pair * 128
        q = qkv_ref[:, at : at + 128]
        k = qkv_ref[:, D + at : D + at + 128]
        v = qkv_ref[:, 2 * D + at : 2 * D + at + 128]
        mixed = []
        for side, mask in enumerate((first, second)):
            s = dot(q * mask, k, NT) * score_scale
            s = jnp.where(seen, s, -1e30)
            e = jnp.exp(s - jnp.max(s, axis=1, keepdims=True))
            p = (e / jnp.sum(e, axis=1, keepdims=True)).astype(low)
            p_ref[2 * pair + side] = p
            mixed.append(dot(p, v))
        o_ref[:, at : at + 128] = jnp.where(low_half, mixed[0], mixed[1]).astype(low)
    moves.start("p", p_ref, outs[4])
    moves.start("o", o_ref, outs[5])
    m = x + dot(o_ref[...], w_ref[:, 2304:3072])
    m_ref[...] = m
    moves.start("m", m_ref, outs[1])
    c = (unit_rows(m)[0] * norms[2:3] + norms[3:4]).astype(low)
    c_ref[...] = c
    moves.start("c", c_ref, outs[6])
    lane = lanes((ROWS, 128))
    logits = jnp.where(lane < EXPERTS, dot(c, w_ref[:, 3072:3200]), -1e30)
    e = jnp.exp(logits - jnp.max(logits, axis=1, keepdims=True))
    r = e / jnp.sum(e, axis=1, keepdims=True)
    r_ref[...] = r
    moves.start("r", r_ref, outs[7])
    slot = lax.broadcasted_iota(jnp.int32, (SLOTS, ROWS), 0)
    picks, grads = [], []
    for j in range(2):
        chosen = lane == ids_ref[:, j : j + 1]
        gate = jnp.sum(jnp.where(chosen, r, 0.0), axis=1, keepdims=True) * keep_ref[:, j : j + 1]
        picks.append((slot == trow_ref[j : j + 1, :]).astype(full).astype(low))
        grads.append((gate * g).astype(low))
    spare[...] = dot(picks[0] + picks[1], c)
    spare2[...] = dot(picks[0], grads[0]) + dot(picks[1], grads[1])
    pack_slots((spare, spare2), send_ref)
    moves.wait("a", "qkv", "p", "o", "m", "c", "r")


def expert_kernel(
    got_ref, w_ref, back_ref, h_ref, du_ref, xt_ref, dzt_ref, z_sum, dx_sum, xs, dzs
):
    step = pl.program_id(0)

    @pl.when(step == 0)
    def _():
        unpack_slots(got_ref, 0, xs)
        unpack_slots(got_ref, 1, dzs)
        xt_ref[...] = xs[...].T
        dzt_ref[...] = dzs[...].T
        z_sum[...] = jnp.zeros_like(z_sum)
        dx_sum[...] = jnp.zeros_like(dx_sum)

    wi = jnp.concatenate([w_ref[0:D, 0:HID], w_ref[D:, 0:HID]], axis=1)
    wot = jnp.concatenate([w_ref[0:D, HID:], w_ref[D:, HID:]], axis=1)
    u = dot(xs[...], wi)
    dh = dot(dzs[...], wot)
    square = u * u
    inner = u * (0.7978845608028654 + (0.7978845608028654 * 0.044715) * square)
    t = jnp.tanh(inner)
    half = 0.5 * t + 0.5
    h = (u * half).astype(low)
    slope = (0.5 * u) * (1.0 - t * t)
    slope = slope * (0.7978845608028654 + (3 * 0.7978845608028654 * 0.044715) * square) + half
    du = (slope * dh).astype(low)
    h_ref[...] = h
    du_ref[...] = du
    z_sum[...] += dot(h, wot, NT)
    dx_sum[...] += dot(du, wi, NT)

    @pl.when(step == pl.num_programs(0) - 1)
    def _():
        pack_slots((z_sum, dx_sum), back_ref)


def expert_grad_kernel(h_ref, du_ref, xt_ref, dzt_ref, out_ref):
    gi = dot(xt_ref[...], du_ref[...]).astype(low)
    go = dot(dzt_ref[...], h_ref[...]).astype(low)
    for i in range(2):
        cols = slice(i * HID, (i + 1) * HID)
        out_ref[i * D : (i + 1) * D, 0:HID] = gi[:, cols]
        out_ref[i * D : (i + 1) * D, HID:] = go[:, cols]


def owner_place(rows_ref, g):
    return (g % 2 + rows_ref[17]) % 2, (g // 2 + 4 - rows_ref[16]) % 4


def spread(rows_ref, grad, part, grads_ref):
    for g in range(GRP):
        side, step = owner_place(rows_ref, g)
        at = pl.multiple_of(step * PIECE, PIECE)
        for r in range(2):
            rows = slice(g * OWN + r * PIECE, g * OWN + (r + 1) * PIECE)
            for k in range(2):
                cols = slice(k * WIDE, (k + 1) * WIDE)
                grads_ref[side, r * 8 + part * 2 + k, pl.ds(at, PIECE), :] = grad[rows, cols]


def spread_extra(rows_ref, extra, rest_ref, grads_ref):
    empty = jnp.zeros((16, 128 - OWN), full)
    for g in range(GRP):
        side, step = owner_place(rows_ref, g)
        cols = slice(g * OWN, (g + 1) * OWN)
        parts = [extra[0:16, cols], empty, extra[16:32, cols], empty, jnp.zeros((16, 128), full)]
        rest_ref[side, step] = jnp.concatenate(parts, axis=1)
    unused = jnp.zeros((12, WIDE), full)
    for side in range(2):
        for e in range(16):
            rows = [rest_ref[side, step, e : e + 1, :] for step in range(4)]
            rows = jnp.concatenate(rows + [unused], axis=0)
            grads_ref[side, e, 4 * PIECE :, :] = rows.astype(low)


def backward_kernel(rows_ref, ids_ref, tcol_ref, keep_ref, back_ref, *refs):
    ins, pieces, refs = refs[:9], refs[9:25], refs[25:]
    outs, refs = refs[:4], refs[4:]
    m_ref, r_ref, g_ref, c_ref, o_ref, qkv_ref, p_ref, a_ref, x_ref = refs[:9]
    result_ref, image_ref = refs[9:11]
    x_pad, g_pad, spare, dqkv, w_ref, w_sem, sem, grads_ref, rest_ref = refs[11:]
    moves = Moves(sem)
    for name in range(1, 5):
        moves.start(name, ins[name - 1], refs[name - 1])
    copies = dense_copies(rows_ref, pieces, w_ref, w_sem)
    for name in range(5, 10):
        moves.start(name, ins[name - 1], refs[name - 1])

    def rows_of(part):
        unpack_slots(back_ref, part, spare)
        return spare[...]

    def send_grads(part):
        rows = pl.ds(0, 4 * PIECE)
        for r in range(2):
            some = pl.ds(r * 8 + part * 2, 2)
            for side in (1, 0):
                moves.start(
                    (part, r, side),
                    grads_ref.at[side, some, rows],
                    outs[2 + side].at[some, rows],
                )

    moves.wait(1, 2, 3)
    g = padded(g_ref, g_pad)
    m = m_ref[...]
    r = r_ref[...]
    lane = lanes((ROWS, 128))
    slot = lanes((ROWS, SLOTS))
    z = rows_of(0)
    total = m
    dr = jnp.zeros((ROWS, 128), full)
    picks = []
    for j in range(2):
        pick = (slot == tcol_ref[:, j : j + 1]).astype(full).astype(low)
        picks.append(pick)
        keep = keep_ref[:, j : j + 1]
        chosen = lane == ids_ref[:, j : j + 1]
        gate = jnp.sum(jnp.where(chosen, r, 0.0), axis=1, keepdims=True) * keep
        zj = dot(pick, z)
        total = total + gate * zj
        dgate = jnp.sum(g * zj, axis=1, keepdims=True) * keep
        dr = dr + jnp.where(chosen, dgate, 0.0)
    result_ref[0] = total[0:TOK].astype(low)
    moves.start("result", result_ref, outs[0])
    for copy in copies:
        copy.wait()
    norms = norm_rows(w_ref)
    moves.wait(4)
    dl = (r * (dr - jnp.sum(dr * r, axis=1, keepdims=True))).astype(low)
    c = c_ref[...]
    gr = dot(dl, c, TN)[0:16]
    dc = dot(dl, w_ref[:, 3072:3200], NT) + dot(picks[0] + picks[1], rows_of(1))
    xh, scale = unit_rows(m)
    dn2 = jnp.sum(dc * xh, axis=0, keepdims=True)
    dn3 = jnp.sum(dc, axis=0, keepdims=True)
    dxh = dc * norms[2:3]
    dm = g + scale * (
        dxh
        - jnp.mean(dxh, axis=1, keepdims=True)
        - xh * jnp.mean(dxh * xh, axis=1, keepdims=True)
    )
    dmb = dm.astype(low)
    moves.wait(5)
    spread(rows_ref, dot(o_ref[...].T, dmb).astype(low), 3, grads_ref)
    send_grads(3)
    do = dot(dmb, w_ref[:, 2304:3072], NT).astype(low)
    first, second = half_masks()
    low_half = lane < HEAD_DIM
    moves.wait(6, 7)
    for pair in range(HEADS // 2):
        at = pair * 128
        q = qkv_ref[:, at : at + 128]
        k = qkv_ref[:, D + at : D + at + 128]
        v = qkv_ref[:, 2 * D + at : 2 * D + at + 128]
        dop = do[:, at : at + 128]
        parts = []
        for side, mask in enumerate((first, second)):
            p_low = p_ref[2 * pair + side]
            p = p_low.astype(full)
            dp = dot(dop * mask, v, NT)
            ds = (p * (dp - jnp.sum(dp * p, axis=1, keepdims=True))).astype(low)
            parts.append((dot(ds, k), dot(ds, q, TN), dot(p_low, dop, TN)))
        for which, factor in enumerate((score_scale, score_scale, 1.0)):
            both = jnp.where(low_half, parts[0][which], parts[1][which]) * factor
            dqkv[:, which * D + at : which * D + at + 128] = both.astype(low)
    moves.wait(8, 9)
    at_rows = a_ref[...].T
    da = jnp.zeros((ROWS, D), full)
    for part in range(3):
        cols = slice(part * D, part * D + D)
        spread(rows_ref, dot(at_rows, dqkv[:, cols]).astype(low), part, grads_ref)
        send_grads(part)
        da = da + dot(dqkv[:, cols], w_ref[:, cols], NT)
    xh, scale = unit_rows(padded(x_ref, x_pad))
    extra = [
        gr,
        jnp.sum(da * xh, axis=0, keepdims=True),
        jnp.sum(da, axis=0, keepdims=True),
        dn2,
        dn3,
        jnp.zeros((12, D), full),
    ]
    spread_extra(rows_ref, jnp.concatenate(extra, axis=0), rest_ref, grads_ref)
    for side in (1, 0):
        rows = pl.ds(4 * PIECE, 16)
        moves.start(("rest", side), grads_ref.at[side, :, rows], outs[2 + side].at[:, rows])
    dxh = da * norms[0:1]
    dx = dm + scale * (
        dxh
        - jnp.mean(dxh, axis=1, keepdims=True)
        - xh * jnp.mean(dxh * xh, axis=1, keepdims=True)
    )
    image_ref[0] = dx[0:TOK]
    moves.start("image", image_ref, outs[1])
    moves.wait(*[name for name in moves.open if name not in range(1, 10)])


def adamw(master, first, second, gradient, rate):
    first = beta_first * first + (1.0 - beta_first) * gradient
    second = beta_second * second + (1.0 - beta_second) * gradient * gradient
    corrected = first * (1.0 / (1.0 - beta_first**STEP))
    scaled = jnp.sqrt(second * (1.0 / (1.0 - beta_second**STEP))) + adam_epsilon
    return (first, second, master - rate * (corrected / scaled + weight_decay * master))


def owner_kernel(pieces_ref, *refs):
    arrays, small, outputs = refs[:6], refs[6:12], refs[12:18]
    small_out, loaded, made, sem = refs[18:24], refs[24:30], refs[30:36], refs[36]
    chunks = [(0, part, 0.04) for part in range(3)] + [(3, 0, 0.2)]
    loads, stores = [], []
    for n, (side, part, _) in enumerate(chunks):
        cols = pl.ds(part * D, D)
        for i in range(side, side + 3):
            slot = n * 3 + i - side
            loads.append(
                pltpu.make_async_copy(
                    arrays[i].at[:, cols], loaded[i].at[:, cols], sem.at[slot]
                )
            )
            loads[-1].start()
            stores.append(
                pltpu.make_async_copy(
                    made[i].at[:, cols], outputs[i].at[:, cols], sem.at[12 + slot]
                )
            )
    rest = jnp.concatenate([pieces_ref[e, PIECE:, :] for e in range(16)], axis=0).astype(full)
    for side, grad, rate in ((0, rest[:, 0:OWN], 0.03), (3, rest[0:4, 128 : 128 + OWN], 0.3)):
        new = adamw(*[ref[...] for ref in small[side : side + 3]], grad, rate)
        for ref, value in zip(small_out[side : side + 3], new):
            ref[...] = value
    for n, (side, part, rate) in enumerate(chunks):
        for load in loads[n * 3 : n * 3 + 3]:
            load.wait()
        for r in range(2):
            rows = slice(r * PIECE, (r + 1) * PIECE)
            for k in range(2):
                cols = slice(part * D + k * WIDE, part * D + (k + 1) * WIDE)
                grad = pieces_ref[r * 8 + n * 2 + k, 0:PIECE, :].astype(full)
                new = adamw(*[ref[rows, cols] for ref in loaded[side : side + 3]], grad, rate)
                for ref, value in zip(made[side : side + 3], new):
                    ref[rows, cols] = value
        for store in stores[n * 3 : n * 3 + 3]:
            store.start()
    for store in stores:
        store.wait()


def expert_step_kernel(grad_ref, *refs):
    inputs, outputs = refs[:6], refs[-6:]
    grad = grad_ref[...].astype(full)
    new = adamw(*[ref[0] for ref in inputs[:3]], grad[:, 0:HID], 0.04)
    new = new + adamw(*[ref[0] for ref in inputs[3:]], grad[:, HID:].T, 0.15)
    for ref, value in zip(outputs, new):
        ref[0] = value


def expert_step(grad, arrays):
    inner = pl.BlockSpec((1, 256, HID), lambda i: (0, i, 0))
    outer = pl.BlockSpec((1, HID, 256), lambda i: (0, 0, i))
    return pl.pallas_call(
        expert_step_kernel,
        grid=(D // 256,),
        out_shape=tuple(hbm(*a.shape) for a in arrays),
        in_specs=[pl.BlockSpec((256, D), lambda i: (i, 0))]
        + [inner] * 3
        + [outer] * 3,
        out_specs=(inner,) * 3 + (outer,) * 3,
        compiler_params=params(32),
        cost_estimate=pl.CostEstimate(
            flops=10**7, bytes_accessed=8 * 10**6, transcendentals=10**6
        ),
        name="expert_step",
    )(*pinned([grad, *arrays]))


def shape(*dims, dtype=jnp.float32):
    return jax.ShapeDtypeStruct(dims, dtype)


def in_vmem(count):
    return [pl.BlockSpec(memory_space=pltpu.VMEM)] * count


def pinned(values):
    return [pltpu.with_memory_space_constraint(v, pltpu.HBM) for v in values]


def hbm(*dims, dtype=jnp.float32):
    return pltpu.HBM(dims, dtype)


def in_smem():
    return pl.BlockSpec(memory_space=pltpu.SMEM)


def in_place(count):
    return [pl.BlockSpec(memory_space=pl.ANY)] * count


def params(mib):
    return pltpu.CompilerParams(vmem_limit_bytes=mib * 2**20)


def pack(qkv, proj, router, norm):
    return pl.pallas_call(
        pack_kernel,
        out_shape=(shape(PIECE, DENSE, dtype=low),) * 2,
        in_specs=in_place(4),
        out_specs=tuple(in_vmem(2)),
        scratch_shapes=vmem_like((qkv, proj, router.T, norm.T)) + [pltpu.SemaphoreType.DMA((4,))],
        compiler_params=params(16),
        cost_estimate=pl.CostEstimate(flops=10**5, bytes_accessed=2 * 10**6, transcendentals=0),
        name="pack",
    )(*pinned((qkv, proj, router.T, norm.T)))


def flat_type(value):
    return value.inner_aval if hasattr(value, "inner_aval") else value


def vmem_like(shapes):
    return [pltpu.VMEM(s.shape, s.dtype) for s in map(flat_type, shapes)]


def token_forward(*args):
    outs = (
        pltpu.VMEM((EXPERTS, 400, 128), low),
        hbm(ROWS, D),
        hbm(ROWS, D, dtype=low),
        hbm(ROWS, 3 * D, dtype=low),
        hbm(HEADS, ROWS, ROWS, dtype=low),
        hbm(ROWS, D, dtype=low),
        hbm(ROWS, D, dtype=low),
        hbm(ROWS, 128),
    )
    return pl.pallas_call(
        forward_kernel,
        out_shape=outs,
        in_specs=[in_smem()] + in_vmem(3) + in_place(18),
        out_specs=tuple(in_vmem(1) + in_place(7)),
        scratch_shapes=vmem_like(outs[1:])
        + [pltpu.VMEM((1, TOK, D), low)] * 2
        + [pltpu.VMEM((ROWS, D), full)] * 2
        + [
            pltpu.VMEM((D, DENSE), low),
            pltpu.SemaphoreType.DMA((16,)),
            pltpu.SemaphoreType.DMA((10,)),
            pltpu.VMEM((SLOTS, D), full),
            pltpu.VMEM((SLOTS, D), full),
        ],
        compiler_params=params(40),
        cost_estimate=pl.CostEstimate(
            flops=4 * 10**9, bytes_accessed=12 * 10**6, transcendentals=10**6
        ),
        name="token_forward",
    )(*args[:4], *pinned(args[4:]))


PAIR = pl.BlockSpec((2 * D, D), lambda i: (i, 0))
HIDDEN = pl.BlockSpec((SLOTS, 2 * HID), lambda i: (0, i))
TURNED = pl.BlockSpec((D, SLOTS), lambda i: (0, 0))


def experts_both_ways(got, weights):
    hidden, turned = hbm(SLOTS, GRP * HID, dtype=low), hbm(D, SLOTS, dtype=low)
    return pl.pallas_call(
        expert_kernel,
        grid=(GRP // 2,),
        out_shape=(
            pltpu.VMEM((EXPERTS, 400, 128), low),
            hidden,
            hidden,
            turned,
            turned,
        ),
        in_specs=in_vmem(1) + [PAIR],
        out_specs=(*in_vmem(1), HIDDEN, HIDDEN, TURNED, TURNED),
        scratch_shapes=[pltpu.VMEM((SLOTS, D), full)] * 2 + [pltpu.VMEM((SLOTS, D), low)] * 2,
        compiler_params=params(44),
        cost_estimate=pl.CostEstimate(
            flops=10 * 10**9, bytes_accessed=23 * 10**6, transcendentals=2 * 10**6
        ),
        name="experts",
    )(got, *pinned([weights]))


def expert_grads(*args):
    return pl.pallas_call(
        expert_grad_kernel,
        grid=(GRP // 2,),
        out_shape=hbm(GRP * D, D, dtype=low),
        in_specs=[HIDDEN, HIDDEN, TURNED, TURNED],
        out_specs=PAIR,
        compiler_params=params(28),
        cost_estimate=pl.CostEstimate(
            flops=6 * 10**9, bytes_accessed=18 * 10**6, transcendentals=0
        ),
        name="expert_grads",
    )(*pinned(args))


def token_backward(*args):
    outs = (
        hbm(1, TOK, D, dtype=low),
        hbm(1, TOK, D),
        hbm(16, BLOCK, WIDE, dtype=low),
        hbm(16, BLOCK, WIDE, dtype=low),
    )
    return pl.pallas_call(
        backward_kernel,
        out_shape=outs,
        in_specs=[in_smem()] + in_vmem(4) + in_place(25),
        out_specs=tuple(in_place(4)),
        scratch_shapes=vmem_like(args[5:14])
        + vmem_like(outs[:2])
        + [
            pltpu.VMEM((ROWS, D), full),
            pltpu.VMEM((ROWS, D), full),
            pltpu.VMEM((SLOTS, D), low),
            pltpu.VMEM((ROWS, 3 * D), low),
            pltpu.VMEM((D, DENSE), low),
            pltpu.SemaphoreType.DMA((16,)),
            pltpu.SemaphoreType.DMA((29,)),
            pltpu.VMEM((2, 16, BLOCK, WIDE), low),
            pltpu.VMEM((2, 4, 16, WIDE), full),
        ],
        compiler_params=params(48),
        cost_estimate=pl.CostEstimate(
            flops=400 * 10**9, bytes_accessed=18 * 10**6, transcendentals=10**4
        ),
        name="token_backward",
    )(*args[:5], *pinned(args[5:]))


def owner_step(pieces, arrays, small):
    return pl.pallas_call(
        owner_kernel,
        out_shape=tuple([hbm(*a.shape) for a in arrays] + [shape(*a.shape) for a in small]),
        in_specs=in_vmem(1) + in_place(6) + in_vmem(6),
        out_specs=tuple(in_place(6) + in_vmem(6)),
        scratch_shapes=vmem_like(arrays) * 2 + [pltpu.SemaphoreType.DMA((24,))],
        compiler_params=params(24),
        cost_estimate=pl.CostEstimate(
            flops=10**7, bytes_accessed=8 * 10**6, transcendentals=10**6
        ),
        name="owner_step",
    )(pieces, *pinned(arrays), *small)


def exchange(value):
    return lax.all_to_all(value, "exp", split_axis=0, concat_axis=0, tiled=True)


def dense_sum(keep, give):
    def along(step, value):
        hops = [(2 * x + c, 2 * ((x + step) % 4) + c) for x in range(4) for c in range(2)]
        return lax.ppermute(value, "grp", hops)

    got = lax.ppermute(give, "grp", [(i, i ^ 1) for i in range(GRP)])
    pieces = exchange((keep.astype(full) + got.astype(full)).astype(low))
    total = jnp.sum(pieces.astype(full), axis=0)
    main, rest = total[: 4 * PIECE].reshape(4, PIECE, WIDE), total[4 * PIECE :][:4, None]
    total = jnp.concatenate([main, rest], axis=1)
    sent = [along(step, total[step].astype(low)).astype(full) for step in (1, 2, 3)]
    return total[0] + sent[0] + sent[1] + sent[2]


def on_device(
    images,
    cotangent,
    expert_ids,
    kept_routes,
    qkv_master,
    qkv_first,
    qkv_second,
    proj_master,
    proj_first,
    proj_second,
    router_master,
    router_first,
    router_second,
    norm_master,
    norm_first,
    norm_second,
    inner_master,
    inner_first,
    inner_second,
    outer_master,
    outer_first,
    outer_second,
):
    pieces = dense_pieces(*pack(qkv_master, proj_master, router_master, norm_master))
    rows = piece_rows(lax.axis_index("grp"))
    mine = jnp.concatenate([inner_master[0].astype(low), outer_master[0].astype(low).T], axis=1)
    mine, *_ = lax.optimization_barrier((mine, pieces[3], pieces[4]))
    weights = lax.all_gather(mine, "grp", axis=0, tiled=True)

    ids = expert_ids.reshape(TOK, 2)
    kept = kept_routes.reshape(TOK, 2)
    flat = ids.reshape(-1)
    marks = (flat[:, None] == jnp.arange(EXPERTS, dtype=jnp.int32)[None, :]).astype(jnp.int32)
    slots = jnp.sum((jnp.cumsum(marks, axis=0) - marks) * marks, axis=1).reshape(TOK, 2)
    places = jnp.where(slots < CAP - 1, ids * 32 + slots, LAST + ids)
    target = jnp.where(kept > 0, places, -1)
    padding = ((0, ROWS - TOK), (0, 0))
    target = jnp.pad(target, padding, constant_values=-1)
    ids = jnp.pad(ids, padding, constant_values=-1)
    keep = jnp.pad(kept.astype(full), padding)

    send, m, a, qkv, p, o, c, r = token_forward(
        rows, ids, keep, target.T, images, cotangent, *pieces
    )
    back, *hidden = experts_both_ways(exchange(send), weights)
    back = exchange(back)
    grad = lax.psum_scatter(expert_grads(*hidden), "grp", scatter_dimension=0, tiled=True)
    result, image_grad, keep_grads, give_grads = token_backward(
        rows, ids, target, keep, back, m, r, cotangent, c, o, qkv, p, a, images, *pieces
    )
    (
        inner_moment,
        inner_square,
        inner_weight,
        outer_moment,
        outer_square,
        outer_weight,
    ) = expert_step(
        grad,
        (inner_master, inner_first, inner_second, outer_master, outer_first, outer_second),
    )
    block = dense_sum(keep_grads, give_grads).astype(low)
    block = exchange(jnp.broadcast_to(block[None], (16, PIECE + 1, WIDE)))
    block, inner_weight = lax.optimization_barrier((block, inner_weight))
    small = (router_master, router_first, router_second, norm_master, norm_first, norm_second)
    new = owner_step(
        block,
        (qkv_master, qkv_first, qkv_second, proj_master, proj_first, proj_second),
        [value.T for value in small],
    )
    qkv_moment, qkv_square, qkv_weight, proj_moment, proj_square, proj_weight = new[:6]
    router_moment, router_square, router_weight = [value.T for value in new[6:9]]
    norm_moment, norm_square, norm_weight = [value.T for value in new[9:]]
    return (
        result,
        image_grad,
        qkv_moment,
        qkv_square,
        qkv_weight,
        proj_moment,
        proj_square,
        proj_weight,
        router_moment,
        router_square,
        router_weight,
        norm_moment,
        norm_square,
        norm_weight,
        inner_moment,
        inner_square,
        inner_weight,
        outer_moment,
        outer_square,
        outer_weight,
    )


def solution(mesh):
    in_specs = (
        P(("grp", "exp"), None, None),
        P(("grp", "exp"), None, None),
        P(("grp", "exp"), None, None),
        P(("grp", "exp"), None, None),
        P("grp", None),
        P("grp", None),
        P("grp", None),
        P("grp", None),
        P("grp", None),
        P("grp", None),
        P("grp", None),
        P("grp", None),
        P("grp", None),
        P("grp", None),
        P("grp", None),
        P("grp", None),
        P("exp", None, "grp"),
        P("exp", None, "grp"),
        P("exp", None, "grp"),
        P("exp", "grp", None),
        P("exp", "grp", None),
        P("exp", "grp", None),
    )
    out_specs = (
        P(("grp", "exp"), None, None),
        P(("grp", "exp"), None, None),
        P("grp", None),
        P("grp", None),
        P("grp", None),
        P("grp", None),
        P("grp", None),
        P("grp", None),
        P("grp", None),
        P("grp", None),
        P("grp", None),
        P("grp", None),
        P("grp", None),
        P("grp", None),
        P("exp", None, "grp"),
        P("exp", None, "grp"),
        P("exp", None, "grp"),
        P("exp", "grp", None),
        P("exp", "grp", None),
        P("exp", "grp", None),
    )
    return jax.shard_map(
        on_device, mesh=mesh, in_specs=in_specs, out_specs=out_specs, check_vma=False
    )
```

```python
import jax
import jax.numpy as jnp
from jax import lax
from jax.experimental import pallas as pl
from jax.experimental.pallas import tpu as pltpu
from jax.sharding import PartitionSpec as P

HEADS = 12
HEAD_DIM = 64
STEP = 10
D = 768
TOK = 197
ROWS = 208
EXPERTS = 16
CAP = 33
SLOTS = EXPERTS * CAP
DENSE = 3200
GRP = 8
OWN = D // GRP
PIECE = 48
WIDE = 384
HID = 384
LAST = EXPERTS * 32
BLOCK = 4 * PIECE + 16

norm_epsilon = 1e-06
beta_first = 0.9
beta_second = 0.999
adam_epsilon = 1e-08
weight_decay = 0.1
score_scale = HEAD_DIM ** (-0.5)
low = jnp.bfloat16
full = jnp.float32


def dot(a, b, dims=((1,), (0,))):
    return lax.dot_general(a, b, (dims, ((), ())), preferred_element_type=jnp.float32)


NT = ((1,), (1,))
TN = ((0,), (0,))


def unit_rows(values):
    centered = values - jnp.mean(values, axis=-1, keepdims=True)
    variance = jnp.mean(centered * centered, axis=-1, keepdims=True)
    scale = lax.rsqrt(variance + norm_epsilon)
    return centered * scale, scale


def norm_rows(w_ref):
    return w_ref[:, 3072:3200].astype(full).T[16:24]


def pack_kernel(qkv_ref, proj_ref, router_ref, norm_ref, *refs):
    first_out, second_out, qkv_in, proj_in, router_in, norm_in, sem = refs
    sources = (qkv_ref, proj_ref, router_ref, norm_ref)
    loads = [
        pltpu.make_async_copy(source, target, sem.at[i])
        for i, (source, target) in enumerate(zip(sources, refs[2:6]))
    ]
    for load in loads:
        load.start()
    for load in loads[2:]:
        load.wait()
    rest = [router_in[...], norm_in[...], jnp.zeros((DENSE - 3092, OWN), full)]
    rest = jnp.concatenate(rest, axis=0).T.astype(low)
    for load in loads[:2]:
        load.wait()
    for i, out_ref in enumerate((first_out, second_out)):
        rows = slice(i * PIECE, (i + 1) * PIECE)
        out_ref[:, 0:2304] = qkv_in[rows, :].astype(low)
        out_ref[:, 2304:3072] = proj_in[rows, :].astype(low)
        out_ref[:, 3072:3200] = rest[rows, :]


def dense_pieces(first, second, target):
    def along(step, value):
        hops = [(2 * x + c, 2 * ((x + step) % 4) + c) for x in range(4) for c in range(2)]
        return lax.ppermute(value, "grp", hops)

    def across(value):
        return lax.ppermute(value, "grp", [(i, i ^ 1) for i in range(GRP)])

    up_first, down_second = along(1, first), along(3, second)
    up_first, down_second, again, other, target = lax.optimization_barrier(
        (up_first, down_second, second, first, target)
    )
    up_second, down_first = along(1, again), along(3, other)
    far_first, far_second = along(1, up_first), along(3, down_second)
    here = [first, second, up_first, up_second, down_first, down_second, far_first, far_second]
    return here + [across(piece) for piece in here], target


def piece_rows(place):
    x, c = place // 2, place % 2
    rows = []
    for core in (c, 1 - c):
        for step in (0, 3, 1, 2):
            near = OWN * (2 * ((x + step) % 4) + core)
            rows += [near, near + PIECE]
    return jnp.stack(rows + [x, c]).astype(jnp.int32)


def dense_copies(rows_ref, pieces, w_ref, sem):
    copies = []
    for i, piece in enumerate(pieces):
        at = pl.multiple_of(rows_ref[i], PIECE)
        copies.append(pltpu.make_async_copy(piece, w_ref.at[pl.ds(at, PIECE), :], sem.at[i]))
        copies[-1].start()
    return copies


class Moves:
    def __init__(self, sem):
        self.sem, self.open = sem, {}

    def start(self, name, source, target):
        self.open[name] = pltpu.make_async_copy(source, target, self.sem.at[len(self.open)])
        self.open[name].start()

    def wait(self, *names):
        for name in names:
            self.open[name].wait()


def pack_slots(totals, out_ref):
    unused = jnp.zeros((4, 128), full)
    for e in range(EXPERTS):
        last = []
        for part, total in enumerate(totals):
            for j in range(6):
                cols, at = slice(j * 128, (j + 1) * 128), (part * 6 + j) * 32
                out_ref[e, at : at + 32, :] = total[e * 32 : (e + 1) * 32, cols].astype(low)
                last.append(total[LAST + e : LAST + e + 1, cols])
        out_ref[e, 384:400, :] = jnp.concatenate(last + [unused], axis=0).astype(low)


def unpack_slots(got_ref, part, rows_ref):
    last = []
    for e in range(EXPERTS):
        for j in range(6):
            cols, at = slice(j * 128, (j + 1) * 128), (part * 6 + j) * 32
            rows_ref[e * 32 : (e + 1) * 32, cols] = got_ref[e, at : at + 32, :]
        block = got_ref[e, 384:400, :].astype(full)
        rows = [block[part * 6 + j : part * 6 + j + 1] for j in range(6)]
        last.append(jnp.concatenate(rows, axis=1))
    rows_ref[LAST:SLOTS, :] = jnp.concatenate(last, axis=0).astype(low)


def padded(ref, pad_ref):
    pad_ref[192:ROWS, :] = jnp.zeros((ROWS - 192, D), full)
    pad_ref[0:TOK, :] = ref[0].astype(full)
    return pad_ref[...]


def lanes(shape):
    return lax.broadcasted_iota(jnp.int32, shape, 1)


def half_masks():
    lane = lanes((1, 128))
    first = (lane < HEAD_DIM).astype(full)
    return first.astype(low), (1.0 - first).astype(low)


def forward_kernel(rows_ref, ids_ref, keep_ref, trow_ref, x_hbm, g_hbm, *refs):
    pieces, refs = refs[:16], refs[16:]
    outs, refs = refs[:8], refs[8:]
    send_ref = outs[0]
    m_ref, a_ref, qkv_ref, p_ref, o_ref, c_ref, r_ref = refs[:7]
    x_ref, g_ref, x_pad, g_pad, w_ref, w_sem, sem, spare, spare2 = refs[7:]
    moves = Moves(sem)
    moves.start("x", x_hbm, x_ref)
    copies = dense_copies(rows_ref, pieces, w_ref, w_sem)
    moves.start("g", g_hbm, g_ref)
    moves.wait("x")
    x = padded(x_ref, x_pad)
    unit = unit_rows(x)[0]
    moves.wait("g")
    g = padded(g_ref, g_pad)
    for copy in copies:
        copy.wait()
    norms = norm_rows(w_ref)
    a = (unit * norms[0:1] + norms[1:2]).astype(low)
    a_ref[...] = a
    moves.start("a", a_ref, outs[2])
    for part in range(3):
        cols = slice(part * D, part * D + D)
        qkv_ref[:, cols] = dot(a, w_ref[:, cols]).astype(low)
    moves.start("qkv", qkv_ref, outs[3])
    first, second = half_masks()
    seen = lanes((ROWS, ROWS)) < TOK
    low_half = lanes((ROWS, 128)) < HEAD_DIM
    for pair in range(HEADS // 2):
        at = pair * 128
        q = qkv_ref[:, at : at + 128]
        k = qkv_ref[:, D + at : D + at + 128]
        v = qkv_ref[:, 2 * D + at : 2 * D + at + 128]
        mixed = []
        for side, mask in enumerate((first, second)):
            s = dot(q * mask, k, NT) * score_scale
            s = jnp.where(seen, s, -1e30)
            e = jnp.exp(s - jnp.max(s, axis=1, keepdims=True))
            p = (e / jnp.sum(e, axis=1, keepdims=True)).astype(low)
            p_ref[2 * pair + side] = p
            mixed.append(dot(p, v))
        o_ref[:, at : at + 128] = jnp.where(low_half, mixed[0], mixed[1]).astype(low)
    moves.start("p", p_ref, outs[4])
    moves.start("o", o_ref, outs[5])
    m = x + dot(o_ref[...], w_ref[:, 2304:3072])
    m_ref[...] = m
    moves.start("m", m_ref, outs[1])
    c = (unit_rows(m)[0] * norms[2:3] + norms[3:4]).astype(low)
    c_ref[...] = c
    moves.start("c", c_ref, outs[6])
    lane = lanes((ROWS, 128))
    logits = jnp.where(lane < EXPERTS, dot(c, w_ref[:, 3072:3200]), -1e30)
    e = jnp.exp(logits - jnp.max(logits, axis=1, keepdims=True))
    r = e / jnp.sum(e, axis=1, keepdims=True)
    r_ref[...] = r
    moves.start("r", r_ref, outs[7])
    slot = lax.broadcasted_iota(jnp.int32, (SLOTS, ROWS), 0)
    picks, grads = [], []
    for j in range(2):
        chosen = lane == ids_ref[:, j : j + 1]
        gate = jnp.sum(jnp.where(chosen, r, 0.0), axis=1, keepdims=True) * keep_ref[:, j : j + 1]
        picks.append((slot == trow_ref[j : j + 1, :]).astype(full).astype(low))
        grads.append((gate * g).astype(low))
    spare[...] = dot(picks[0] + picks[1], c)
    spare2[...] = dot(picks[0], grads[0]) + dot(picks[1], grads[1])
    pack_slots((spare, spare2), send_ref)
    moves.wait("a", "qkv", "p", "o", "m", "c", "r")


def expert_kernel(
    got_ref, w_ref, back_ref, h_ref, du_ref, xt_ref, dzt_ref, z_sum, dx_sum, xs, dzs
):
    step = pl.program_id(0)

    @pl.when(step == 0)
    def _():
        unpack_slots(got_ref, 0, xs)
        unpack_slots(got_ref, 1, dzs)
        xt_ref[...] = xs[...].T
        dzt_ref[...] = dzs[...].T
        z_sum[...] = jnp.zeros_like(z_sum)
        dx_sum[...] = jnp.zeros_like(dx_sum)

    wi = jnp.concatenate([w_ref[0:D, 0:HID], w_ref[D:, 0:HID]], axis=1)
    wot = jnp.concatenate([w_ref[0:D, HID:], w_ref[D:, HID:]], axis=1)
    u = dot(xs[...], wi)
    dh = dot(dzs[...], wot)
    square = u * u
    inner = u * (0.7978845608028654 + (0.7978845608028654 * 0.044715) * square)
    t = jnp.tanh(inner)
    half = 0.5 * t + 0.5
    h = (u * half).astype(low)
    slope = (0.5 * u) * (1.0 - t * t)
    slope = slope * (0.7978845608028654 + (3 * 0.7978845608028654 * 0.044715) * square) + half
    du = (slope * dh).astype(low)
    h_ref[...] = h
    du_ref[...] = du
    z_sum[...] += dot(h, wot, NT)
    dx_sum[...] += dot(du, wi, NT)

    @pl.when(step == pl.num_programs(0) - 1)
    def _():
        pack_slots((z_sum, dx_sum), back_ref)


def expert_grad_kernel(h_ref, du_ref, xt_ref, dzt_ref, out_ref):
    gi = dot(xt_ref[...], du_ref[...]).astype(low)
    go = dot(dzt_ref[...], h_ref[...]).astype(low)
    for i in range(2):
        cols = slice(i * HID, (i + 1) * HID)
        out_ref[i * D : (i + 1) * D, 0:HID] = gi[:, cols]
        out_ref[i * D : (i + 1) * D, HID:] = go[:, cols]


def owner_place(rows_ref, g):
    return (g % 2 + rows_ref[17]) % 2, (g // 2 + 4 - rows_ref[16]) % 4


def spread(rows_ref, grad, part, grads_ref):
    for g in range(GRP):
        side, step = owner_place(rows_ref, g)
        at = pl.multiple_of(step * PIECE, PIECE)
        for r in range(2):
            rows = slice(g * OWN + r * PIECE, g * OWN + (r + 1) * PIECE)
            for k in range(2):
                cols = slice(k * WIDE, (k + 1) * WIDE)
                grads_ref[side, r * 8 + part * 2 + k, pl.ds(at, PIECE), :] = grad[rows, cols]


def spread_extra(rows_ref, extra, rest_ref, grads_ref):
    empty = jnp.zeros((16, 128 - OWN), full)
    for g in range(GRP):
        side, step = owner_place(rows_ref, g)
        cols = slice(g * OWN, (g + 1) * OWN)
        parts = [extra[0:16, cols], empty, extra[16:32, cols], empty, jnp.zeros((16, 128), full)]
        rest_ref[side, step] = jnp.concatenate(parts, axis=1)
    unused = jnp.zeros((12, WIDE), full)
    for side in range(2):
        for e in range(16):
            rows = [rest_ref[side, step, e : e + 1, :] for step in range(4)]
            rows = jnp.concatenate(rows + [unused], axis=0)
            grads_ref[side, e, 4 * PIECE :, :] = rows.astype(low)


def backward_kernel(rows_ref, ids_ref, tcol_ref, keep_ref, back_ref, *refs):
    ins, pieces, refs = refs[:9], refs[9:25], refs[25:]
    outs, refs = refs[:4], refs[4:]
    m_ref, r_ref, g_ref, c_ref, o_ref, qkv_ref, p_ref, a_ref, x_ref = refs[:9]
    result_ref, image_ref = refs[9:11]
    x_pad, g_pad, spare, dqkv, w_ref, w_sem, sem, grads_ref, rest_ref = refs[11:]
    moves = Moves(sem)
    for name in range(1, 5):
        moves.start(name, ins[name - 1], refs[name - 1])
    copies = dense_copies(rows_ref, pieces, w_ref, w_sem)
    for name in range(5, 10):
        moves.start(name, ins[name - 1], refs[name - 1])

    def rows_of(part):
        unpack_slots(back_ref, part, spare)
        return spare[...]

    def send_grads(part):
        rows = pl.ds(0, 4 * PIECE)
        for r in range(2):
            some = pl.ds(r * 8 + part * 2, 2)
            for side in (1, 0):
                moves.start(
                    (part, r, side),
                    grads_ref.at[side, some, rows],
                    outs[2 + side].at[some, rows],
                )

    moves.wait(1, 2, 3)
    g = padded(g_ref, g_pad)
    m = m_ref[...]
    r = r_ref[...]
    lane = lanes((ROWS, 128))
    slot = lanes((ROWS, SLOTS))
    z = rows_of(0)
    total = m
    dr = jnp.zeros((ROWS, 128), full)
    picks = []
    for j in range(2):
        pick = (slot == tcol_ref[:, j : j + 1]).astype(full).astype(low)
        picks.append(pick)
        keep = keep_ref[:, j : j + 1]
        chosen = lane == ids_ref[:, j : j + 1]
        gate = jnp.sum(jnp.where(chosen, r, 0.0), axis=1, keepdims=True) * keep
        zj = dot(pick, z)
        total = total + gate * zj
        dgate = jnp.sum(g * zj, axis=1, keepdims=True) * keep
        dr = dr + jnp.where(chosen, dgate, 0.0)
    result_ref[0] = total[0:TOK].astype(low)
    moves.start("result", result_ref, outs[0])
    for copy in copies:
        copy.wait()
    norms = norm_rows(w_ref)
    moves.wait(4)
    dl = (r * (dr - jnp.sum(dr * r, axis=1, keepdims=True))).astype(low)
    c = c_ref[...]
    gr = dot(dl, c, TN)[0:16]
    dc = dot(dl, w_ref[:, 3072:3200], NT) + dot(picks[0] + picks[1], rows_of(1))
    xh, scale = unit_rows(m)
    dn2 = jnp.sum(dc * xh, axis=0, keepdims=True)
    dn3 = jnp.sum(dc, axis=0, keepdims=True)
    dxh = dc * norms[2:3]
    dm = g + scale * (
        dxh
        - jnp.mean(dxh, axis=1, keepdims=True)
        - xh * jnp.mean(dxh * xh, axis=1, keepdims=True)
    )
    dmb = dm.astype(low)
    moves.wait(5)
    spread(rows_ref, dot(o_ref[...].T, dmb).astype(low), 3, grads_ref)
    send_grads(3)
    do = dot(dmb, w_ref[:, 2304:3072], NT).astype(low)
    first, second = half_masks()
    low_half = lane < HEAD_DIM
    moves.wait(6, 7)
    for pair in range(HEADS // 2):
        at = pair * 128
        q = qkv_ref[:, at : at + 128]
        k = qkv_ref[:, D + at : D + at + 128]
        v = qkv_ref[:, 2 * D + at : 2 * D + at + 128]
        dop = do[:, at : at + 128]
        parts = []
        for side, mask in enumerate((first, second)):
            p_low = p_ref[2 * pair + side]
            p = p_low.astype(full)
            dp = dot(dop * mask, v, NT)
            ds = (p * (dp - jnp.sum(dp * p, axis=1, keepdims=True))).astype(low)
            parts.append((dot(ds, k), dot(ds, q, TN), dot(p_low, dop, TN)))
        for which, factor in enumerate((score_scale, score_scale, 1.0)):
            both = jnp.where(low_half, parts[0][which], parts[1][which]) * factor
            dqkv[:, which * D + at : which * D + at + 128] = both.astype(low)
    moves.wait(8, 9)
    at_rows = a_ref[...].T
    da = jnp.zeros((ROWS, D), full)
    for part in range(3):
        cols = slice(part * D, part * D + D)
        spread(rows_ref, dot(at_rows, dqkv[:, cols]).astype(low), part, grads_ref)
        send_grads(part)
        da = da + dot(dqkv[:, cols], w_ref[:, cols], NT)
    xh, scale = unit_rows(padded(x_ref, x_pad))
    extra = [
        gr,
        jnp.sum(da * xh, axis=0, keepdims=True),
        jnp.sum(da, axis=0, keepdims=True),
        dn2,
        dn3,
        jnp.zeros((12, D), full),
    ]
    spread_extra(rows_ref, jnp.concatenate(extra, axis=0), rest_ref, grads_ref)
    for side in (1, 0):
        rows = pl.ds(4 * PIECE, 16)
        moves.start(("rest", side), grads_ref.at[side, :, rows], outs[2 + side].at[:, rows])
    dxh = da * norms[0:1]
    dx = dm + scale * (
        dxh
        - jnp.mean(dxh, axis=1, keepdims=True)
        - xh * jnp.mean(dxh * xh, axis=1, keepdims=True)
    )
    image_ref[0] = dx[0:TOK]
    moves.start("image", image_ref, outs[1])
    moves.wait(*[name for name in moves.open if name not in range(1, 10)])


def adamw(master, first, second, gradient, rate):
    first = beta_first * first + (1.0 - beta_first) * gradient
    second = beta_second * second + (1.0 - beta_second) * gradient * gradient
    corrected = first * (1.0 / (1.0 - beta_first**STEP))
    scaled = jnp.sqrt(second * (1.0 / (1.0 - beta_second**STEP))) + adam_epsilon
    return (first, second, master - rate * (corrected / scaled + weight_decay * master))


def owner_kernel(pieces_ref, *refs):
    arrays, small, outputs = refs[:6], refs[6:12], refs[12:18]
    small_out, loaded, made, sem = refs[18:24], refs[24:30], refs[30:36], refs[36]
    chunks = [(0, part, 0.04) for part in range(3)] + [(3, 0, 0.2)]
    loads, stores = [], []
    for n, (side, part, _) in enumerate(chunks):
        cols = pl.ds(part * D, D)
        for i in range(side, side + 3):
            slot = n * 3 + i - side
            loads.append(
                pltpu.make_async_copy(
                    arrays[i].at[:, cols], loaded[i].at[:, cols], sem.at[slot]
                )
            )
            loads[-1].start()
            stores.append(
                pltpu.make_async_copy(
                    made[i].at[:, cols], outputs[i].at[:, cols], sem.at[12 + slot]
                )
            )
    rest = jnp.concatenate([pieces_ref[e, PIECE:, :] for e in range(16)], axis=0).astype(full)
    for side, grad, rate in ((0, rest[:, 0:OWN], 0.03), (3, rest[0:4, 128 : 128 + OWN], 0.3)):
        new = adamw(*[ref[...] for ref in small[side : side + 3]], grad, rate)
        for ref, value in zip(small_out[side : side + 3], new):
            ref[...] = value
    for n, (side, part, rate) in enumerate(chunks):
        for load in loads[n * 3 : n * 3 + 3]:
            load.wait()
        for r in range(2):
            rows = slice(r * PIECE, (r + 1) * PIECE)
            for k in range(2):
                cols = slice(part * D + k * WIDE, part * D + (k + 1) * WIDE)
                grad = pieces_ref[r * 8 + n * 2 + k, 0:PIECE, :].astype(full)
                new = adamw(*[ref[rows, cols] for ref in loaded[side : side + 3]], grad, rate)
                for ref, value in zip(made[side : side + 3], new):
                    ref[rows, cols] = value
        for store in stores[n * 3 : n * 3 + 3]:
            store.start()
    for store in stores:
        store.wait()


def expert_step_kernel(grad_ref, *refs):
    inputs, outputs = refs[:6], refs[-6:]
    grad = grad_ref[...].astype(full)
    new = adamw(*[ref[0] for ref in inputs[:3]], grad[:, 0:HID], 0.04)
    new = new + adamw(*[ref[0] for ref in inputs[3:]], grad[:, HID:].T, 0.15)
    for ref, value in zip(outputs, new):
        ref[0] = value


def expert_step(grad, arrays):
    inner = pl.BlockSpec((1, 256, HID), lambda i: (0, i, 0))
    outer = pl.BlockSpec((1, HID, 256), lambda i: (0, 0, i))
    return pl.pallas_call(
        expert_step_kernel,
        grid=(D // 256,),
        out_shape=tuple(hbm(*a.shape) for a in arrays),
        in_specs=[pl.BlockSpec((256, D), lambda i: (i, 0))]
        + [inner] * 3
        + [outer] * 3,
        out_specs=(inner,) * 3 + (outer,) * 3,
        compiler_params=params(32),
        cost_estimate=pl.CostEstimate(
            flops=10**7, bytes_accessed=8 * 10**6, transcendentals=10**6
        ),
        name="expert_step",
    )(*pinned([grad, *arrays]))


def shape(*dims, dtype=jnp.float32):
    return jax.ShapeDtypeStruct(dims, dtype)


def in_vmem(count):
    return [pl.BlockSpec(memory_space=pltpu.VMEM)] * count


def pinned(values):
    return [pltpu.with_memory_space_constraint(v, pltpu.HBM) for v in values]


def hbm(*dims, dtype=jnp.float32):
    return pltpu.HBM(dims, dtype)


def in_smem():
    return pl.BlockSpec(memory_space=pltpu.SMEM)


def in_place(count):
    return [pl.BlockSpec(memory_space=pl.ANY)] * count


def params(mib):
    return pltpu.CompilerParams(vmem_limit_bytes=mib * 2**20)


def pack(qkv, proj, router, norm):
    return pl.pallas_call(
        pack_kernel,
        out_shape=(shape(PIECE, DENSE, dtype=low),) * 2,
        in_specs=in_place(4),
        out_specs=tuple(in_vmem(2)),
        scratch_shapes=vmem_like((qkv, proj, router.T, norm.T)) + [pltpu.SemaphoreType.DMA((4,))],
        compiler_params=params(16),
        cost_estimate=pl.CostEstimate(flops=10**5, bytes_accessed=2 * 10**6, transcendentals=0),
        name="pack",
    )(*pinned((qkv, proj, router.T, norm.T)))


def flat_type(value):
    return value.inner_aval if hasattr(value, "inner_aval") else value


def vmem_like(shapes):
    return [pltpu.VMEM(s.shape, s.dtype) for s in map(flat_type, shapes)]


def token_forward(*args):
    outs = (
        pltpu.VMEM((EXPERTS, 400, 128), low),
        hbm(ROWS, D),
        hbm(ROWS, D, dtype=low),
        hbm(ROWS, 3 * D, dtype=low),
        hbm(HEADS, ROWS, ROWS, dtype=low),
        hbm(ROWS, D, dtype=low),
        hbm(ROWS, D, dtype=low),
        hbm(ROWS, 128),
    )
    return pl.pallas_call(
        forward_kernel,
        out_shape=outs,
        in_specs=[in_smem()] + in_vmem(3) + in_place(18),
        out_specs=tuple(in_vmem(1) + in_place(7)),
        scratch_shapes=vmem_like(outs[1:])
        + [pltpu.VMEM((1, TOK, D), low)] * 2
        + [pltpu.VMEM((ROWS, D), full)] * 2
        + [
            pltpu.VMEM((D, DENSE), low),
            pltpu.SemaphoreType.DMA((16,)),
            pltpu.SemaphoreType.DMA((10,)),
            pltpu.VMEM((SLOTS, D), full),
            pltpu.VMEM((SLOTS, D), full),
        ],
        compiler_params=params(40),
        cost_estimate=pl.CostEstimate(
            flops=4 * 10**9, bytes_accessed=12 * 10**6, transcendentals=10**6
        ),
        name="token_forward",
    )(*args[:4], *pinned(args[4:]))


PAIR = pl.BlockSpec((2 * D, D), lambda i: (i, 0))
HIDDEN = pl.BlockSpec((SLOTS, 2 * HID), lambda i: (0, i))
TURNED = pl.BlockSpec((D, SLOTS), lambda i: (0, 0))


def experts_both_ways(got, weights):
    hidden, turned = hbm(SLOTS, GRP * HID, dtype=low), hbm(D, SLOTS, dtype=low)
    return pl.pallas_call(
        expert_kernel,
        grid=(GRP // 2,),
        out_shape=(
            pltpu.VMEM((EXPERTS, 400, 128), low),
            hidden,
            hidden,
            turned,
            turned,
        ),
        in_specs=in_vmem(1) + [PAIR],
        out_specs=(*in_vmem(1), HIDDEN, HIDDEN, TURNED, TURNED),
        scratch_shapes=[pltpu.VMEM((SLOTS, D), full)] * 2 + [pltpu.VMEM((SLOTS, D), low)] * 2,
        compiler_params=params(44),
        cost_estimate=pl.CostEstimate(
            flops=10 * 10**9, bytes_accessed=23 * 10**6, transcendentals=2 * 10**6
        ),
        name="experts",
    )(got, *pinned([weights]))


def expert_grads(*args):
    return pl.pallas_call(
        expert_grad_kernel,
        grid=(GRP // 2,),
        out_shape=hbm(GRP * D, D, dtype=low),
        in_specs=[HIDDEN, HIDDEN, TURNED, TURNED],
        out_specs=PAIR,
        compiler_params=params(28),
        cost_estimate=pl.CostEstimate(
            flops=6 * 10**9, bytes_accessed=18 * 10**6, transcendentals=0
        ),
        name="expert_grads",
    )(*pinned(args))


def token_backward(*args):
    outs = (
        hbm(1, TOK, D, dtype=low),
        hbm(1, TOK, D),
        hbm(16, BLOCK, WIDE, dtype=low),
        hbm(16, BLOCK, WIDE, dtype=low),
    )
    return pl.pallas_call(
        backward_kernel,
        out_shape=outs,
        in_specs=[in_smem()] + in_vmem(4) + in_place(25),
        out_specs=tuple(in_place(4)),
        scratch_shapes=vmem_like(args[5:14])
        + vmem_like(outs[:2])
        + [
            pltpu.VMEM((ROWS, D), full),
            pltpu.VMEM((ROWS, D), full),
            pltpu.VMEM((SLOTS, D), low),
            pltpu.VMEM((ROWS, 3 * D), low),
            pltpu.VMEM((D, DENSE), low),
            pltpu.SemaphoreType.DMA((16,)),
            pltpu.SemaphoreType.DMA((29,)),
            pltpu.VMEM((2, 16, BLOCK, WIDE), low),
            pltpu.VMEM((2, 4, 16, WIDE), full),
        ],
        compiler_params=params(48),
        cost_estimate=pl.CostEstimate(
            flops=400 * 10**9, bytes_accessed=18 * 10**6, transcendentals=10**4
        ),
        name="token_backward",
    )(*args[:5], *pinned(args[5:]))


def owner_step(pieces, arrays, small):
    return pl.pallas_call(
        owner_kernel,
        out_shape=tuple([hbm(*a.shape) for a in arrays] + [shape(*a.shape) for a in small]),
        in_specs=in_vmem(1) + in_place(6) + in_vmem(6),
        out_specs=tuple(in_place(6) + in_vmem(6)),
        scratch_shapes=vmem_like(arrays) * 2 + [pltpu.SemaphoreType.DMA((24,))],
        compiler_params=params(24),
        cost_estimate=pl.CostEstimate(
            flops=10**7, bytes_accessed=8 * 10**6, transcendentals=10**6
        ),
        name="owner_step",
    )(pieces, *pinned(arrays), *small)


def exchange(value):
    return lax.all_to_all(value, "exp", split_axis=0, concat_axis=0, tiled=True)


def dense_sum(keep, give):
    def along(step, value):
        hops = [(2 * x + c, 2 * ((x + step) % 4) + c) for x in range(4) for c in range(2)]
        return lax.ppermute(value, "grp", hops)

    got = lax.ppermute(give, "grp", [(i, i ^ 1) for i in range(GRP)])
    pieces = exchange((keep.astype(full) + got.astype(full)).astype(low))
    total = jnp.sum(pieces.astype(full), axis=0)
    main, rest = total[: 4 * PIECE].reshape(4, PIECE, WIDE), total[4 * PIECE :][:4, None]
    total = jnp.concatenate([main, rest], axis=1)
    sent = [along(step, total[step].astype(low)).astype(full) for step in (1, 2, 3)]
    return total[0] + sent[0] + sent[1] + sent[2]


def on_device(
    images,
    cotangent,
    expert_ids,
    kept_routes,
    qkv_master,
    qkv_first,
    qkv_second,
    proj_master,
    proj_first,
    proj_second,
    router_master,
    router_first,
    router_second,
    norm_master,
    norm_first,
    norm_second,
    inner_master,
    inner_first,
    inner_second,
    outer_master,
    outer_first,
    outer_second,
):
    ids = expert_ids.reshape(TOK, 2)
    kept = kept_routes.reshape(TOK, 2)
    flat = ids.reshape(-1)
    marks = (flat[:, None] == jnp.arange(EXPERTS, dtype=jnp.int32)[None, :]).astype(jnp.int32)
    slots = jnp.sum((jnp.cumsum(marks, axis=0) - marks) * marks, axis=1).reshape(TOK, 2)
    places = jnp.where(slots < CAP - 1, ids * 32 + slots, LAST + ids)
    target = jnp.where(kept > 0, places, -1)
    padding = ((0, ROWS - TOK), (0, 0))
    target = jnp.pad(target, padding, constant_values=-1)
    ids = jnp.pad(ids, padding, constant_values=-1)
    keep = jnp.pad(kept.astype(full), padding)

    packed = pack(qkv_master, proj_master, router_master, norm_master)
    pieces, target = dense_pieces(*packed, target)
    rows = piece_rows(lax.axis_index("grp"))
    mine = jnp.concatenate([inner_master[0].astype(low), outer_master[0].astype(low).T], axis=1)
    mine, *_ = lax.optimization_barrier((mine, pieces[3], pieces[4]))
    weights = lax.all_gather(mine, "grp", axis=0, tiled=True)

    send, m, a, qkv, p, o, c, r = token_forward(
        rows, ids, keep, target.T, images, cotangent, *pieces
    )
    back, *hidden = experts_both_ways(exchange(send), weights)
    back = exchange(back)
    grad = lax.psum_scatter(expert_grads(*hidden), "grp", scatter_dimension=0, tiled=True)
    result, image_grad, keep_grads, give_grads = token_backward(
        rows, ids, target, keep, back, m, r, cotangent, c, o, qkv, p, a, images, *pieces
    )
    (
        inner_moment,
        inner_square,
        inner_weight,
        outer_moment,
        outer_square,
        outer_weight,
    ) = expert_step(
        grad,
        (inner_master, inner_first, inner_second, outer_master, outer_first, outer_second),
    )
    block = dense_sum(keep_grads, give_grads).astype(low)
    block = exchange(jnp.broadcast_to(block[None], (16, PIECE + 1, WIDE)))
    block, inner_weight = lax.optimization_barrier((block, inner_weight))
    small = (router_master, router_first, router_second, norm_master, norm_first, norm_second)
    new = owner_step(
        block,
        (qkv_master, qkv_first, qkv_second, proj_master, proj_first, proj_second),
        [value.T for value in small],
    )
    qkv_moment, qkv_square, qkv_weight, proj_moment, proj_square, proj_weight = new[:6]
    router_moment, router_square, router_weight = [value.T for value in new[6:9]]
    norm_moment, norm_square, norm_weight = [value.T for value in new[9:]]
    return (
        result,
        image_grad,
        qkv_moment,
        qkv_square,
        qkv_weight,
        proj_moment,
        proj_square,
        proj_weight,
        router_moment,
        router_square,
        router_weight,
        norm_moment,
        norm_square,
        norm_weight,
        inner_moment,
        inner_square,
        inner_weight,
        outer_moment,
        outer_square,
        outer_weight,
    )


def solution(mesh):
    in_specs = (
        P(("grp", "exp"), None, None),
        P(("grp", "exp"), None, None),
        P(("grp", "exp"), None, None),
        P(("grp", "exp"), None, None),
        P("grp", None),
        P("grp", None),
        P("grp", None),
        P("grp", None),
        P("grp", None),
        P("grp", None),
        P("grp", None),
        P("grp", None),
        P("grp", None),
        P("grp", None),
        P("grp", None),
        P("grp", None),
        P("exp", None, "grp"),
        P("exp", None, "grp"),
        P("exp", None, "grp"),
        P("exp", "grp", None),
        P("exp", "grp", None),
        P("exp", "grp", None),
    )
    out_specs = (
        P(("grp", "exp"), None, None),
        P(("grp", "exp"), None, None),
        P("grp", None),
        P("grp", None),
        P("grp", None),
        P("grp", None),
        P("grp", None),
        P("grp", None),
        P("grp", None),
        P("grp", None),
        P("grp", None),
        P("grp", None),
        P("grp", None),
        P("grp", None),
        P("exp", None, "grp"),
        P("exp", None, "grp"),
        P("exp", None, "grp"),
        P("exp", "grp", None),
        P("exp", "grp", None),
        P("exp", "grp", None),
    )
    return jax.shard_map(
        on_device, mesh=mesh, in_specs=in_specs, out_specs=out_specs, check_vma=False
    )
```
